32 devices in a mesh: dp: 8 (over z, core), tensor: 4 (over y, x).
Axes of the slice: x: 2, y: 2, z: 4, core: 2. Of those that a mesh axis runs over, the one named last changes fastest.
Arguments:
- tokens: bfloat16 [16384, 1024], P(('dp', 'tensor')), may hold values from -6 to 6
- lengths: int32 [8, 3], P('dp'), may hold values from 1 to 1024, 2048 in all within a row
- first_values: bfloat16 [16384, 1024], P('dp', 'tensor'), may hold values from -6 to 6
- attn_gain: bfloat16 [1024], P(('dp', 'tensor')), may hold values from 0.25 to 1.75
- query_weight: bfloat16 [1024, 1024], P('dp', 'tensor'), may hold values from -0.1875 to 0.1875
- key_weight: bfloat16 [1024, 1024], P('dp', 'tensor'), may hold values from -0.1875 to 0.1875
- value_weight: bfloat16 [1024, 1024], P('dp', 'tensor'), may hold values from -0.1875 to 0.1875
- output_weight: bfloat16 [1024, 1024], P('dp', 'tensor'), may hold values from -1.5 to 1.5
- mlp_gain: bfloat16 [1024], P(('dp', 'tensor')), may hold values from 0.25 to 1.75
- gate_weight: bfloat16 [1024, 2816], P(('dp', 'tensor')), may hold values from -0.1875 to 0.1875
- up_weight: bfloat16 [1024, 2816], P(('dp', 'tensor')), may hold values from -0.1875 to 0.1875
- down_weight: bfloat16 [2816, 1024], P(('dp', 'tensor')), may hold values from -0.109375 to 0.109375
- out_cotangent: bfloat16 [16384, 1024], P(('dp', 'tensor')), may hold values from -6 to 6
Outputs:
- layer_out: bfloat16 [16384, 1024], P(('dp', 'tensor'))
- grad_input: float32 [16384, 1024], P(('dp', 'tensor'))
- grad_first_values: float32 [16384, 1024], P('dp', 'tensor')
- grad_attn_gain: float32 [1024], P(('dp', 'tensor'))
- grad_query: float32 [1024, 1024], P('dp', 'tensor')
- grad_key: float32 [1024, 1024], P('dp', 'tensor')
- grad_value: float32 [1024, 1024], P('dp', 'tensor')
- grad_output: float32 [1024, 1024], P('dp', 'tensor')
- grad_mlp_gain: float32 [1024], P(('dp', 'tensor'))
- grad_gate: float32 [1024, 2816], P(('dp', 'tensor'))
- grad_up: float32 [1024, 2816], P(('dp', 'tensor'))
- grad_down: float32 [2816, 1024], P(('dp', 'tensor'))
The draws below stay inside these ranges and needn't reach their ends.
Inputs may be any that keep to these rules, and one draw needn't show every extreme that they name: Each row's 3 lengths sum to 2048; the longest of each row is exactly 1024.
All inputs are finite; a program needn't handle non-finite values.
Results may differ from the reference program's by a relative error of at most 0.019.
Values may be sent and summed in bfloat16 or wider, within the bound.
No kernel may reach another device: no remote copies, remote signals or barrier semaphores. Data moves between devices by JAX's collectives and lax.ppermute only.
A program may use at most 192 MiB of HBM per device.

```python
import math
import jax
import jax.numpy as jnp
import numpy as np
from jax import lax

D = 1024
HEADS = 16
HEAD_DIM = 64
FF = 2816
TOK_DEV = 512
NDOC = 3
ROW = 2048
TOKENS = 16384
N_DP = 8
N_TENSOR = 4


def block_scale(key, shape, split, low, top_value):
    factor_of, own = 1.0, jax.random.fold_in(key, 6)
    for dim, parts in split:
        draws = jnp.exp(jax.random.uniform(jax.random.fold_in(own, dim), (parts,), jnp.float32, low / len(split), top_value / len(split)))
        factor_of = factor_of * jnp.repeat(draws, shape[dim] // parts).reshape([-1 if axis == dim else 1 for axis in range(len(shape))])
    return factor_of


def split_up(number_of, total, most, slope):
    weights = [(1 << 20) // math.isqrt(rank ** slope) + 1 for rank in range(2, number_of + 1)]
    spare, holding = total - most - (number_of - 1), [1] * (number_of - 1)
    while spare > 0:
        free = [i for i in range(number_of - 1) if holding[i] < most]
        pool, remaining = sum([weights[i] for i in free]), spare
        for i in free:
            more = min(most - holding[i], max(1, remaining * weights[i] // pool), spare)
            holding[i] = holding[i] + more
            spare = spare - more
    return np.array([most] + holding)


def ragged(own_key, number_of, total, limit, skew):
    if number_of == 2:
        one = jax.random.randint(own_key, (), max(1, total - limit), min(limit, total - 1) + 1)
        return jnp.stack([one, total - one])
    sizes = jnp.asarray(split_up(number_of, total, limit, skew), jnp.int32)
    couples = (number_of - 1) // 2
    source_of, sink = sizes[1:1 + 2 * couples:2], sizes[2:2 + 2 * couples:2]
    margin = jnp.minimum(source_of - 1, limit - sink)
    moved = jax.random.randint(jax.random.fold_in(own_key, 1), (couples,), 0, 1 << 20) % (margin + 1)
    sizes = sizes.at[1:1 + 2 * couples:2].set(source_of - moved).at[2:2 + 2 * couples:2].set(sink + moved)
    return sizes[jax.random.permutation(jax.random.fold_in(own_key, 2), number_of)]


def gaussian(key, dims, spread, most, split=(), kind=jnp.bfloat16):
    values = spread * jax.random.normal(key, dims, jnp.float32)
    if split:
        values = values * block_scale(key, dims, split, -0.22, 0.18)
    return jnp.clip(values, -most, most).astype(kind)


def setup_inputs(seed: int = 0) -> dict:
    keys = jax.random.split(jax.random.key(seed), 14)
    tokens = gaussian(keys[0], (TOKENS, D), 1.0, 6.0, ((0, 32),))
    lengths = jax.vmap(lambda own: ragged(own, NDOC, TOK_DEV * N_TENSOR, min(2048, TOK_DEV * N_TENSOR // 2), 2))(jax.random.split(keys[1], N_DP)).reshape((N_DP, NDOC)).astype(jnp.int32)
    first_values = gaussian(keys[2], (TOKENS, D), 1.0, 6.0, ((0, 8), (1, 4)))
    attn_gain = jnp.clip(1.0 + 0.15 * jax.random.normal(keys[3], (D,), jnp.float32), 0.25, 1.75).astype(jnp.bfloat16)
    query_weight = gaussian(keys[4], (D, D), D ** -0.5, 0.1875, ((0, 8), (1, 4)))
    key_weight = gaussian(keys[5], (D, D), D ** -0.5, 0.1875, ((0, 8), (1, 4)))
    value_weight = gaussian(keys[6], (D, D), D ** -0.5, 0.1875, ((0, 8), (1, 4)))
    output_weight = gaussian(keys[7], (D, D), (D // 64) ** -0.5, 1.5, ((0, 8), (1, 4)))
    mlp_gain = jnp.clip(1.0 + 0.15 * jax.random.normal(keys[8], (D,), jnp.float32), 0.25, 1.75).astype(jnp.bfloat16)
    gate_weight = gaussian(keys[9], (D, FF), D ** -0.5, 0.1875, ((0, 32),))
    up_weight = gaussian(keys[10], (D, FF), D ** -0.5, 0.1875, ((0, 32),))
    down_weight = gaussian(keys[11], (FF, D), FF ** -0.5, 0.109375, ((0, 32),))
    out_cotangent = gaussian(keys[12], (TOKENS, D), 1.0, 6.0, ((0, 32),))
    return dict(tokens=tokens, lengths=lengths, first_values=first_values, attn_gain=attn_gain, query_weight=query_weight, key_weight=key_weight, value_weight=value_weight, output_weight=output_weight, mlp_gain=mlp_gain, gate_weight=gate_weight, up_weight=up_weight, down_weight=down_weight, out_cotangent=out_cotangent)


eps = 1e-06
rope_base = 10000.0

@jax.custom_vjp
def low(v):
    return lax.optimization_barrier(v.astype(jnp.bfloat16)).astype(jnp.float32)

@jax.custom_vjp
def low_back(v):
    return v

def low_keep(v):
    return (low(v), None)

def low_pass(kept, grad):
    return (grad,)

def back_keep(v):
    return (v, None)

def back_low(kept, grad):
    return (low(grad),)
low.defvjp(low_keep, low_pass)
low_back.defvjp(back_keep, back_low)

def matmul(left, right):
    return jnp.dot(left, right, precision=lax.Precision.HIGHEST, preferred_element_type=jnp.float32)

def rms_norm(values, gain):
    return values * lax.rsqrt(lax.optimization_barrier(jnp.mean(values * values, axis=-1, keepdims=True)) + eps) * gain

def doc_layout(doc_lengths, total):
    doc_ends = jnp.cumsum(doc_lengths)
    position = jnp.arange(total, dtype=jnp.int32)
    passed = (position[:, None] >= doc_ends[None, :]).astype(jnp.int32)
    segment = lax.optimization_barrier(jnp.sum(passed, axis=1))
    offsets = lax.optimization_barrier(jnp.sum(passed * doc_lengths[None, :], axis=1))
    return (segment, position - offsets)

def rope_tables(positions):
    middle = HEAD_DIM // 2
    freqs = rope_base ** (-jnp.arange(middle, dtype=jnp.float32) * 2.0 / HEAD_DIM)
    angles = positions.astype(jnp.float32)[:, None] * freqs[None, :]
    return (jnp.cos(angles), jnp.sin(angles))

def rotate(values, cosine, sine):
    middle = values.shape[-1] // 2
    front_half = values[..., :middle]
    back_half = values[..., middle:]
    cos_b = cosine[:, None, :]
    sin_b = sine[:, None, :]
    return jnp.concatenate([front_half * cos_b - back_half * sin_b, back_half * cos_b + front_half * sin_b], axis=-1)

def row_forward(row_tokens, row_first, doc_lengths, params):
    gain_in, query_weight, key_weight, value_weight, output_weight, gain_mid, gate_weight, up_weight, down_weight = params
    segment, positions = doc_layout(doc_lengths, ROW)
    cosine, sine = rope_tables(positions)
    normed = low(rms_norm(row_tokens, gain_in))
    query = low_back(matmul(normed, query_weight))
    key_proj = low_back(matmul(normed, key_weight))
    value = low_back(matmul(normed, value_weight))
    query_rot = low(rotate(query.reshape(ROW, HEADS, HEAD_DIM), cosine, sine))
    key_rot = low(rotate(key_proj.reshape(ROW, HEADS, HEAD_DIM), cosine, sine))
    mixed = low(0.5 * value + 0.5 * row_first).reshape(ROW, HEADS, HEAD_DIM)
    block_rows = min(512, ROW)
    key_pos = jnp.arange(ROW, dtype=jnp.int32)

    def attend(block_index):
        offset = block_index * block_rows
        query_block = lax.dynamic_slice_in_dim(query_rot, offset, block_rows, 0)
        scores = jnp.einsum('qhd,khd->hqk', query_block, key_rot, precision=lax.Precision.HIGHEST) * HEAD_DIM ** (-0.5)
        scores = low_back(scores)
        query_pos = offset + jnp.arange(block_rows, dtype=jnp.int32)
        query_seg = lax.dynamic_slice_in_dim(segment, offset, block_rows, 0)
        allowed = (key_pos[None, :] <= query_pos[:, None]) & (segment[None, :] == query_seg[:, None])
        scores = jnp.where(allowed[None], scores, -1e+30)
        probs = low(jax.nn.softmax(scores, axis=-1))
        return jnp.einsum('hqk,khd->qhd', probs, mixed, precision=lax.Precision.HIGHEST)
    blocks = lax.map(jax.checkpoint(attend), jnp.arange(ROW // block_rows, dtype=jnp.int32))
    attended = low(low_back(blocks.reshape(ROW, D)))
    hidden = row_tokens + low_back(matmul(attended, output_weight.T))
    normed_mid = low(rms_norm(hidden, gain_mid))
    gate_value = low_back(matmul(normed_mid, gate_weight))
    up_value = low_back(matmul(normed_mid, up_weight))
    inner = low(jax.nn.silu(gate_value) * up_value)
    return hidden + low_back(matmul(inner, down_weight))

def reference(tokens, lengths, first_values, attn_gain, query_weight, key_weight, value_weight, output_weight, mlp_gain, gate_weight, up_weight, down_weight, out_cotangent):
    params = tuple((item.astype(jnp.float32) for item in (attn_gain, query_weight, key_weight, value_weight, output_weight, mlp_gain, gate_weight, up_weight, down_weight)))
    row_tokens = tokens.astype(jnp.float32).reshape(N_DP, ROW, D)
    row_first = first_values.astype(jnp.float32).reshape(N_DP, ROW, D)

    def forward(token_rows, first_rows, weights):
        return lax.map(lambda row_item: row_forward(row_item[0], row_item[1], row_item[2], weights), (token_rows, first_rows, lengths))
    outputs, pullback = jax.vjp(forward, row_tokens, row_first, params)
    grad_tokens, grad_first, grads = pullback(out_cotangent.astype(jnp.float32).reshape(N_DP, ROW, D))
    return (outputs.reshape(TOKENS, D).astype(jnp.bfloat16), grad_tokens.reshape(TOKENS, D), grad_first.reshape(TOKENS, D), grads[0], grads[1], grads[2], grads[3], grads[4], grads[5], grads[6], grads[7], grads[8])
```

```python
import functools

import jax
import jax.numpy as jnp
from jax import lax
from jax.experimental import pallas as pl
from jax.experimental.pallas import tpu as pltpu
from jax.sharding import PartitionSpec as P

HEAD_DIM = 64
HALF = HEAD_DIM // 2
BLOCK = 256
VMEM_LIMIT = 60 * 1024 * 1024

eps = 1e-06
rope_base = 10000.0
bf16 = jnp.bfloat16
f32 = jnp.float32

NN = (((1,), (0,)), ((), ()))
NT = (((1,), (1,)), ((), ()))
TN = (((0,), (0,)), ((), ()))


def mm(left, right, dims=NN):
    return lax.dot_general(left, right, dims, preferred_element_type=f32)


def swap_tensor(value, mask):
    size = lax.axis_size("tensor")
    return lax.ppermute(value, "tensor", [(i, i ^ mask) for i in range(size)])


def swap_core(value):
    size = lax.axis_size("dp")
    return lax.ppermute(value, "dp", [(i, i ^ 1) for i in range(size)])


def shift_z(value, step):
    size = lax.axis_size("dp")
    return lax.ppermute(value, "dp", [(i, (i + 2 * step) % size) for i in range(size)])


def bit_orders():
    bits = [1 << b for b in range(lax.axis_size("tensor").bit_length() - 1)]
    return bits, bits[1:] + bits[:1]


def gather_tensor(value, bits):
    have = {0: value}
    for bit in bits:
        have.update({mask ^ bit: swap_tensor(piece, bit) for mask, piece in list(have.items())})
    return have


def scatter_tensor(parts, bits):
    parts = dict(parts)
    for bit in bits:
        for mask in [m for m in parts if not m & bit]:
            got = swap_tensor(parts.pop(mask | bit), bit)
            parts[mask] = (parts[mask].astype(f32) + got.astype(f32)).astype(bf16)
    return parts[0]


def gather_z(value):
    depth = lax.axis_size("dp") // 2
    here = lax.axis_index("dp") // 2
    buffer = jnp.zeros((depth,) + value.shape, value.dtype)
    for step in range(depth):
        piece = value if step == 0 else shift_z(value, step)
        buffer = lax.dynamic_update_index_in_dim(buffer, piece, (here - step) % depth, 0)
    return buffer


def scatter_z(value):
    depth = value.shape[0]
    here = lax.axis_index("dp") // 2
    take = lambda step: lax.dynamic_index_in_dim(value, (here + step) % depth, 0, False)
    total = take(0).astype(f32)
    for step in range(1, depth):
        total = total + shift_z(take(step), step).astype(f32)
    return total


def attend_forward_kernel(
    heads, lo_ref, full_ref, x_ref, w_ref, fv_ref, cos_ref, sin_ref, start_ref,
    qt_ref, kt_ref, kn_ref, vn_ref, ot_ref, o_ref, lse_ref, wt, vt, acc,
):
    cols = heads * HEAD_DIM
    blocks = x_ref.shape[0] // BLOCK
    wt[...] = w_ref[...].T

    def project(i, carry):
        at = pl.ds(pl.multiple_of(i * BLOCK, BLOCK), BLOCK)
        joint = mm(wt[...], x_ref[at, :], NT)
        cosine, sine = cos_ref[:, at], sin_ref[:, at]
        first = fv_ref[at, :].astype(f32).T
        for h in range(heads):
            lo, mid, hi = h * HEAD_DIM, h * HEAD_DIM + HALF, (h + 1) * HEAD_DIM
            qa, qb = joint[lo:mid], joint[mid:hi]
            q = jnp.concatenate([qa * cosine - qb * sine, qb * cosine + qa * sine], axis=0)
            qt_ref[lo:hi, at] = (q * HEAD_DIM ** (-0.5)).astype(bf16)
            ka, kb = joint[cols + lo : cols + mid], joint[cols + mid : cols + hi]
            k = jnp.concatenate([ka * cosine - kb * sine, kb * cosine + ka * sine], axis=0)
            kt_ref[lo:hi, at] = k.astype(bf16)
            kn_ref[h, at, :] = k.T.astype(bf16)
            v = 0.5 * joint[2 * cols + lo : 2 * cols + hi] + 0.5 * first[lo:hi]
            vt[lo:hi, at] = v.astype(bf16)
            vn_ref[h, at, :] = v.T.astype(bf16)
        return carry

    lax.fori_loop(0, blocks, project, 0)

    def query_block(i, carry):
        qs = pl.ds(pl.multiple_of(i * BLOCK, BLOCK), BLOCK)
        start = start_ref[:, qs]
        key_iota = lax.broadcasted_iota(jnp.int32, (BLOCK, BLOCK), 0)
        query_pos = lax.broadcasted_iota(jnp.int32, (BLOCK, BLOCK), 1) + i * BLOCK

        def tile(j, state, masked, opening):
            ks = pl.ds(pl.multiple_of(j * BLOCK, BLOCK), BLOCK)
            if masked:
                key_pos = key_iota + j * BLOCK
                allowed = (key_pos <= query_pos) & (key_pos >= start)
            result = []
            for h in range(heads):
                rows = slice(h * HEAD_DIM, (h + 1) * HEAD_DIM)
                scores = mm(kn_ref[h, ks, :], qt_ref[rows, qs])
                if masked:
                    scores = jnp.where(allowed, scores, -1e30)
                peak = jnp.max(scores, axis=0, keepdims=True)
                if not opening:
                    old_peak, old_total = state[h]
                    peak = jnp.maximum(old_peak, peak)
                    shrink = jnp.exp(old_peak - peak)
                probs = jnp.exp(scores - peak)
                total = jnp.sum(probs, axis=0, keepdims=True)
                out = mm(vt[rows, ks], probs.astype(bf16))
                if not opening:
                    total = total + old_total * shrink
                    out = out + acc[rows, :] * shrink
                acc[rows, :] = out
                result.append((peak, total))
            return tuple(result)

        lo, full = lo_ref[i], full_ref[i]
        state = tile(i, None, True, True)
        state = lax.fori_loop(full, i, lambda j, s: tile(j, s, False, False), state)
        state = lax.fori_loop(lo, full, lambda j, s: tile(j, s, True, False), state)
        for h in range(heads):
            rows = slice(h * HEAD_DIM, (h + 1) * HEAD_DIM)
            peak, total = state[h]
            acc[rows, :] = acc[rows, :] * (1.0 / total)
            lse_ref[h : h + 1, qs] = peak + jnp.log(total)
        out = acc[...]
        ot_ref[:, qs] = out.astype(bf16)
        o_ref[qs, :] = out.T.astype(bf16)
        return carry

    lax.fori_loop(0, blocks, query_block, 0)


def attend_backward_kernel(
    heads, lo_ref, full_ref, qt_ref, kt_ref, kn_ref, vn_ref, ot_ref, lse_ref, do_ref,
    cos_ref, sin_ref, start_ref, w_ref, gj_ref, gn_ref, gf_ref, dot_, delta, dq, dk, dv,
):
    cols = heads * HEAD_DIM
    blocks = do_ref.shape[0] // BLOCK
    dk[...] = jnp.zeros_like(dk)
    dv[...] = jnp.zeros_like(dv)

    def prepare(i, carry):
        at = pl.ds(pl.multiple_of(i * BLOCK, BLOCK), BLOCK)
        grads = do_ref[at, :].astype(f32).T
        dot_[:, at] = grads.astype(bf16)
        prod = grads * ot_ref[:, at].astype(f32)
        for h in range(heads):
            delta[h : h + 1, at] = jnp.sum(
                prod[h * HEAD_DIM : (h + 1) * HEAD_DIM], axis=0, keepdims=True
            )
        return carry

    lax.fori_loop(0, blocks, prepare, 0)

    def query_block(step, carry):
        i = blocks - 1 - step
        qs = pl.ds(pl.multiple_of(i * BLOCK, BLOCK), BLOCK)
        start = start_ref[:, qs]
        key_iota = lax.broadcasted_iota(jnp.int32, (BLOCK, BLOCK), 0)
        query_pos = lax.broadcasted_iota(jnp.int32, (BLOCK, BLOCK), 1) + i * BLOCK
        dq[...] = jnp.zeros_like(dq)

        def tile(j, carry, masked):
            ks = pl.ds(pl.multiple_of(j * BLOCK, BLOCK), BLOCK)
            if masked:
                key_pos = key_iota + j * BLOCK
                allowed = (key_pos <= query_pos) & (key_pos >= start)
            for h in range(heads):
                rows = slice(h * HEAD_DIM, (h + 1) * HEAD_DIM)
                q_h, do_h = qt_ref[rows, qs], dot_[rows, qs]
                scores = mm(kn_ref[h, ks, :], q_h)
                if masked:
                    scores = jnp.where(allowed, scores, -1e30)
                probs = jnp.exp(scores - lse_ref[h : h + 1, qs])
                grad_probs = mm(vn_ref[h, ks, :], do_h)
                grad_scores = (probs * (grad_probs - delta[h : h + 1, qs])).astype(bf16)
                dv[rows, ks] += mm(do_h, probs.astype(bf16), NT)
                dk[rows, ks] += mm(q_h, grad_scores, NT)
                dq[rows, :] += mm(kt_ref[rows, ks], grad_scores)
            return carry

        lo, full = lo_ref[i], full_ref[i]
        tile(i, 0, True)
        lax.fori_loop(full, i, lambda j, s: tile(j, s, False), 0)
        lax.fori_loop(lo, full, lambda j, s: tile(j, s, True), 0)

        cosine, sine = cos_ref[:, qs], sin_ref[:, qs]
        pieces = []
        for source, factor in ((dq, HEAD_DIM ** (-0.5)), (dk, 1.0)):
            for h in range(heads):
                lo_row, mid, hi = h * HEAD_DIM, h * HEAD_DIM + HALF, (h + 1) * HEAD_DIM
                where = slice(None) if source is dq else qs
                a, b = source[lo_row:mid, where] * factor, source[mid:hi, where] * factor
                pieces += [a * cosine + b * sine, b * cosine - a * sine]
        half_v = 0.5 * dv[:, qs]
        gf_ref[qs, :] = half_v.T
        grads = jnp.concatenate(pieces + [half_v], axis=0).T.astype(bf16)
        gj_ref[qs, :] = grads
        gn_ref[qs, :] = mm(grads, w_ref[...], NT).astype(bf16)
        return carry

    lax.fori_loop(0, blocks, query_block, 0)


def feed_forward_kernel(
    n_z, n_t, place_ref, xa_ref, xb_ref, ga_ref, gb_ref, wd_ref, *rest
):
    pieces = rest[: 2 * n_t]
    inner_ref, gvu_ref, u_ref, w, sems = rest[2 * n_t :]
    half_z = n_z // 2
    z, t = place_ref[0], place_ref[1]
    copies = []
    for part in range(2):
        for mask in range(n_t):
            for r in range(half_z):
                copy = pltpu.make_async_copy(
                    pieces[part * n_t + mask].at[r],
                    w.at[part * half_z + r, :, jnp.bitwise_xor(t, mask)],
                    sems.at[(part * n_t + mask) * half_z + r],
                )
                copy.start()
                copies.append(copy)
    for copy in copies:
        copy.wait()
    features = xa_ref.shape[1]
    ff = wd_ref.shape[0]
    tokens = xa_ref.shape[0]
    step = 256
    edges = list(range(0, ff, step)) + [ff]

    def weight(lo, hi):
        return w[:, :, :, :, lo:hi].reshape(features, hi - lo)

    for source, (x_ref, g_ref) in enumerate(((xa_ref, ga_ref), (xb_ref, gb_ref))):

        def rows_step(i, carry, x_ref=x_ref, g_ref=g_ref, source=source):
            rows = pl.ds(pl.multiple_of(i * step, step), step)
            outs = pl.ds(pl.multiple_of(source * tokens + i * step, step), step)
            x, g = x_ref[rows, :], g_ref[rows, :]
            for lo, hi in zip(edges[:-1], edges[1:]):
                gate = mm(x, weight(lo, hi))
                up = mm(x, weight(ff + lo, ff + hi))
                grad_inner = mm(g, wd_ref[lo:hi, :], NT)
                sig = jax.nn.sigmoid(gate)
                act = gate * sig
                inner_ref[outs, lo:hi] = (act * up).astype(bf16)
                gvu_ref[outs, lo:hi] = (
                    grad_inner * up * (sig * (1.0 + gate * (1.0 - sig)))
                ).astype(bf16)
                gvu_ref[outs, ff + lo : ff + hi] = (grad_inner * act).astype(bf16)
            u_ref[outs, :] = mm(gvu_ref[outs, :], weight(0, 2 * ff), NT)
            return carry

        lax.fori_loop(0, tokens // step, rows_step, 0)


def vmem(n):
    return [pl.BlockSpec(memory_space=pltpu.VMEM)] * n


def smem(n):
    return [pl.BlockSpec(memory_space=pltpu.SMEM)] * n


def params():
    return pltpu.CompilerParams(vmem_limit_bytes=VMEM_LIMIT)


def attend_forward(heads, lo, full, x, w, fv, cosine, sine, start):
    rows, cols = x.shape[0], heads * HEAD_DIM
    sds = jax.ShapeDtypeStruct
    return pl.pallas_call(
        functools.partial(attend_forward_kernel, heads),
        out_shape=(
            sds((cols, rows), bf16),
            sds((cols, rows), bf16),
            sds((heads, rows, HEAD_DIM), bf16),
            sds((heads, rows, HEAD_DIM), bf16),
            sds((cols, rows), bf16),
            sds((rows, cols), bf16),
            sds((heads, rows), f32),
        ),
        in_specs=smem(2) + vmem(6),
        out_specs=tuple(vmem(7)),
        scratch_shapes=[
            pltpu.VMEM((3 * cols, x.shape[1]), bf16),
            pltpu.VMEM((cols, rows), bf16),
            pltpu.VMEM((cols, BLOCK), f32),
        ],
        compiler_params=params(),
        cost_estimate=pl.CostEstimate(
            flops=30_000_000_000, bytes_accessed=20_000_000, transcendentals=0
        ),
        name="attend_forward",
    )(lo, full, x, w, fv, cosine, sine, start)


def attend_backward(heads, lo, full, saved, grads, cosine, sine, start, w):
    rows, cols = grads.shape[0], heads * HEAD_DIM
    sds = jax.ShapeDtypeStruct
    qt, kt, kn, vn, ot, lse = saved
    return pl.pallas_call(
        functools.partial(attend_backward_kernel, heads),
        out_shape=(
            sds((rows, 3 * cols), bf16),
            sds((rows, w.shape[0]), bf16),
            sds((rows, cols), f32),
        ),
        in_specs=smem(2) + vmem(11),
        out_specs=tuple(vmem(3)),
        scratch_shapes=[
            pltpu.VMEM((cols, rows), bf16),
            pltpu.VMEM((heads, rows), f32),
            pltpu.VMEM((cols, BLOCK), f32),
            pltpu.VMEM((cols, rows), f32),
            pltpu.VMEM((cols, rows), f32),
        ],
        compiler_params=params(),
        cost_estimate=pl.CostEstimate(
            flops=60_000_000_000, bytes_accessed=20_000_000, transcendentals=0
        ),
        name="attend_backward",
    )(lo, full, qt, kt, kn, vn, ot, lse, grads, cosine, sine, start, w)


def feed_forward(n_z, n_t, place, xa, xb, ga, gb, wd, pieces):
    tokens, features = xa.shape
    ff = wd.shape[0]
    sds = jax.ShapeDtypeStruct
    own_rows = pieces[0].shape[2]
    return pl.pallas_call(
        functools.partial(feed_forward_kernel, n_z, n_t),
        out_shape=(
            sds((2 * tokens, ff), bf16),
            sds((2 * tokens, 2 * ff), bf16),
            sds((2 * tokens, features), f32),
        ),
        in_specs=smem(1) + vmem(5) + [pl.BlockSpec(memory_space=pl.ANY)] * len(pieces),
        out_specs=tuple(vmem(3)),
        scratch_shapes=[
            pltpu.VMEM((n_z, 2, n_t, own_rows, 2 * ff), bf16),
            pltpu.SemaphoreType.DMA((n_z * n_t,)),
        ],
        compiler_params=params(),
        cost_estimate=pl.CostEstimate(
            flops=16_000_000_000, bytes_accessed=30_000_000, transcendentals=0
        ),
        name="feed_forward",
    )(place, xa, xb, ga, gb, wd, *pieces)


def doc_layout(doc_lengths, total):
    doc_ends = jnp.cumsum(doc_lengths)
    index = jnp.arange(total, dtype=jnp.int32)
    passed = (index[:, None] >= doc_ends[None, :]).astype(jnp.int32)
    return jnp.sum(passed * doc_lengths[None, :], axis=1)


def split_cols(weight, n_z):
    rows = weight.shape[0]
    return weight.reshape(rows, n_z, 2, -1).transpose(2, 0, 1, 3).reshape(2, rows, -1)


def join_cols(parts, n_z):
    rows = parts.shape[1]
    return parts.reshape(2, rows, n_z, -1).transpose(1, 2, 0, 3).reshape(rows, -1)


def body(
    tokens, lengths, first_values, attn_gain, query_weight, key_weight, value_weight,
    output_weight, mlp_gain, gate_weight, up_weight, down_weight, out_cotangent,
):
    n_t = lax.axis_size("tensor")
    n_dp = lax.axis_size("dp")
    n_z = n_dp // 2
    t = lax.axis_index("tensor")
    core = lax.axis_index("dp") % 2
    z = lax.axis_index("dp") // 2
    masks = range(n_t)
    bits_a, bits_b = bit_orders()
    count, features = tokens.shape
    rows = count * n_t
    cols = query_weight.shape[1]
    heads = cols // HEAD_DIM
    half = count // 2
    ff_core = gate_weight.shape[1] // 2

    def token_slice(value, mask, offset, size):
        return lax.dynamic_slice_in_dim(value, (t ^ mask) * count + offset, size, 0)

    token_f = tokens.astype(f32)
    inverse_in = lax.rsqrt(jnp.mean(token_f * token_f, axis=-1, keepdims=True) + eps)
    unit_in = (token_f * inverse_in).astype(bf16)
    x_full = jnp.zeros((rows, features), bf16)
    for offset, bits in ((0, bits_a), (half, bits_b)):
        for mask, piece in gather_tensor(unit_in[offset : offset + half], bits).items():
            x_full = lax.dynamic_update_slice_in_dim(
                x_full, piece, (t ^ mask) * count + offset, 0
            )

    own_gain = attn_gain.astype(f32)[None]
    row_index = lax.broadcasted_iota(jnp.int32, (n_t, own_gain.shape[1]), 0)
    gain_rows = jnp.zeros((n_t, own_gain.shape[1]), f32)
    for mask in masks:
        piece = swap_tensor(own_gain, mask) if mask else own_gain
        gain_rows = jnp.where(row_index == t ^ mask, piece, gain_rows)
    gain_rows = gain_rows.reshape(-1, 1)

    own_joint = jnp.concatenate([query_weight, key_weight, value_weight], axis=1).astype(f32)
    near = gather_z((own_joint * gain_rows).astype(bf16))
    far = swap_core(near)
    joint_weight = jnp.where(
        core == 0, jnp.stack([near, far], axis=1), jnp.stack([far, near], axis=1)
    ).reshape(features, 3 * cols)

    start = doc_layout(lengths[0], rows)
    position = (jnp.arange(rows, dtype=jnp.int32) - start).astype(f32)
    freqs = rope_base ** (-jnp.arange(HALF, dtype=f32) * 2.0 / HEAD_DIM)
    angles = freqs[:, None] * position[None, :]
    cosine, sine = jnp.cos(angles), jnp.sin(angles)
    block_starts = start.reshape(-1, BLOCK)
    lo = block_starts[:, 0] // BLOCK
    full = jnp.minimum(
        (block_starts[:, -1] + BLOCK - 1) // BLOCK,
        jnp.arange(rows // BLOCK, dtype=jnp.int32),
    )
    start = start[None]

    qt, kt, kn, vn, ot, attended, lse = attend_forward(
        heads, lo, full, x_full, joint_weight, first_values, cosine, sine, start
    )

    gain_mid = mlp_gain.astype(f32)[:, None]
    gate_parts = split_cols(gate_weight, n_z)
    up_parts = split_cols(up_weight, n_z)
    both = jnp.concatenate([gate_parts, up_parts], axis=2).astype(f32)
    both = (both * gain_mid[None]).astype(bf16)
    mine = lax.dynamic_index_in_dim(both, core, 0, False)
    theirs = swap_core(lax.dynamic_index_in_dim(both, 1 - core, 0, False))
    pair = jnp.where(core == 0, jnp.stack([mine, theirs]), jnp.stack([theirs, mine]))
    column = gather_z(pair)
    half_z = n_z // 2
    gathered = []
    for offset, bits in ((0, bits_a), (half_z, bits_b)):
        pieces = gather_tensor(column[offset : offset + half_z], bits)
        gathered += [pieces[mask] for mask in masks]

    down_column = gather_z(down_weight)
    down = jnp.zeros((n_z, n_t) + down_weight.shape, bf16)
    for offset, bits in ((0, bits_b), (half_z, bits_a)):
        for mask, piece in gather_tensor(down_column[offset : offset + half_z], bits).items():
            down = lax.dynamic_update_slice(
                down, piece[:, None], (offset, t ^ mask, 0, 0)
            )
    down = down.reshape(ff_core, features)

    out_column = gather_z(output_weight)
    out_parts = [{}, {}]
    for part, (offset, bits) in enumerate(((0, bits_a), (half_z, bits_b))):
        out_parts[part] = gather_tensor(out_column[offset : offset + half_z], bits)
    out_near = jnp.concatenate(
        [jnp.concatenate([out_parts[p][mask] for p in range(2)], axis=0) for mask in masks],
        axis=-1,
    )
    out_far = swap_core(out_near)
    out_weight = jnp.where(
        core == 0, jnp.stack([out_near, out_far], axis=1), jnp.stack([out_far, out_near], axis=1)
    ).reshape(features, n_t * cols)

    att = jnp.concatenate(
        [token_slice(attended, 0, 0, count)]
        + [swap_tensor(token_slice(attended, m, 0, count), m) for m in masks if m],
        axis=1,
    )
    hidden = token_f + mm(att, out_weight, NT)
    inverse_mid = lax.rsqrt(jnp.mean(hidden * hidden, axis=-1, keepdims=True) + eps)
    unit_mid = (hidden * inverse_mid).astype(bf16)

    unit_far = swap_core(unit_mid)
    grad_far = swap_core(out_cotangent)
    place = jnp.stack([z, t]).astype(jnp.int32)
    inner, gvu, u_part = feed_forward(
        n_z, n_t, place, unit_mid, unit_far, out_cotangent, grad_far, down, gathered
    )
    u = u_part[:count] + swap_core(u_part[count:].astype(bf16)).astype(f32)
    cotangent = out_cotangent.astype(f32)
    grad_hidden = (
        cotangent
        + inverse_mid * u
        - hidden
        * (inverse_mid ** 3 * jnp.sum(u * hidden, axis=-1, keepdims=True) / features)
    )
    grad_branch = grad_hidden.astype(bf16)
    grad_att = mm(grad_branch, out_weight).astype(bf16)
    grad_attended = jnp.zeros((rows, cols), bf16)
    for mask in masks:
        piece = grad_att[:, mask * cols : (mask + 1) * cols]
        piece = swap_tensor(piece, mask) if mask else piece
        grad_attended = lax.dynamic_update_slice_in_dim(
            grad_attended, piece, (t ^ mask) * count, 0
        )

    grad_joint, grad_unit, grad_first = attend_backward(
        heads, lo, full, (qt, kt, kn, vn, ot, lse), grad_attended, cosine, sine, start,
        joint_weight,
    )

    out_part = mm(inner, down)
    layer_out = (
        hidden + out_part[:count] + swap_core(out_part[count:].astype(bf16)).astype(f32)
    ).astype(bf16)

    unit_both = jnp.concatenate([unit_mid, unit_far], axis=0)
    grad_both = jnp.concatenate([out_cotangent, grad_far], axis=0)
    grad_gu = mm(unit_both, gvu, TN).astype(bf16).reshape(n_z, 2, n_t, -1, 2 * ff_core)
    grad_dn = mm(inner, grad_both, TN).astype(bf16).reshape(n_z, n_t, -1, features)

    def over_tensor(pick, orders):
        parts = []
        for offset, bits in zip((0, half_z), orders):
            parts.append(scatter_tensor({m: pick(m, offset) for m in masks}, bits))
        return jnp.concatenate(parts, axis=0)

    gu = over_tensor(
        lambda m, offset: lax.dynamic_index_in_dim(
            grad_gu[offset : offset + half_z], t ^ m, 2, False
        ),
        (bits_a, bits_b),
    )
    gu = scatter_z(gu)
    gu_mine = lax.dynamic_index_in_dim(gu, core, 0, False)
    gu_far = swap_core(lax.dynamic_index_in_dim(gu, 1 - core, 0, False))
    gu = jnp.where(core == 0, jnp.stack([gu_mine, gu_far]), jnp.stack([gu_far, gu_mine]))
    grad_gate = join_cols(gu[:, :, :ff_core], n_z)
    grad_up = join_cols(gu[:, :, ff_core:], n_z)
    grad_mlp_gain = jnp.sum(
        grad_gate * gate_weight.astype(f32) + grad_up * up_weight.astype(f32), axis=1
    )
    grad_gate = grad_gate * gain_mid
    grad_up = grad_up * gain_mid

    dn = over_tensor(
        lambda m, offset: lax.dynamic_index_in_dim(
            grad_dn[offset : offset + half_z], t ^ m, 1, False
        ),
        (bits_b, bits_a),
    )
    grad_down = scatter_z(dn)

    grad_ow = mm(grad_branch, att, TN).astype(bf16).reshape(n_z, 2, -1, n_t * cols)
    keep = lax.dynamic_index_in_dim(grad_ow, core, 1, False)
    give = lax.dynamic_index_in_dim(grad_ow, 1 - core, 1, False)
    grad_ow = (keep.astype(f32) + swap_core(give).astype(f32)).astype(bf16)
    ow = over_tensor(
        lambda m, offset: grad_ow[offset : offset + half_z, :, m * cols : (m + 1) * cols],
        (bits_a, bits_b),
    )
    grad_output = scatter_z(ow)

    u_halves = []
    for offset, bits in ((0, bits_a), (half, bits_b)):
        parts = {m: token_slice(grad_unit, m, offset, half) for m in masks}
        u_halves.append(scatter_tensor(parts, bits).astype(f32))
    u_in = jnp.concatenate(u_halves, axis=0)
    grad_input = (
        grad_hidden
        + inverse_in * u_in
        - token_f
        * (inverse_in ** 3 * jnp.sum(u_in * token_f, axis=-1, keepdims=True) / features)
    )

    grad_jw = mm(x_full, grad_joint, TN).astype(bf16).reshape(n_z, 2, -1, 3 * cols)
    keep = lax.dynamic_index_in_dim(grad_jw, core, 1, False)
    give = lax.dynamic_index_in_dim(grad_jw, 1 - core, 1, False)
    grad_jw = scatter_z((keep.astype(f32) + swap_core(give).astype(f32)).astype(bf16))
    gain_part = jnp.sum(grad_jw * own_joint, axis=1).reshape(n_t, -1)
    grad_attn_gain = lax.dynamic_index_in_dim(gain_part, t, 0, True)
    for mask in masks:
        if mask:
            grad_attn_gain = grad_attn_gain + swap_tensor(
                lax.dynamic_index_in_dim(gain_part, t ^ mask, 0, True), mask
            )
    grad_jw = grad_jw * gain_rows

    return (
        layer_out,
        grad_input,
        grad_first,
        grad_attn_gain[0],
        grad_jw[:, :cols],
        grad_jw[:, cols : 2 * cols],
        grad_jw[:, 2 * cols :],
        grad_output,
        grad_mlp_gain,
        grad_gate,
        grad_up,
        grad_down,
    )


def solution(mesh):
    both = ("dp", "tensor")
    in_specs = (
        P(both, None),
        P("dp", None),
        P("dp", "tensor"),
        P(both),
        P("dp", "tensor"),
        P("dp", "tensor"),
        P("dp", "tensor"),
        P("dp", "tensor"),
        P(both),
        P(both, None),
        P(both, None),
        P(both, None),
        P(both, None),
    )
    out_specs = (
        P(both, None),
        P(both, None),
        P("dp", "tensor"),
        P(both),
        P("dp", "tensor"),
        P("dp", "tensor"),
        P("dp", "tensor"),
        P("dp", "tensor"),
        P(both),
        P(both, None),
        P(both, None),
        P(both, None),
    )
    return jax.shard_map(body, mesh=mesh, in_specs=in_specs, out_specs=out_specs, check_vma=False)
```

```python
import functools

import jax
import jax.numpy as jnp
from jax import lax
from jax.experimental import pallas as pl
from jax.experimental.pallas import tpu as pltpu
from jax.sharding import Mesh, PartitionSpec as P

HEAD_DIM = 64
HALF = HEAD_DIM // 2
BLOCK = 256
VMEM_LIMIT = 60 * 1024 * 1024

eps = 1e-06
rope_base = 10000.0
bf16 = jnp.bfloat16
f32 = jnp.float32

NN = (((1,), (0,)), ((), ()))
NT = (((1,), (1,)), ((), ()))
TN = (((0,), (0,)), ((), ()))


def mm(left, right, dims=NN):
    return lax.dot_general(left, right, dims, preferred_element_type=f32)


def swap_tensor(value, mask):
    size = lax.axis_size("tensor")
    return lax.ppermute(value, "tensor", [(i, i ^ mask) for i in range(size)])


def swap_core(value):
    return lax.ppermute(value, "core", [(0, 1), (1, 0)])


def shift_z(value, step):
    size = lax.axis_size("z")
    return lax.ppermute(value, "z", [(i, (i + step) % size) for i in range(size)])


def bit_orders():
    bits = [1 << b for b in range(lax.axis_size("tensor").bit_length() - 1)]
    return bits, bits[1:] + bits[:1]


def together(*values):
    return lax.optimization_barrier(values)


def halves(value):
    middle = value.shape[0] // 2
    return value[:middle], value[middle:]


def gather_near(value):
    if lax.axis_size("tensor") != 4:
        return []
    return [swap_tensor(value, 1), swap_tensor(value, 2)]


def pass_on(near):
    return [halves(near[0])[0], halves(near[1])[1]] if near else []


def gather_far(value, near, passed=()):
    if near:
        if not passed:
            passed = pass_on(near)
        far = [swap_tensor(passed[0], 2), swap_tensor(passed[1], 1)]
        return {0: [value], 1: [near[0]], 2: [near[1]], 3: far}
    parts = []
    for piece, bits in zip(halves(value), bit_orders()):
        have = {0: piece}
        for bit in bits:
            have.update({m ^ bit: swap_tensor(got, bit) for m, got in list(have.items())})
        parts.append(have)
    return {mask: [part[mask] for part in parts] for mask in parts[0]}


def add(left, right):
    return (left.astype(f32) + right.astype(f32)).astype(bf16)


def scatter_far(parts):
    if lax.axis_size("tensor") != 4:
        return []
    upper, lower = parts[3]
    return [swap_tensor(upper, 1), swap_tensor(lower, 2)]


def scatter_join(parts, far):
    if not far:
        return []
    to_x, to_y = parts[1][0], parts[2][0]
    middle = to_y.shape[0] // 2
    return [
        lax.dynamic_update_slice_in_dim(to_x, add(to_x[middle:], far[1]), middle, 0),
        lax.dynamic_update_slice_in_dim(to_y, add(to_y[:middle], far[0]), 0, 0),
    ]


def scatter_near(parts, joined):
    if joined:
        return [parts[0][0], swap_tensor(joined[0], 1), swap_tensor(joined[1], 2)]
    parts = {mask: jnp.concatenate(part, axis=0) for mask, part in parts.items()}
    sums = []
    for which, bits in enumerate(bit_orders()):
        left = {mask: halves(part)[which] for mask, part in parts.items()}
        for bit in bits:
            for mask in [m for m in left if not m & bit]:
                left[mask] = add(left[mask], swap_tensor(left.pop(mask | bit), bit))
        sums.append(left[0])
    return [jnp.concatenate(sums, axis=0)]


def spread_tensor(value):
    return swap_all([value] * lax.axis_size("tensor"))


def swap_all(pieces):
    return [swap_tensor(piece, mask) if mask else piece for mask, piece in enumerate(pieces)]


def by_index(pieces):
    here = lax.axis_index("tensor")
    order = []
    for place in range(len(pieces)):
        piece = pieces[0]
        for mask in range(1, len(pieces)):
            piece = jnp.where(here ^ place == mask, pieces[mask], piece)
        order.append(piece)
    return jnp.stack(order)


def send_z(value):
    return jnp.stack([value] + [shift_z(value, i) for i in range(1, lax.axis_size("z"))])


def sums_z(terms):
    depth = lax.axis_size("z")
    here = lax.axis_index("z")
    take = lambda term, i: lax.dynamic_index_in_dim(term, (here + i) % depth, 0, False)
    sums = [total([take(term, i) for term in terms]) for i in range(depth)]
    return [sums[0]] + [part.astype(bf16) for part in sums[1:]]


def scatter_z(sums):
    return [sums[0]] + [shift_z(part, i + 1) for i, part in enumerate(sums[1:])]


def exchange(value, axis):
    return lax.all_to_all(value, axis, 0, 0)


def spread(value, axis):
    return exchange(jnp.broadcast_to(value[None], (lax.axis_size(axis),) + value.shape), axis)


def piece_rows(mask, height, n_t):
    return [height // 2] * 2 if mask == 3 and n_t == 4 else [height]


def total(terms):
    terms = [terms[i].astype(f32) for i in range(len(terms))]
    return sum(terms[1:], terms[0])


def attend_forward_kernel(
    heads, n_t, x_at, place_ref, lo_ref, full_ref, fv_ref, cos_ref, sin_ref, start_ref, gain_ref, *rest
):
    x_in, w_in, rest = rest[: len(x_at)], rest[len(x_at) : len(x_at) + 2], rest[len(x_at) + 2 :]
    qt_ref, kt_ref, kn_ref, vn_ref, ot_ref, lse_ref, x_out, w_out = rest[:8]
    o_out, (x_ref, w_ref, wt, vt, o_ref, acc, sems) = rest[8 : 8 + n_t], rest[8 + n_t :]
    core, t = place_ref[1], place_ref[2]
    n_z = w_in[0].shape[0]
    height = w_ref.shape[0] // (2 * n_z)
    cols = heads * HEAD_DIM
    blocks = x_ref.shape[0] // BLOCK
    count = x_ref.shape[0] // n_t
    copies = []
    for other, ref in enumerate(w_in):
        for z in range(n_z):
            row = pl.multiple_of((2 * z + jnp.bitwise_xor(core, other)) * height, height)
            copies.append((ref.at[z, pl.ds(0, height)], w_ref.at[pl.ds(row, height)]))
    for ref, (mask, offset) in zip(x_in, x_at):
        row = jnp.bitwise_xor(t, mask) * count + offset
        size = ref.shape[0]
        copies.append((ref, x_ref.at[pl.ds(pl.multiple_of(row, size), size)]))
    copies = [pltpu.make_async_copy(a, b, sems.at[i]) for i, (a, b) in enumerate(copies)]
    for copy in copies:
        copy.start()
    for copy in copies:
        copy.wait()
    keep = [
        pltpu.make_async_copy(x_ref, x_out, sems.at[len(copies)]),
        pltpu.make_async_copy(w_ref, w_out, sems.at[len(copies) + 1]),
    ]
    for copy in keep:
        copy.start()
    wt[...] = (w_ref[...].astype(f32).T * gain_ref[...]).astype(bf16)

    def project(i, carry):
        at = pl.ds(pl.multiple_of(i * BLOCK, BLOCK), BLOCK)
        joint = mm(wt[...], x_ref[at, :], NT)
        cosine, sine = cos_ref[:, at], sin_ref[:, at]
        first = fv_ref[at, :].astype(f32).T
        for h in range(heads):
            lo, mid, hi = h * HEAD_DIM, h * HEAD_DIM + HALF, (h + 1) * HEAD_DIM
            qa, qb = joint[lo:mid], joint[mid:hi]
            q = jnp.concatenate([qa * cosine - qb * sine, qb * cosine + qa * sine], axis=0)
            qt_ref[lo:hi, at] = (q * HEAD_DIM ** (-0.5)).astype(bf16)
            ka, kb = joint[cols + lo : cols + mid], joint[cols + mid : cols + hi]
            k = jnp.concatenate([ka * cosine - kb * sine, kb * cosine + ka * sine], axis=0)
            kt_ref[lo:hi, at] = k.astype(bf16)
            kn_ref[h, at, :] = k.T.astype(bf16)
            v = 0.5 * joint[2 * cols + lo : 2 * cols + hi] + 0.5 * first[lo:hi]
            vt[lo:hi, at] = v.astype(bf16)
            vn_ref[h, at, :] = v.T.astype(bf16)
        return carry

    lax.fori_loop(0, blocks, project, 0)

    def query_block(i, carry):
        qs = pl.ds(pl.multiple_of(i * BLOCK, BLOCK), BLOCK)
        start = start_ref[:, qs]
        key_iota = lax.broadcasted_iota(jnp.int32, (BLOCK, BLOCK), 0)
        query_pos = lax.broadcasted_iota(jnp.int32, (BLOCK, BLOCK), 1) + i * BLOCK

        def tile(j, state, masked, opening):
            ks = pl.ds(pl.multiple_of(j * BLOCK, BLOCK), BLOCK)
            if masked:
                key_pos = key_iota + j * BLOCK
                allowed = (key_pos <= query_pos) & (key_pos >= start)
            result = []
            all_scores = [
                mm(kn_ref[h, ks, :], qt_ref[h * HEAD_DIM : (h + 1) * HEAD_DIM, qs])
                for h in range(heads)
            ]
            if masked:
                all_scores = [jnp.where(allowed, sc, -1e30) for sc in all_scores]
            peaks = [jnp.max(sc, axis=0, keepdims=True) for sc in all_scores]
            if not opening:
                shrinks = []
                for h in range(heads):
                    peaks[h] = jnp.maximum(state[h][0], peaks[h])
                    shrinks.append(jnp.exp(state[h][0] - peaks[h]))
            all_probs = [jnp.exp(sc - pk) for sc, pk in zip(all_scores, peaks)]
            for h in range(heads):
                rows = slice(h * HEAD_DIM, (h + 1) * HEAD_DIM)
                total = jnp.sum(all_probs[h], axis=0, keepdims=True)
                out = mm(vt[rows, ks], all_probs[h].astype(bf16))
                if not opening:
                    total = total + state[h][1] * shrinks[h]
                    out = out + acc[rows, :] * shrinks[h]
                acc[rows, :] = out
                result.append((peaks[h], total))
            return tuple(result)

        lo, full = lo_ref[i], full_ref[i]
        state = tile(i, None, True, True)
        state = lax.fori_loop(full, i, lambda j, s: tile(j, s, False, False), state)
        state = lax.fori_loop(lo, full, lambda j, s: tile(j, s, True, False), state)
        for h in range(heads):
            rows = slice(h * HEAD_DIM, (h + 1) * HEAD_DIM)
            peak, total = state[h]
            acc[rows, :] = acc[rows, :] * (1.0 / total)
            lse_ref[h : h + 1, qs] = peak + jnp.log(total)
        out = acc[...]
        ot_ref[:, qs] = out.astype(bf16)
        o_ref[qs, :] = out.T.astype(bf16)
        return carry

    lax.fori_loop(0, blocks, query_block, 0)
    for mask in range(n_t):
        row = pl.multiple_of(jnp.bitwise_xor(t, mask) * count, count)
        copy = pltpu.make_async_copy(o_ref.at[pl.ds(row, count)], o_out[mask], sems.at[mask])
        copy.start()
        keep.append(copy)
    for copy in keep:
        copy.wait()


def attend_backward_kernel(
    heads, n_t, place_ref, lo_ref, full_ref, qt_ref, kt_ref, kn_ref, vn_ref, ot_ref, lse_ref,
    cos_ref, sin_ref, start_ref, w_ref, gain_ref, *rest
):
    do_in, rest = rest[:n_t], rest[n_t:]
    gt_ref, gf_ref, *gn_out = rest[:-8]
    do_ref, gn_ref, dot_, delta, dq, dk, dv, sems = rest[-8:]
    t = place_ref[2]
    cols = heads * HEAD_DIM
    blocks = do_ref.shape[0] // BLOCK
    count = do_ref.shape[0] // n_t
    copies = []
    for mask in range(n_t):
        row = pl.multiple_of(jnp.bitwise_xor(t, mask) * count, count)
        copies.append(
            pltpu.make_async_copy(do_in[mask], do_ref.at[pl.ds(row, count)], sems.at[mask])
        )
        copies[-1].start()
    for copy in copies:
        copy.wait()
    dk[...] = jnp.zeros_like(dk)
    dv[...] = jnp.zeros_like(dv)

    def prepare(i, carry):
        at = pl.ds(pl.multiple_of(i * BLOCK, BLOCK), BLOCK)
        grads = do_ref[at, :].astype(f32).T
        dot_[:, at] = grads.astype(bf16)
        prod = grads * ot_ref[:, at].astype(f32)
        for h in range(heads):
            delta[h : h + 1, at] = jnp.sum(
                prod[h * HEAD_DIM : (h + 1) * HEAD_DIM], axis=0, keepdims=True
            )
        return carry

    lax.fori_loop(0, blocks, prepare, 0)

    def query_block(step, carry):
        i = blocks - 1 - step
        qs = pl.ds(pl.multiple_of(i * BLOCK, BLOCK), BLOCK)
        start = start_ref[:, qs]
        key_iota = lax.broadcasted_iota(jnp.int32, (BLOCK, BLOCK), 0)
        query_pos = lax.broadcasted_iota(jnp.int32, (BLOCK, BLOCK), 1) + i * BLOCK
        dq[...] = jnp.zeros_like(dq)

        def tile(j, carry, masked):
            ks = pl.ds(pl.multiple_of(j * BLOCK, BLOCK), BLOCK)
            if masked:
                key_pos = key_iota + j * BLOCK
                allowed = (key_pos <= query_pos) & (key_pos >= start)
            hs = range(heads)
            rows = [slice(h * HEAD_DIM, (h + 1) * HEAD_DIM) for h in hs]
            q_h = [qt_ref[rows[h], qs] for h in hs]
            do_h = [dot_[rows[h], qs] for h in hs]
            scores = [mm(kn_ref[h, ks, :], q_h[h]) for h in hs]
            gp = [mm(vn_ref[h, ks, :], do_h[h]) for h in hs]
            for h in hs:
                s = scores[h]
                if masked:
                    s = jnp.where(allowed, s, -1e30)
                probs = jnp.exp(s - lse_ref[h : h + 1, qs])
                grad_scores = (probs * (gp[h] - delta[h : h + 1, qs])).astype(bf16)
                dv[rows[h], ks] += mm(do_h[h], probs.astype(bf16), NT)
                dk[rows[h], ks] += mm(q_h[h], grad_scores, NT)
                dq[rows[h], :] += mm(kt_ref[rows[h], ks], grad_scores)
            return carry

        lo, full = lo_ref[i], full_ref[i]
        tile(i, 0, True)
        lax.fori_loop(full, i, lambda j, s: tile(j, s, False), 0)
        lax.fori_loop(lo, full, lambda j, s: tile(j, s, True), 0)

        cosine, sine = cos_ref[:, qs], sin_ref[:, qs]
        pieces = []
        for source, factor in ((dq, HEAD_DIM ** (-0.5)), (dk, 1.0)):
            for h in range(heads):
                lo_row, mid, hi = h * HEAD_DIM, h * HEAD_DIM + HALF, (h + 1) * HEAD_DIM
                where = slice(None) if source is dq else qs
                a, b = source[lo_row:mid, where] * factor, source[mid:hi, where] * factor
                pieces += [a * cosine + b * sine, b * cosine - a * sine]
        half_v = 0.5 * dv[:, qs]
        gf_ref[qs, :] = half_v.T
        grads = jnp.concatenate(pieces + [half_v], axis=0)
        gt_ref[:, qs] = grads.astype(bf16)
        gn_ref[qs, :] = (mm(grads.T.astype(bf16), w_ref[...], NT) * gain_ref[...]).astype(bf16)
        return carry

    lax.fori_loop(0, blocks, query_block, 0)
    copies, outs = [], list(gn_out)
    for mask in range(n_t):
        row = jnp.bitwise_xor(t, mask) * count
        for size in piece_rows(mask, count, n_t):
            copies.append(
                pltpu.make_async_copy(
                    gn_ref.at[pl.ds(pl.multiple_of(row, size), size)],
                    outs.pop(0),
                    sems.at[len(copies)],
                )
            )
            row = row + size
    for copy in copies:
        copy.start()
    for copy in copies:
        copy.wait()


def feed_forward_kernel(
    masks, place_ref, xa_ref, xb_ref, ga_ref, gb_ref, wd_ref, *rest
):
    count = len(masks)
    pieces, (inner_ref, gvu_ref, u_ref, u_far_ref, w, sems) = rest[:count], rest[count:]
    t = place_ref[2]
    copies = []
    for piece, (mask, first) in zip(pieces, masks):
        at = w.at[pl.ds(first, piece.shape[0]), :, jnp.bitwise_xor(t, mask)]
        copies.append(pltpu.make_async_copy(piece, at, sems.at[len(copies)]))
        copies[-1].start()
    for copy in copies:
        copy.wait()
    features = xa_ref.shape[1]
    tokens = xa_ref.shape[0]
    ff = wd_ref.shape[0]
    step, high = 256, min(512, tokens)
    edges = list(range(0, ff, step)) + [ff]

    def weight(lo, hi):
        return w[:, :, :, :, lo:hi].reshape(features, hi - lo)

    for source, (x_ref, g_ref) in enumerate(((xa_ref, ga_ref), (xb_ref, gb_ref))):

        def rows_step(i, carry, x_ref=x_ref, g_ref=g_ref, source=source):
            rows = pl.ds(pl.multiple_of(i * high, high), high)
            outs = pl.ds(pl.multiple_of(source * tokens + i * high, high), high)
            x, g = x_ref[rows, :], g_ref[rows, :]
            for lo, hi in zip(edges[:-1], edges[1:]):
                gate = mm(x, weight(lo, hi))
                up = mm(x, weight(ff + lo, ff + hi))
                grad_inner = mm(g, wd_ref[lo:hi, :], NT)
                sig = jax.nn.sigmoid(gate)
                act = gate * sig
                inner_ref[outs, lo:hi] = (act * up).astype(bf16)
                gvu_ref[outs, lo:hi] = (
                    grad_inner * up * (sig * (1.0 + gate * (1.0 - sig)))
                ).astype(bf16)
                gvu_ref[outs, ff + lo : ff + hi] = (grad_inner * act).astype(bf16)
            u = mm(gvu_ref[outs, :], weight(0, 2 * ff), NT)
            if source == 0:
                u_ref[rows, :] = u
            else:
                u_far_ref[rows, :] = u.astype(bf16)
            return carry

        lax.fori_loop(0, tokens // high, rows_step, 0)


def gate_up_grad_kernel(n_t, place_ref, xa_ref, xb_ref, gvu_ref, *rest):
    *outs, xt, grads, sems = rest
    t = place_ref[2]
    tokens, features = xa_ref.shape
    n_z = grads.shape[0]
    own = grads.shape[3]
    step = 256
    for i in range(0, tokens, step):
        xt[:, i : i + step] = xa_ref[i : i + step, :].T
        xt[:, tokens + i : tokens + i + step] = xb_ref[i : i + step, :].T

    def columns(i, carry):
        at = pl.ds(pl.multiple_of(i * step, step), step)
        part = mm(xt[...], gvu_ref[:, at]).astype(bf16)
        grads[:, :, :, :, at] = part.reshape(n_z, 2, n_t, own, step)
        return carry

    lax.fori_loop(0, gvu_ref.shape[1] // step, columns, 0)
    copies, outs = [], list(outs)
    for mask in range(n_t):
        copy = pltpu.make_async_copy(
            grads.at[:, :, jnp.bitwise_xor(t, mask)], outs[mask], sems.at[mask]
        )
        copy.start()
        copies.append(copy)
    for copy in copies:
        copy.wait()


def load_output_weight(place_ref, near, far, wo, sems):
    z, core = place_ref[0], place_ref[1]
    n_z = near.shape[0]
    copies = []
    for other, ref in enumerate((near, far)):
        for i in range(n_z):
            at = wo.at[2 * lax.rem(z - i + n_z, n_z) + jnp.bitwise_xor(core, other)]
            copies.append(pltpu.make_async_copy(ref.at[i], at, sems.at[len(copies)]))
            copies[-1].start()
    for copy in copies:
        copy.wait()


def project_out_kernel(n_t, place_ref, token_ref, near, far, *rest):
    *att, hidden_ref, unit_ref, wo, sems = rest
    load_output_weight(place_ref, near, far, wo, sems)
    t = place_ref[2]
    n_dp, _, height, cols = wo.shape
    step = 256

    def rows_step(i, carry):
        rows = pl.ds(pl.multiple_of(i * step, step), step)
        hidden = token_ref[rows, :].astype(f32)
        for mask, ref in enumerate(att):
            weight = wo[:, jnp.bitwise_xor(t, mask)].reshape(n_dp * height, cols)
            hidden = hidden + mm(ref[rows, :], weight, NT)
        hidden_ref[rows, :] = hidden
        mean = jnp.mean(hidden * hidden, axis=-1, keepdims=True)
        unit_ref[rows, :] = (hidden * lax.rsqrt(mean + eps)).astype(bf16)
        return carry

    lax.fori_loop(0, token_ref.shape[0] // step, rows_step, 0)


def norm_backward(values, scaled, inverse):
    dot = jnp.sum(scaled * values, axis=-1, keepdims=True) / values.shape[-1]
    return inverse * scaled - values * (inverse * inverse * inverse * dot)


def branch_grad_kernel(
    place_ref, hidden_ref, u_ref, u_got_ref, g_ref, near, far, grad_ref, branch_ref, *rest
):
    *outs, wo, sems = rest
    load_output_weight(place_ref, near, far, wo, sems)
    t = place_ref[2]
    n_dp, n_t, height, cols = wo.shape
    step = 256

    def rows_step(i, carry):
        rows = pl.ds(pl.multiple_of(i * step, step), step)
        hidden = hidden_ref[rows, :]
        scaled = u_ref[rows, :] + u_got_ref[rows, :].astype(f32)
        inverse = lax.rsqrt(jnp.mean(hidden * hidden, axis=-1, keepdims=True) + eps)
        grad = g_ref[rows, :].astype(f32) + norm_backward(hidden, scaled, inverse)
        grad_ref[rows, :] = grad
        branch = grad.astype(bf16)
        branch_ref[rows, :] = branch
        for mask, out in enumerate(outs):
            weight = wo[:, jnp.bitwise_xor(t, mask)].reshape(n_dp * height, cols)
            out[rows, :] = mm(branch, weight).astype(bf16)
        return carry

    lax.fori_loop(0, hidden_ref.shape[0] // step, rows_step, 0)


def output_grad_kernel(place_ref, branch_ref, *rest):
    *att, keep_ref, give_ref, turned, grads = rest
    core, t = place_ref[1], place_ref[2]
    n_z, n_t, height, cols = keep_ref.shape
    turned[...] = branch_ref[...].T
    for mask, ref in enumerate(att):
        part = mm(turned[...], ref[...]).astype(bf16).reshape(n_z, 2, height, cols)
        for which in range(2):
            grads[which, :, jnp.bitwise_xor(t, mask)] = part[:, which]
    keep_ref[...] = grads[core]
    give_ref[...] = grads[1 - core]


def projection_grad_kernel(place_ref, gt_ref, x_ref, keep_ref, give_ref, grads, sems):
    core = place_ref[1]
    _, n_z, height, _ = grads.shape

    def columns(i, carry):
        at = pl.ds(pl.multiple_of(i * 2 * height, 2 * height), 2 * height)
        part = mm(gt_ref[...], x_ref[:, at]).T.astype(bf16)
        grads[0, i] = part[:height]
        grads[1, i] = part[height:]
        return carry

    lax.fori_loop(0, n_z, columns, 0)
    copies = [
        pltpu.make_async_copy(grads.at[core], keep_ref, sems.at[0]),
        pltpu.make_async_copy(grads.at[1 - core], give_ref, sems.at[1]),
    ]
    for copy in copies:
        copy.start()
    for copy in copies:
        copy.wait()


def vmem(n):
    return [pl.BlockSpec(memory_space=pltpu.VMEM)] * n


def smem(n):
    return [pl.BlockSpec(memory_space=pltpu.SMEM)] * n


def hbm(n):
    return [pl.BlockSpec(memory_space=pl.ANY)] * n


sds = jax.ShapeDtypeStruct


def call(kernel, name, gflops, in_specs, out_specs, out_shape, scratch, args):
    return pl.pallas_call(
        kernel,
        out_shape=tuple(out_shape),
        in_specs=in_specs,
        out_specs=tuple(out_specs),
        scratch_shapes=scratch,
        compiler_params=pltpu.CompilerParams(vmem_limit_bytes=VMEM_LIMIT),
        cost_estimate=pl.CostEstimate(
            flops=int(gflops * 1e9), bytes_accessed=1000, transcendentals=0
        ),
        name=name,
    )(*args)


def attend_forward(
    heads, n_t, place, lo, full, x_pieces, near, far, fv, cosine, sine, start, gain
):
    rows, cols = fv.shape
    x_at = [(mask, offset) for mask, offset, _ in x_pieces]
    pieces = [piece for _, _, piece in x_pieces]
    features, width = pieces[0].shape[1], near.shape[2]
    return call(
        functools.partial(attend_forward_kernel, heads, n_t, x_at),
        "attend_forward",
        5,
        smem(3) + vmem(5) + hbm(len(pieces) + 2),
        vmem(6) + hbm(2 + n_t),
        [
            sds((cols, rows), bf16),
            sds((cols, rows), bf16),
            sds((heads, rows, HEAD_DIM), bf16),
            sds((heads, rows, HEAD_DIM), bf16),
            sds((cols, rows), bf16),
            sds((heads, rows), f32),
            sds((rows, features), bf16),
            sds((features, width), bf16),
        ]
        + [sds((rows // n_t, cols), bf16)] * n_t,
        [
            pltpu.VMEM((rows, features), bf16),
            pltpu.VMEM((features, width), bf16),
            pltpu.VMEM((width, features), bf16),
            pltpu.VMEM((cols, rows), bf16),
            pltpu.VMEM((rows, cols), bf16),
            pltpu.VMEM((cols, BLOCK), f32),
            pltpu.SemaphoreType.DMA((len(pieces) + 2 * near.shape[0] + 2,)),
        ],
        (place, lo, full, fv, cosine, sine, start, gain, *pieces, near, far),
    )


def attend_backward(
    heads, n_t, place, lo, full, saved, grads, cosine, sine, start, w, gain
):
    rows, cols = start.shape[1], heads * HEAD_DIM
    count = rows // n_t
    features = w.shape[0]
    sizes = {mask: piece_rows(mask, count, n_t) for mask in range(n_t)}
    flat = [size for mask in range(n_t) for size in sizes[mask]]
    outs = call(
        functools.partial(attend_backward_kernel, heads, n_t),
        "attend_backward",
        10,
        smem(3) + vmem(11) + hbm(n_t),
        vmem(2) + hbm(len(flat)),
        [sds((3 * cols, rows), bf16), sds((rows, cols), f32)]
        + [sds((size, features), bf16) for size in flat],
        [
            pltpu.VMEM((rows, cols), bf16),
            pltpu.VMEM((rows, features), bf16),
            pltpu.VMEM((cols, rows), bf16),
            pltpu.VMEM((heads, rows), f32),
            pltpu.VMEM((cols, BLOCK), f32),
            pltpu.VMEM((cols, rows), f32),
            pltpu.VMEM((cols, rows), f32),
            pltpu.SemaphoreType.DMA((len(flat),)),
        ],
        (place, lo, full, *saved, cosine, sine, start, w, gain, *grads),
    )
    pieces = list(outs[2:])
    return outs[0], outs[1], {m: [pieces.pop(0) for _ in sizes[m]] for m in range(n_t)}


def feed_forward(n_z, n_t, place, xa, xb, ga, gb, wd, gathered):
    tokens, features = xa.shape
    ff = wd.shape[0]
    pieces, masks = [], []
    for mask, parts in gathered.items():
        first = 0
        for part in parts:
            pieces.append(part)
            masks.append((mask, first))
            first += part.shape[0]
    return call(
        functools.partial(feed_forward_kernel, masks),
        "feed_forward",
        0,
        smem(1) + vmem(5) + hbm(len(pieces)),
        vmem(4),
        [
            sds((2 * tokens, ff), bf16),
            sds((2 * tokens, 2 * ff), bf16),
            sds((tokens, features), f32),
            sds((tokens, features), bf16),
        ],
        [
            pltpu.VMEM((n_z, 2, n_t, features // (2 * n_z * n_t), 2 * ff), bf16),
            pltpu.SemaphoreType.DMA((len(pieces),)),
        ],
        (place, xa, xb, ga, gb, wd, *pieces),
    )


def gate_up_grad(n_z, n_t, place, xa, xb, gvu):
    tokens, features = xa.shape
    own = features // (2 * n_z * n_t)
    outs = call(
        functools.partial(gate_up_grad_kernel, n_t),
        "gate_up_grad",
        0,
        smem(1) + vmem(3),
        hbm(n_t),
        [sds((n_z, 2, own, gvu.shape[1]), bf16)] * n_t,
        [
            pltpu.VMEM((features, 2 * tokens), bf16),
            pltpu.VMEM((n_z, 2, n_t, own, gvu.shape[1]), bf16),
            pltpu.SemaphoreType.DMA((n_t,)),
        ],
        (place, xa, xb, gvu),
    )
    return list(outs)


def output_weight_scratch(near):
    n_z, n_t, height, cols = near.shape
    return [
        pltpu.VMEM((2 * n_z, n_t, height, cols), bf16),
        pltpu.SemaphoreType.DMA((2 * n_z,)),
    ]


def project_out(place, tokens, att, near, far):
    return call(
        functools.partial(project_out_kernel, len(att)),
        "project_out",
        20,
        smem(1) + vmem(1) + hbm(2) + vmem(len(att)),
        vmem(2),
        [sds(tokens.shape, f32), sds(tokens.shape, bf16)],
        output_weight_scratch(near),
        (place, tokens, near, far, *att),
    )


def branch_grad(place, hidden, u, u_got, g, near, far):
    _, n_t, _, cols = near.shape
    outs = call(
        branch_grad_kernel,
        "branch_grad",
        0,
        smem(1) + vmem(4) + hbm(2),
        vmem(2 + n_t),
        [sds(hidden.shape, f32), sds(hidden.shape, bf16)]
        + [sds((hidden.shape[0], cols), bf16)] * n_t,
        output_weight_scratch(near),
        (place, hidden, u, u_got, g, near, far),
    )
    return outs[0], outs[1], list(outs[2:])


def output_grad(n_z, place, branch, att):
    n_t, cols = len(att), att[0].shape[1]
    shape = (n_z, n_t, branch.shape[1] // (2 * n_z), cols)
    return call(
        output_grad_kernel,
        "output_grad",
        0,
        smem(1) + vmem(1 + n_t),
        vmem(2),
        [sds(shape, bf16)] * 2,
        [pltpu.VMEM(branch.shape[::-1], bf16), pltpu.VMEM((2,) + shape, bf16)],
        (place, branch, *att),
    )


def projection_grad(n_z, place, gt, x):
    height = x.shape[1] // (2 * n_z)
    return call(
        projection_grad_kernel,
        "projection_grad",
        0,
        smem(1) + vmem(2),
        hbm(2),
        [sds((n_z, height, gt.shape[0]), bf16)] * 2,
        [
            pltpu.VMEM((2, n_z, height, gt.shape[0]), bf16),
            pltpu.SemaphoreType.DMA((2,)),
        ],
        (place, gt, x),
    )


def doc_layout(doc_lengths, total):
    doc_ends = jnp.cumsum(doc_lengths)
    index = jnp.arange(total, dtype=jnp.int32)
    passed = (index[:, None] >= doc_ends[None, :]).astype(jnp.int32)
    return jnp.sum(passed * doc_lengths[None, :], axis=1)


def split_cols(weight, n_z):
    rows = weight.shape[0]
    return weight.reshape(rows, n_z, 2, -1).transpose(2, 0, 1, 3).reshape(2, rows, -1)


def join_cols(parts, n_z):
    rows = parts.shape[1]
    return parts.reshape(2, rows, n_z, -1).transpose(1, 2, 0, 3).reshape(rows, -1)


def body(
    tokens, lengths, first_values, attn_gain, query_weight, key_weight, value_weight,
    output_weight, mlp_gain, gate_weight, up_weight, down_weight, out_cotangent,
):
    n_t = lax.axis_size("tensor")
    n_z = lax.axis_size("z")
    t = lax.axis_index("tensor")
    core = lax.axis_index("core")
    place = jnp.stack([lax.axis_index("z"), core, t]).astype(jnp.int32)
    masks = range(n_t)
    count, features = tokens.shape
    rows = count * n_t
    wrows, cols = query_weight.shape
    heads = cols // HEAD_DIM
    ff_core = gate_weight.shape[1] // 2

    def by_core(near, far, axis):
        return jnp.where(
            core == 0, jnp.stack([near, far], axis=axis), jnp.stack([far, near], axis=axis)
        )

    token_f = tokens.astype(f32)
    inverse_in = lax.rsqrt(jnp.mean(token_f * token_f, axis=-1, keepdims=True) + eps)
    unit_in = (token_f * inverse_in).astype(bf16)
    with jax.named_scope("normed_tokens"):
        x_near = gather_near(unit_in)

    own_joint = jnp.concatenate([query_weight, key_weight, value_weight], axis=1)
    own_gains = attn_gain.shape[0]
    gain_rows = jnp.pad(attn_gain[None], ((0, 15), (0, 3 * cols - own_gains)))
    with jax.named_scope("attention_weights_z"):
        near = spread(jnp.concatenate([own_joint, gain_rows]), "z")

    gain_mid = mlp_gain.astype(f32)[:, None]
    both = jnp.concatenate(
        [split_cols(gate_weight, n_z), split_cols(up_weight, n_z)], axis=2
    ).astype(f32)
    both = (both * gain_mid[None]).astype(bf16)
    mine = lax.dynamic_index_in_dim(both, core, 0, False)
    with jax.named_scope("gate_up_core"):
        theirs = swap_core(lax.dynamic_index_in_dim(both, 1 - core, 0, False))
    with jax.named_scope("core_tokens"):
        grad_far = swap_core(out_cotangent)
    pair = by_core(mine, theirs, 0)

    start = doc_layout(lengths[0], rows)
    position = (jnp.arange(rows, dtype=jnp.int32) - start).astype(f32)
    freqs = rope_base ** (-jnp.arange(HALF, dtype=f32) * 2.0 / HEAD_DIM)
    angles = freqs[:, None] * position[None, :]
    cosine, sine = jnp.cos(angles), jnp.sin(angles)
    block_starts = start.reshape(-1, BLOCK)
    lo = block_starts[:, 0] // BLOCK
    full = jnp.minimum(
        (block_starts[:, -1] + BLOCK - 1) // BLOCK,
        jnp.arange(rows // BLOCK, dtype=jnp.int32),
    )
    start = start[None]

    x_near, near, pair, grad_far, output_weight, down_weight = together(
        x_near, near, pair, grad_far, output_weight, down_weight
    )

    with jax.named_scope("gate_up_z"):
        column = spread(pair, "z")
    with jax.named_scope("normed_tokens"):
        x_far = gather_far(unit_in, x_near)
    with jax.named_scope("attention_weights_core"):
        far = swap_core(near)
    drows = down_weight.shape[0]
    brows = drows + output_weight.size // features
    column_gain = by_core(near[:, wrows, :own_gains], far[:, wrows, :own_gains], 1).reshape(1, -1)
    with jax.named_scope("output_down_tensor"):
        slab = [
            down_weight,
            output_weight.reshape(-1, features),
            jnp.pad(column_gain, ((0, 15), (0, features - column_gain.shape[1]))),
        ]
        slabs = spread_tensor(jnp.concatenate(slab, axis=0))

    x_far, far, slabs, column = together(x_far, far, slabs, column)

    slab = by_index(slabs)
    with jax.named_scope("down_z"):
        down = lax.all_gather(slab[:, :drows].reshape(-1, features), "z", tiled=True)
    with jax.named_scope("output_weight_z"):
        out_near = send_z(slab[:, drows:brows].reshape(n_t, wrows, cols))
    gain = slab[:, brows, : column_gain.shape[1]].reshape(n_t, 2 * n_z, own_gains)
    gain = gain.transpose(1, 0, 2).astype(f32)
    gain_rows = lax.dynamic_index_in_dim(gain, place[0] * 2 + core, 0, False).reshape(-1, 1)
    gain = gain.reshape(1, features)
    with jax.named_scope("gate_up_tensor"):
        gu_near = gather_near(column)
    x_pieces = []
    for mask, parts in x_far.items():
        offset = 0
        for part in parts:
            x_pieces.append((mask, offset, part))
            offset += part.shape[0]
    qt, kt, kn, vn, ot, lse, x_full, joint_weight, *attended = attend_forward(
        heads, n_t, place, lo, full, x_pieces, near, far, first_values, cosine, sine, start, gain
    )

    attended, gu_near = together(attended, gu_near)

    with jax.named_scope("attended"):
        att = swap_all(attended)
    lse, out_near = together(lse, out_near)
    with jax.named_scope("output_weight_core"):
        out_far = swap_core(out_near)
    att, out_far, passed = together(att, out_far, pass_on(gu_near))
    with jax.named_scope("gate_up_tensor"):
        gathered = gather_far(column, gu_near, passed)
    hidden, unit_mid = project_out(place, tokens, att, out_near, out_far)
    unit_mid, gathered = together(unit_mid, gathered)
    with jax.named_scope("core_tokens"):
        unit_far = swap_core(unit_mid)

    inner, gvu, u_own, u_give = feed_forward(
        n_z, n_t, place, unit_mid, unit_far, out_cotangent, grad_far, down, gathered
    )
    with jax.named_scope("u_core"):
        u_got = swap_core(u_give)
    grad_both = jnp.concatenate([out_cotangent, grad_far], axis=0)
    grad_dn = mm(inner, grad_both, TN).astype(bf16).reshape(n_z, -1, features)

    u_got, grad_dn = together(u_got, grad_dn)

    with jax.named_scope("grad_down_z"):
        dn = lax.psum_scatter(grad_dn.reshape(-1, features), "z", scatter_dimension=0, tiled=True)
    grad_hidden, branch, grad_att = branch_grad(
        place, hidden, u_own, u_got, out_cotangent, out_near, out_far
    )
    with jax.named_scope("grad_attended"):
        grad_att = swap_all(grad_att)
    gu_parts = gate_up_grad(n_z, n_t, place, unit_mid, unit_far, gvu)
    keep_ow, give_ow = output_grad(n_z, place, branch, att)
    with jax.named_scope("grad_output_core"):
        got_ow = swap_core(give_ow)

    grad_att, gu_parts, got_ow = together(grad_att, gu_parts, got_ow)

    with jax.named_scope("grad_gate_up_tensor"):
        gu_terms = swap_all(gu_parts)
    with jax.named_scope("grad_output_z"):
        ow_terms = exchange(add(keep_ow, got_ow), "z")
    gt, grad_first, in_parts = attend_backward(
        heads, n_t, place, lo, full, (qt, kt, kn, vn, ot, lse), grad_att, cosine, sine, start,
        joint_weight, gain,
    )

    near_terms, last_term = gu_terms[:-1], gu_terms[-1:]
    in_parts, gt, ow_terms, inner, near_terms = together(
        in_parts, gt, ow_terms, inner, near_terms
    )

    with jax.named_scope("grad_normed"):
        in_far = scatter_far(in_parts)
    keep_jw, give_jw = projection_grad(n_z, place, gt, x_full)
    with jax.named_scope("grad_projection_core"):
        got_jw = swap_core(give_jw)
    jw_sum = add(keep_jw, got_jw)
    with jax.named_scope("grad_projection_z"):
        jw_terms = exchange(jw_sum, "z")
    out_part = mm(inner, down)
    out_give = out_part[count:].astype(bf16)

    jw_terms, last_term, out_give, dn = together(jw_terms, last_term, out_give, dn)
    gu_terms = near_terms + last_term

    with jax.named_scope("layer_out"):
        out_got = swap_core(out_give)
    layer_out = (hidden + out_part[:count] + out_got.astype(f32)).astype(bf16)
    gu_sums = sums_z(gu_terms)
    gu_sums, in_far = together(gu_sums, in_far)
    with jax.named_scope("grad_gate_up_z"):
        gu_terms = scatter_z(gu_sums)
    in_joined = scatter_join(in_parts, in_far)
    in_joined, jw_terms, ow_terms, dn = together(in_joined, jw_terms, ow_terms, dn)
    with jax.named_scope("grad_normed"):
        in_terms = scatter_near(in_parts, in_joined)

    ow = total(ow_terms).astype(bf16).reshape(n_t, -1, features)
    with jax.named_scope("grad_output_down_tensor"):
        both_terms = exchange(jnp.concatenate([dn.reshape(n_t, -1, features), ow], axis=1), "tensor")

    in_terms, gu_terms, jw_terms, both_terms = together(in_terms, gu_terms, jw_terms, both_terms)
    grad_down = total(both_terms)
    grad_output = grad_down[drows:].reshape(wrows, cols)
    grad_down = grad_down[:drows]

    grad_jw = total(jw_terms)
    gain_part = jnp.sum(grad_jw * own_joint.astype(f32), axis=1).reshape(n_t, -1)
    with jax.named_scope("grad_gain"):
        grad_attn_gain = total(exchange(gain_part, "tensor"))[None]
    grad_jw = grad_jw * gain_rows

    gu = total(gu_terms)
    gu_mine = lax.dynamic_index_in_dim(gu, core, 0, False)
    with jax.named_scope("grad_gate_up_core"):
        gu_other = swap_core(lax.dynamic_index_in_dim(gu, 1 - core, 0, False))

    grad_input = grad_hidden + norm_backward(token_f, total(in_terms), inverse_in)

    gu = by_core(gu_mine, gu_other, 0)
    grad_gate = join_cols(gu[:, :, :ff_core], n_z)
    grad_up = join_cols(gu[:, :, ff_core:], n_z)
    grad_mlp_gain = jnp.sum(
        grad_gate * gate_weight.astype(f32) + grad_up * up_weight.astype(f32), axis=1
    )
    grad_gate = grad_gate * gain_mid
    grad_up = grad_up * gain_mid

    return (
        layer_out,
        grad_input,
        grad_first,
        grad_attn_gain[0],
        grad_jw[:, :cols],
        grad_jw[:, cols : 2 * cols],
        grad_jw[:, 2 * cols :],
        grad_output,
        grad_mlp_gain,
        grad_gate,
        grad_up,
        grad_down,
    )


def solution(mesh):
    n_dp, n_t = mesh.shape["dp"], mesh.shape["tensor"]
    mesh = Mesh(mesh.devices.reshape(n_dp // 2, 2, n_t), ("z", "core", "tensor"))
    dp = ("z", "core")
    both = ("z", "core", "tensor")
    in_specs = (
        P(both, None),
        P(dp, None),
        P(dp, "tensor"),
        P(both),
        P(dp, "tensor"),
        P(dp, "tensor"),
        P(dp, "tensor"),
        P(dp, "tensor"),
        P(both),
        P(both, None),
        P(both, None),
        P(both, None),
        P(both, None),
    )
    out_specs = (
        P(both, None),
        P(both, None),
        P(dp, "tensor"),
        P(both),
        P(dp, "tensor"),
        P(dp, "tensor"),
        P(dp, "tensor"),
        P(dp, "tensor"),
        P(both),
        P(both, None),
        P(both, None),
        P(both, None),
    )
    return jax.shard_map(body, mesh=mesh, in_specs=in_specs, out_specs=out_specs, check_vma=False)
```

```python
import functools

import jax
import jax.numpy as jnp
from jax import lax
from jax.experimental import pallas as pl
from jax.experimental.pallas import tpu as pltpu
from jax.sharding import Mesh, PartitionSpec as P

HEAD_DIM = 64
HALF = HEAD_DIM // 2
BLOCK = 256
VMEM_LIMIT = 60 * 1024 * 1024

eps = 1e-06
rope_base = 10000.0
bf16 = jnp.bfloat16
f32 = jnp.float32

NN = (((1,), (0,)), ((), ()))
NT = (((1,), (1,)), ((), ()))
TN = (((0,), (0,)), ((), ()))


def mm(left, right, dims=NN):
    return lax.dot_general(left, right, dims, preferred_element_type=f32)


def swap_tensor(value, mask):
    size = lax.axis_size("tensor")
    return lax.ppermute(value, "tensor", [(i, i ^ mask) for i in range(size)])


def swap_core(value):
    return lax.ppermute(value, "core", [(0, 1), (1, 0)])


def shift_z(value, step):
    size = lax.axis_size("z")
    return lax.ppermute(value, "z", [(i, (i + step) % size) for i in range(size)])


def bit_orders():
    bits = [1 << b for b in range(lax.axis_size("tensor").bit_length() - 1)]
    return bits, bits[1:] + bits[:1]


def together(*values):
    return lax.optimization_barrier(values)


def halves(value):
    middle = value.shape[0] // 2
    return value[:middle], value[middle:]


def gather_near(value):
    if lax.axis_size("tensor") != 4:
        return []
    return [swap_tensor(value, 1), swap_tensor(value, 2)]


def pass_on(near):
    return [halves(near[0])[0], halves(near[1])[1]] if near else []


def gather_far(value, near, passed=()):
    if near:
        if not passed:
            passed = pass_on(near)
        far = [swap_tensor(passed[0], 2), swap_tensor(passed[1], 1)]
        return {0: [value], 1: [near[0]], 2: [near[1]], 3: far}
    parts = []
    for piece, bits in zip(halves(value), bit_orders()):
        have = {0: piece}
        for bit in bits:
            have.update({m ^ bit: swap_tensor(got, bit) for m, got in list(have.items())})
        parts.append(have)
    return {mask: [part[mask] for part in parts] for mask in parts[0]}


def add(left, right):
    return (left.astype(f32) + right.astype(f32)).astype(bf16)


def scatter_far(parts):
    if lax.axis_size("tensor") != 4:
        return []
    upper, lower = parts[3]
    return [swap_tensor(upper, 1), swap_tensor(lower, 2)]


def scatter_join(parts, far):
    if not far:
        return []
    to_x, to_y = parts[1][0], parts[2][0]
    middle = to_y.shape[0] // 2
    return [
        lax.dynamic_update_slice_in_dim(to_x, add(to_x[middle:], far[1]), middle, 0),
        lax.dynamic_update_slice_in_dim(to_y, add(to_y[:middle], far[0]), 0, 0),
    ]


def scatter_near(parts, joined):
    if joined:
        return [parts[0][0], swap_tensor(joined[0], 1), swap_tensor(joined[1], 2)]
    parts = {mask: jnp.concatenate(part, axis=0) for mask, part in parts.items()}
    sums = []
    for which, bits in enumerate(bit_orders()):
        left = {mask: halves(part)[which] for mask, part in parts.items()}
        for bit in bits:
            for mask in [m for m in left if not m & bit]:
                left[mask] = add(left[mask], swap_tensor(left.pop(mask | bit), bit))
        sums.append(left[0])
    return [jnp.concatenate(sums, axis=0)]


def spread_tensor(value):
    return swap_all([value] * lax.axis_size("tensor"))


def swap_all(pieces):
    return [swap_tensor(piece, mask) if mask else piece for mask, piece in enumerate(pieces)]


def by_index(pieces):
    here = lax.axis_index("tensor")
    order = []
    for place in range(len(pieces)):
        piece = pieces[0]
        for mask in range(1, len(pieces)):
            piece = jnp.where(here ^ place == mask, pieces[mask], piece)
        order.append(piece)
    return jnp.stack(order)


def send_z(value):
    return jnp.stack([value] + [shift_z(value, i) for i in range(1, lax.axis_size("z"))])


def sums_z(terms):
    depth = lax.axis_size("z")
    here = lax.axis_index("z")
    take = lambda term, i: lax.dynamic_index_in_dim(term, (here + i) % depth, 0, False)
    sums = [total([take(term, i) for term in terms]) for i in range(depth)]
    return [sums[0]] + [part.astype(bf16) for part in sums[1:]]


def scatter_z(sums):
    return [sums[0]] + [shift_z(part, i + 1) for i, part in enumerate(sums[1:])]


def exchange(value, axis):
    return lax.all_to_all(value, axis, 0, 0)


def spread(value, axis):
    return exchange(jnp.broadcast_to(value[None], (lax.axis_size(axis),) + value.shape), axis)


def piece_rows(mask, height, n_t):
    return [height // 2] * 2 if mask == 3 and n_t == 4 else [height]


def total(terms):
    terms = [terms[i].astype(f32) for i in range(len(terms))]
    return sum(terms[1:], terms[0])


def attend_forward_kernel(
    heads, n_t, x_at, place_ref, lo_ref, full_ref, fv_ref, cos_ref, sin_ref, start_ref, gain_ref, *rest
):
    x_in, w_in, rest = rest[: len(x_at)], rest[len(x_at) : len(x_at) + 2], rest[len(x_at) + 2 :]
    qt_ref, kt_ref, kn_ref, vn_ref, ot_ref, lse_ref, x_out, w_out = rest[:8]
    o_out, (x_ref, w_ref, wt, vt, o_ref, acc, sems) = rest[8 : 8 + n_t], rest[8 + n_t :]
    core, t = place_ref[1], place_ref[2]
    n_z = w_in[0].shape[0]
    height = w_ref.shape[0] // (2 * n_z)
    cols = heads * HEAD_DIM
    blocks = x_ref.shape[0] // BLOCK
    count = x_ref.shape[0] // n_t
    copies = []
    for other, ref in enumerate(w_in):
        for z in range(n_z):
            row = pl.multiple_of((2 * z + jnp.bitwise_xor(core, other)) * height, height)
            copies.append((ref.at[z, pl.ds(0, height)], w_ref.at[pl.ds(row, height)]))
    for ref, (mask, offset) in zip(x_in, x_at):
        row = jnp.bitwise_xor(t, mask) * count + offset
        size = ref.shape[0]
        copies.append((ref, x_ref.at[pl.ds(pl.multiple_of(row, size), size)]))
    copies = [pltpu.make_async_copy(a, b, sems.at[i]) for i, (a, b) in enumerate(copies)]
    for copy in copies:
        copy.start()
    for copy in copies:
        copy.wait()
    keep = [
        pltpu.make_async_copy(x_ref, x_out, sems.at[len(copies)]),
        pltpu.make_async_copy(w_ref, w_out, sems.at[len(copies) + 1]),
    ]
    for copy in keep:
        copy.start()
    wt[...] = (w_ref[...].astype(f32).T * gain_ref[...]).astype(bf16)

    def project(i, carry):
        at = pl.ds(pl.multiple_of(i * BLOCK, BLOCK), BLOCK)
        joint = mm(wt[...], x_ref[at, :], NT)
        cosine, sine = cos_ref[:, at], sin_ref[:, at]
        first = fv_ref[at, :].astype(f32).T
        for h in range(heads):
            lo, mid, hi = h * HEAD_DIM, h * HEAD_DIM + HALF, (h + 1) * HEAD_DIM
            qa, qb = joint[lo:mid], joint[mid:hi]
            q = jnp.concatenate([qa * cosine - qb * sine, qb * cosine + qa * sine], axis=0)
            qt_ref[lo:hi, at] = (q * HEAD_DIM ** (-0.5)).astype(bf16)
            ka, kb = joint[cols + lo : cols + mid], joint[cols + mid : cols + hi]
            k = jnp.concatenate([ka * cosine - kb * sine, kb * cosine + ka * sine], axis=0)
            kt_ref[lo:hi, at] = k.astype(bf16)
            kn_ref[h, at, :] = k.T.astype(bf16)
            v = 0.5 * joint[2 * cols + lo : 2 * cols + hi] + 0.5 * first[lo:hi]
            vt[lo:hi, at] = v.astype(bf16)
            vn_ref[h, at, :] = v.T.astype(bf16)
        return carry

    lax.fori_loop(0, blocks, project, 0)

    def query_block(i, carry):
        qs = pl.ds(pl.multiple_of(i * BLOCK, BLOCK), BLOCK)
        start = start_ref[:, qs]
        key_iota = lax.broadcasted_iota(jnp.int32, (BLOCK, BLOCK), 0)
        query_pos = lax.broadcasted_iota(jnp.int32, (BLOCK, BLOCK), 1) + i * BLOCK

        def tile(j, state, masked, opening):
            ks = pl.ds(pl.multiple_of(j * BLOCK, BLOCK), BLOCK)
            if masked:
                key_pos = key_iota + j * BLOCK
                allowed = (key_pos <= query_pos) & (key_pos >= start)
            result = []
            all_scores = [
                mm(kn_ref[h, ks, :], qt_ref[h * HEAD_DIM : (h + 1) * HEAD_DIM, qs])
                for h in range(heads)
            ]
            if masked:
                all_scores = [jnp.where(allowed, sc, -1e30) for sc in all_scores]
            peaks = [jnp.max(sc, axis=0, keepdims=True) for sc in all_scores]
            if not opening:
                shrinks = []
                for h in range(heads):
                    peaks[h] = jnp.maximum(state[h][0], peaks[h])
                    shrinks.append(jnp.exp(state[h][0] - peaks[h]))
            all_probs = [jnp.exp(sc - pk) for sc, pk in zip(all_scores, peaks)]
            for h in range(heads):
                rows = slice(h * HEAD_DIM, (h + 1) * HEAD_DIM)
                total = jnp.sum(all_probs[h], axis=0, keepdims=True)
                out = mm(vt[rows, ks], all_probs[h].astype(bf16))
                if not opening:
                    total = total + state[h][1] * shrinks[h]
                    out = out + acc[rows, :] * shrinks[h]
                acc[rows, :] = out
                result.append((peaks[h], total))
            return tuple(result)

        lo, full = lo_ref[i], full_ref[i]
        state = tile(i, None, True, True)
        state = lax.fori_loop(full, i, lambda j, s: tile(j, s, False, False), state)
        state = lax.fori_loop(lo, full, lambda j, s: tile(j, s, True, False), state)
        for h in range(heads):
            rows = slice(h * HEAD_DIM, (h + 1) * HEAD_DIM)
            peak, total = state[h]
            acc[rows, :] = acc[rows, :] * (1.0 / total)
            lse_ref[h : h + 1, qs] = peak + jnp.log(total)
        out = acc[...]
        ot_ref[:, qs] = out.astype(bf16)
        o_ref[qs, :] = out.T.astype(bf16)
        return carry

    lax.fori_loop(0, blocks, query_block, 0)
    for mask in range(n_t):
        row = pl.multiple_of(jnp.bitwise_xor(t, mask) * count, count)
        copy = pltpu.make_async_copy(o_ref.at[pl.ds(row, count)], o_out[mask], sems.at[mask])
        copy.start()
        keep.append(copy)
    for copy in keep:
        copy.wait()


def attend_backward_kernel(
    heads, n_t, place_ref, lo_ref, full_ref, qt_ref, kt_ref, kn_ref, vn_ref, ot_ref, lse_ref,
    cos_ref, sin_ref, start_ref, w_ref, gain_ref, *rest
):
    do_in, rest = rest[:n_t], rest[n_t:]
    gt_ref, gf_ref, *gn_out = rest[:-8]
    do_ref, gn_ref, dot_, delta, dq, dk, dv, sems = rest[-8:]
    t = place_ref[2]
    cols = heads * HEAD_DIM
    blocks = do_ref.shape[0] // BLOCK
    count = do_ref.shape[0] // n_t
    copies = []
    for mask in range(n_t):
        row = pl.multiple_of(jnp.bitwise_xor(t, mask) * count, count)
        copies.append(
            pltpu.make_async_copy(do_in[mask], do_ref.at[pl.ds(row, count)], sems.at[mask])
        )
        copies[-1].start()
    for copy in copies:
        copy.wait()
    dk[...] = jnp.zeros_like(dk)
    dv[...] = jnp.zeros_like(dv)

    def prepare(i, carry):
        at = pl.ds(pl.multiple_of(i * BLOCK, BLOCK), BLOCK)
        grads = do_ref[at, :].astype(f32).T
        dot_[:, at] = grads.astype(bf16)
        prod = grads * ot_ref[:, at].astype(f32)
        for h in range(heads):
            delta[h : h + 1, at] = jnp.sum(
                prod[h * HEAD_DIM : (h + 1) * HEAD_DIM], axis=0, keepdims=True
            )
        return carry

    lax.fori_loop(0, blocks, prepare, 0)

    def query_block(step, carry):
        i = blocks - 1 - step
        qs = pl.ds(pl.multiple_of(i * BLOCK, BLOCK), BLOCK)
        start = start_ref[:, qs]
        key_iota = lax.broadcasted_iota(jnp.int32, (BLOCK, BLOCK), 0)
        query_pos = lax.broadcasted_iota(jnp.int32, (BLOCK, BLOCK), 1) + i * BLOCK
        dq[...] = jnp.zeros_like(dq)

        def tile(j, carry, masked):
            ks = pl.ds(pl.multiple_of(j * BLOCK, BLOCK), BLOCK)
            if masked:
                key_pos = key_iota + j * BLOCK
                allowed = (key_pos <= query_pos) & (key_pos >= start)
            hs = range(heads)
            rows = [slice(h * HEAD_DIM, (h + 1) * HEAD_DIM) for h in hs]
            q_h = [qt_ref[rows[h], qs] for h in hs]
            do_h = [dot_[rows[h], qs] for h in hs]
            scores = [mm(kn_ref[h, ks, :], q_h[h]) for h in hs]
            gp = [mm(vn_ref[h, ks, :], do_h[h]) for h in hs]
            for h in hs:
                s = scores[h]
                if masked:
                    s = jnp.where(allowed, s, -1e30)
                probs = jnp.exp(s - lse_ref[h : h + 1, qs])
                grad_scores = (probs * (gp[h] - delta[h : h + 1, qs])).astype(bf16)
                dv[rows[h], ks] += mm(do_h[h], probs.astype(bf16), NT)
                dk[rows[h], ks] += mm(q_h[h], grad_scores, NT)
                dq[rows[h], :] += mm(kt_ref[rows[h], ks], grad_scores)
            return carry

        lo, full = lo_ref[i], full_ref[i]
        tile(i, 0, True)
        lax.fori_loop(full, i, lambda j, s: tile(j, s, False), 0)
        lax.fori_loop(lo, full, lambda j, s: tile(j, s, True), 0)

        cosine, sine = cos_ref[:, qs], sin_ref[:, qs]
        pieces = []
        for source, factor in ((dq, HEAD_DIM ** (-0.5)), (dk, 1.0)):
            for h in range(heads):
                lo_row, mid, hi = h * HEAD_DIM, h * HEAD_DIM + HALF, (h + 1) * HEAD_DIM
                where = slice(None) if source is dq else qs
                a, b = source[lo_row:mid, where] * factor, source[mid:hi, where] * factor
                pieces += [a * cosine + b * sine, b * cosine - a * sine]
        half_v = 0.5 * dv[:, qs]
        gf_ref[qs, :] = half_v.T
        grads = jnp.concatenate(pieces + [half_v], axis=0)
        gt_ref[:, qs] = grads.astype(bf16)
        gn_ref[qs, :] = (mm(grads.T.astype(bf16), w_ref[...], NT) * gain_ref[...]).astype(bf16)
        return carry

    lax.fori_loop(0, blocks, query_block, 0)
    copies, outs = [], list(gn_out)
    for mask in range(n_t):
        row = jnp.bitwise_xor(t, mask) * count
        for size in piece_rows(mask, count, n_t):
            copies.append(
                pltpu.make_async_copy(
                    gn_ref.at[pl.ds(pl.multiple_of(row, size), size)],
                    outs.pop(0),
                    sems.at[len(copies)],
                )
            )
            row = row + size
    for copy in copies:
        copy.start()
    for copy in copies:
        copy.wait()


def feed_forward_kernel(
    masks, place_ref, xa_ref, xb_ref, ga_ref, gb_ref, wd_ref, *rest
):
    count = len(masks)
    pieces, (inner_ref, gvu_ref, u_ref, u_far_ref, w, sems) = rest[:count], rest[count:]
    t = place_ref[2]
    copies = []
    for piece, (mask, first) in zip(pieces, masks):
        at = w.at[pl.ds(first, piece.shape[0]), :, jnp.bitwise_xor(t, mask)]
        copies.append(pltpu.make_async_copy(piece, at, sems.at[len(copies)]))
        copies[-1].start()
    for copy in copies:
        copy.wait()
    features = xa_ref.shape[1]
    tokens = xa_ref.shape[0]
    ff = wd_ref.shape[0]
    step, high = 256, min(512, tokens)
    edges = list(range(0, ff, step)) + [ff]

    def weight(lo, hi):
        return w[:, :, :, :, lo:hi].reshape(features, hi - lo)

    for source, (x_ref, g_ref) in enumerate(((xa_ref, ga_ref), (xb_ref, gb_ref))):

        def rows_step(i, carry, x_ref=x_ref, g_ref=g_ref, source=source):
            rows = pl.ds(pl.multiple_of(i * high, high), high)
            outs = pl.ds(pl.multiple_of(source * tokens + i * high, high), high)
            x, g = x_ref[rows, :], g_ref[rows, :]
            for lo, hi in zip(edges[:-1], edges[1:]):
                gate = mm(x, weight(lo, hi))
                up = mm(x, weight(ff + lo, ff + hi))
                grad_inner = mm(g, wd_ref[lo:hi, :], NT)
                sig = jax.nn.sigmoid(gate)
                act = gate * sig
                inner_ref[outs, lo:hi] = (act * up).astype(bf16)
                gvu_ref[outs, lo:hi] = (
                    grad_inner * up * (sig * (1.0 + gate * (1.0 - sig)))
                ).astype(bf16)
                gvu_ref[outs, ff + lo : ff + hi] = (grad_inner * act).astype(bf16)
            u = mm(gvu_ref[outs, :], weight(0, 2 * ff), NT)
            if source == 0:
                u_ref[rows, :] = u
            else:
                u_far_ref[rows, :] = u.astype(bf16)
            return carry

        lax.fori_loop(0, tokens // high, rows_step, 0)


def gate_up_grad_kernel(n_t, place_ref, xa_ref, xb_ref, gvu_ref, *rest):
    out_ref, xt, grads, sems = rest
    tokens, features = xa_ref.shape
    n_z = grads.shape[0]
    own = grads.shape[3]
    step = 256
    for i in range(0, tokens, step):
        xt[:, i : i + step] = xa_ref[i : i + step, :].T
        xt[:, tokens + i : tokens + i + step] = xb_ref[i : i + step, :].T

    def columns(i, carry):
        at = pl.ds(pl.multiple_of(i * step, step), step)
        part = mm(xt[...], gvu_ref[:, at]).astype(bf16)
        grads[:, :, :, :, at] = part.reshape(n_z, 2, n_t, own, step)
        return carry

    lax.fori_loop(0, gvu_ref.shape[1] // step, columns, 0)
    copies = []
    for i in range(n_t):
        copy = pltpu.make_async_copy(grads.at[:, :, i], out_ref.at[i], sems.at[i])
        copy.start()
        copies.append(copy)
    for copy in copies:
        copy.wait()


def load_output_weight(place_ref, near, far, wo, sems):
    z, core = place_ref[0], place_ref[1]
    n_z = near.shape[0]
    copies = []
    for other, ref in enumerate((near, far)):
        for i in range(n_z):
            at = wo.at[2 * lax.rem(z - i + n_z, n_z) + jnp.bitwise_xor(core, other)]
            copies.append(pltpu.make_async_copy(ref.at[i], at, sems.at[len(copies)]))
            copies[-1].start()
    for copy in copies:
        copy.wait()


def project_out_kernel(n_t, place_ref, token_ref, near, far, *rest):
    *att, hidden_ref, unit_ref, wo, sems = rest
    load_output_weight(place_ref, near, far, wo, sems)
    t = place_ref[2]
    n_dp, _, height, cols = wo.shape
    step = 256

    def rows_step(i, carry):
        rows = pl.ds(pl.multiple_of(i * step, step), step)
        hidden = token_ref[rows, :].astype(f32)
        for mask, ref in enumerate(att):
            weight = wo[:, jnp.bitwise_xor(t, mask)].reshape(n_dp * height, cols)
            hidden = hidden + mm(ref[rows, :], weight, NT)
        hidden_ref[rows, :] = hidden
        mean = jnp.mean(hidden * hidden, axis=-1, keepdims=True)
        unit_ref[rows, :] = (hidden * lax.rsqrt(mean + eps)).astype(bf16)
        return carry

    lax.fori_loop(0, token_ref.shape[0] // step, rows_step, 0)


def norm_backward(values, scaled, inverse):
    dot = jnp.sum(scaled * values, axis=-1, keepdims=True) / values.shape[-1]
    return inverse * scaled - values * (inverse * inverse * inverse * dot)


def branch_grad_kernel(
    place_ref, hidden_ref, u_ref, u_got_ref, g_ref, near, far, grad_ref, branch_ref, *rest
):
    *outs, wo, sems = rest
    load_output_weight(place_ref, near, far, wo, sems)
    t = place_ref[2]
    n_dp, n_t, height, cols = wo.shape
    step = 256

    def rows_step(i, carry):
        rows = pl.ds(pl.multiple_of(i * step, step), step)
        hidden = hidden_ref[rows, :]
        scaled = u_ref[rows, :] + u_got_ref[rows, :].astype(f32)
        inverse = lax.rsqrt(jnp.mean(hidden * hidden, axis=-1, keepdims=True) + eps)
        grad = g_ref[rows, :].astype(f32) + norm_backward(hidden, scaled, inverse)
        grad_ref[rows, :] = grad
        branch = grad.astype(bf16)
        branch_ref[rows, :] = branch
        for mask, out in enumerate(outs):
            weight = wo[:, jnp.bitwise_xor(t, mask)].reshape(n_dp * height, cols)
            out[rows, :] = mm(branch, weight).astype(bf16)
        return carry

    lax.fori_loop(0, hidden_ref.shape[0] // step, rows_step, 0)


def output_grad_kernel(place_ref, branch_ref, *rest):
    *att, keep_ref, give_ref, turned, grads = rest
    core, t = place_ref[1], place_ref[2]
    n_z, n_t, height, cols = keep_ref.shape
    turned[...] = branch_ref[...].T
    for mask, ref in enumerate(att):
        part = mm(turned[...], ref[...]).astype(bf16).reshape(n_z, 2, height, cols)
        for which in range(2):
            grads[which, :, jnp.bitwise_xor(t, mask)] = part[:, which]
    keep_ref[...] = grads[core]
    give_ref[...] = grads[1 - core]


def projection_grad_kernel(place_ref, gt_ref, x_ref, keep_ref, give_ref, grads, sems):
    core = place_ref[1]
    _, n_z, height, _ = grads.shape

    def columns(i, carry):
        at = pl.ds(pl.multiple_of(i * 2 * height, 2 * height), 2 * height)
        part = mm(gt_ref[...], x_ref[:, at]).T.astype(bf16)
        grads[0, i] = part[:height]
        grads[1, i] = part[height:]
        return carry

    lax.fori_loop(0, n_z, columns, 0)
    copies = [
        pltpu.make_async_copy(grads.at[core], keep_ref, sems.at[0]),
        pltpu.make_async_copy(grads.at[1 - core], give_ref, sems.at[1]),
    ]
    for copy in copies:
        copy.start()
    for copy in copies:
        copy.wait()


def vmem(n):
    return [pl.BlockSpec(memory_space=pltpu.VMEM)] * n


def smem(n):
    return [pl.BlockSpec(memory_space=pltpu.SMEM)] * n


def hbm(n):
    return [pl.BlockSpec(memory_space=pl.ANY)] * n


sds = jax.ShapeDtypeStruct


def call(kernel, name, gflops, in_specs, out_specs, out_shape, scratch, args):
    return pl.pallas_call(
        kernel,
        out_shape=tuple(out_shape),
        in_specs=in_specs,
        out_specs=tuple(out_specs),
        scratch_shapes=scratch,
        compiler_params=pltpu.CompilerParams(vmem_limit_bytes=VMEM_LIMIT),
        cost_estimate=pl.CostEstimate(
            flops=int(gflops * 1e9), bytes_accessed=1000, transcendentals=0
        ),
        name=name,
    )(*args)


def attend_forward(
    heads, n_t, place, lo, full, x_pieces, near, far, fv, cosine, sine, start, gain
):
    rows, cols = fv.shape
    x_at = [(mask, offset) for mask, offset, _ in x_pieces]
    pieces = [piece for _, _, piece in x_pieces]
    features, width = pieces[0].shape[1], near.shape[2]
    return call(
        functools.partial(attend_forward_kernel, heads, n_t, x_at),
        "attend_forward",
        5,
        smem(3) + vmem(5) + hbm(len(pieces) + 2),
        vmem(6) + hbm(2 + n_t),
        [
            sds((cols, rows), bf16),
            sds((cols, rows), bf16),
            sds((heads, rows, HEAD_DIM), bf16),
            sds((heads, rows, HEAD_DIM), bf16),
            sds((cols, rows), bf16),
            sds((heads, rows), f32),
            sds((rows, features), bf16),
            sds((features, width), bf16),
        ]
        + [sds((rows // n_t, cols), bf16)] * n_t,
        [
            pltpu.VMEM((rows, features), bf16),
            pltpu.VMEM((features, width), bf16),
            pltpu.VMEM((width, features), bf16),
            pltpu.VMEM((cols, rows), bf16),
            pltpu.VMEM((rows, cols), bf16),
            pltpu.VMEM((cols, BLOCK), f32),
            pltpu.SemaphoreType.DMA((len(pieces) + 2 * near.shape[0] + 2,)),
        ],
        (place, lo, full, fv, cosine, sine, start, gain, *pieces, near, far),
    )


def attend_backward(
    heads, n_t, place, lo, full, saved, grads, cosine, sine, start, w, gain
):
    rows, cols = start.shape[1], heads * HEAD_DIM
    count = rows // n_t
    features = w.shape[0]
    sizes = {mask: piece_rows(mask, count, n_t) for mask in range(n_t)}
    flat = [size for mask in range(n_t) for size in sizes[mask]]
    outs = call(
        functools.partial(attend_backward_kernel, heads, n_t),
        "attend_backward",
        10,
        smem(3) + vmem(11) + hbm(n_t),
        vmem(2) + hbm(len(flat)),
        [sds((3 * cols, rows), bf16), sds((rows, cols), f32)]
        + [sds((size, features), bf16) for size in flat],
        [
            pltpu.VMEM((rows, cols), bf16),
            pltpu.VMEM((rows, features), bf16),
            pltpu.VMEM((cols, rows), bf16),
            pltpu.VMEM((heads, rows), f32),
            pltpu.VMEM((cols, BLOCK), f32),
            pltpu.VMEM((cols, rows), f32),
            pltpu.VMEM((cols, rows), f32),
            pltpu.SemaphoreType.DMA((len(flat),)),
        ],
        (place, lo, full, *saved, cosine, sine, start, w, gain, *grads),
    )
    pieces = list(outs[2:])
    return outs[0], outs[1], {m: [pieces.pop(0) for _ in sizes[m]] for m in range(n_t)}


def feed_forward(n_z, n_t, place, xa, xb, ga, gb, wd, gathered):
    tokens, features = xa.shape
    ff = wd.shape[0]
    pieces, masks = [], []
    for mask, parts in gathered.items():
        first = 0
        for part in parts:
            pieces.append(part)
            masks.append((mask, first))
            first += part.shape[0]
    return call(
        functools.partial(feed_forward_kernel, masks),
        "feed_forward",
        0,
        smem(1) + vmem(5) + hbm(len(pieces)),
        vmem(4),
        [
            sds((2 * tokens, ff), bf16),
            sds((2 * tokens, 2 * ff), bf16),
            sds((tokens, features), f32),
            sds((tokens, features), bf16),
        ],
        [
            pltpu.VMEM((n_z, 2, n_t, features // (2 * n_z * n_t), 2 * ff), bf16),
            pltpu.SemaphoreType.DMA((len(pieces),)),
        ],
        (place, xa, xb, ga, gb, wd, *pieces),
    )


def gate_up_grad(n_z, n_t, place, xa, xb, gvu):
    tokens, features = xa.shape
    own = features // (2 * n_z * n_t)
    return call(
        functools.partial(gate_up_grad_kernel, n_t),
        "gate_up_grad",
        0,
        smem(1) + vmem(3),
        hbm(1),
        [sds((n_t, n_z, 2, own, gvu.shape[1]), bf16)],
        [
            pltpu.VMEM((features, 2 * tokens), bf16),
            pltpu.VMEM((n_z, 2, n_t, own, gvu.shape[1]), bf16),
            pltpu.SemaphoreType.DMA((n_t,)),
        ],
        (place, xa, xb, gvu),
    )[0]


def output_weight_scratch(near):
    n_z, n_t, height, cols = near.shape
    return [
        pltpu.VMEM((2 * n_z, n_t, height, cols), bf16),
        pltpu.SemaphoreType.DMA((2 * n_z,)),
    ]


def project_out(place, tokens, att, near, far):
    return call(
        functools.partial(project_out_kernel, len(att)),
        "project_out",
        20,
        smem(1) + vmem(1) + hbm(2) + vmem(len(att)),
        vmem(2),
        [sds(tokens.shape, f32), sds(tokens.shape, bf16)],
        output_weight_scratch(near),
        (place, tokens, near, far, *att),
    )


def branch_grad(place, hidden, u, u_got, g, near, far):
    _, n_t, _, cols = near.shape
    outs = call(
        branch_grad_kernel,
        "branch_grad",
        0,
        smem(1) + vmem(4) + hbm(2),
        vmem(2 + n_t),
        [sds(hidden.shape, f32), sds(hidden.shape, bf16)]
        + [sds((hidden.shape[0], cols), bf16)] * n_t,
        output_weight_scratch(near),
        (place, hidden, u, u_got, g, near, far),
    )
    return outs[0], outs[1], list(outs[2:])


def output_grad(n_z, place, branch, att):
    n_t, cols = len(att), att[0].shape[1]
    shape = (n_z, n_t, branch.shape[1] // (2 * n_z), cols)
    return call(
        output_grad_kernel,
        "output_grad",
        0,
        smem(1) + vmem(1 + n_t),
        vmem(2),
        [sds(shape, bf16)] * 2,
        [pltpu.VMEM(branch.shape[::-1], bf16), pltpu.VMEM((2,) + shape, bf16)],
        (place, branch, *att),
    )


def projection_grad(n_z, place, gt, x):
    height = x.shape[1] // (2 * n_z)
    return call(
        projection_grad_kernel,
        "projection_grad",
        0,
        smem(1) + vmem(2),
        hbm(2),
        [sds((n_z, height, gt.shape[0]), bf16)] * 2,
        [
            pltpu.VMEM((2, n_z, height, gt.shape[0]), bf16),
            pltpu.SemaphoreType.DMA((2,)),
        ],
        (place, gt, x),
    )


def doc_layout(doc_lengths, total):
    doc_ends = jnp.cumsum(doc_lengths)
    index = jnp.arange(total, dtype=jnp.int32)
    passed = (index[:, None] >= doc_ends[None, :]).astype(jnp.int32)
    return jnp.sum(passed * doc_lengths[None, :], axis=1)


def split_cols(weight, n_z):
    rows = weight.shape[0]
    return weight.reshape(rows, n_z, 2, -1).transpose(2, 0, 1, 3).reshape(2, rows, -1)


def join_cols(parts, n_z):
    rows = parts.shape[1]
    return parts.reshape(2, rows, n_z, -1).transpose(1, 2, 0, 3).reshape(rows, -1)


def body(
    tokens, lengths, first_values, attn_gain, query_weight, key_weight, value_weight,
    output_weight, mlp_gain, gate_weight, up_weight, down_weight, out_cotangent,
):
    n_t = lax.axis_size("tensor")
    n_z = lax.axis_size("z")
    t = lax.axis_index("tensor")
    core = lax.axis_index("core")
    place = jnp.stack([lax.axis_index("z"), core, t]).astype(jnp.int32)
    masks = range(n_t)
    count, features = tokens.shape
    rows = count * n_t
    wrows, cols = query_weight.shape
    heads = cols // HEAD_DIM
    ff_core = gate_weight.shape[1] // 2

    def by_core(near, far, axis):
        return jnp.where(
            core == 0, jnp.stack([near, far], axis=axis), jnp.stack([far, near], axis=axis)
        )

    token_f = tokens.astype(f32)
    inverse_in = lax.rsqrt(jnp.mean(token_f * token_f, axis=-1, keepdims=True) + eps)
    unit_in = (token_f * inverse_in).astype(bf16)
    with jax.named_scope("normed_tokens"):
        x_near = gather_near(unit_in)

    own_joint = jnp.concatenate([query_weight, key_weight, value_weight], axis=1)
    own_gains = attn_gain.shape[0]
    gain_rows = jnp.pad(attn_gain[None], ((0, 15), (0, 3 * cols - own_gains)))
    with jax.named_scope("attention_weights_z"):
        near = spread(jnp.concatenate([own_joint, gain_rows]), "z")

    gain_mid = mlp_gain.astype(f32)[:, None]
    both = jnp.concatenate(
        [split_cols(gate_weight, n_z), split_cols(up_weight, n_z)], axis=2
    ).astype(f32)
    both = (both * gain_mid[None]).astype(bf16)
    mine = lax.dynamic_index_in_dim(both, core, 0, False)
    with jax.named_scope("gate_up_core"):
        theirs = swap_core(lax.dynamic_index_in_dim(both, 1 - core, 0, False))
    with jax.named_scope("core_tokens"):
        grad_far = swap_core(out_cotangent)
    pair = by_core(mine, theirs, 0)

    start = doc_layout(lengths[0], rows)
    position = (jnp.arange(rows, dtype=jnp.int32) - start).astype(f32)
    freqs = rope_base ** (-jnp.arange(HALF, dtype=f32) * 2.0 / HEAD_DIM)
    angles = freqs[:, None] * position[None, :]
    cosine, sine = jnp.cos(angles), jnp.sin(angles)
    block_starts = start.reshape(-1, BLOCK)
    lo = block_starts[:, 0] // BLOCK
    full = jnp.minimum(
        (block_starts[:, -1] + BLOCK - 1) // BLOCK,
        jnp.arange(rows // BLOCK, dtype=jnp.int32),
    )
    start = start[None]

    x_near, near, pair, grad_far, output_weight, down_weight = together(
        x_near, near, pair, grad_far, output_weight, down_weight
    )

    with jax.named_scope("gate_up_z"):
        column = spread(pair, "z")
    with jax.named_scope("normed_tokens"):
        x_far = gather_far(unit_in, x_near)
    with jax.named_scope("attention_weights_core"):
        far = swap_core(near)
    drows = down_weight.shape[0]
    brows = drows + output_weight.size // features
    column_gain = by_core(near[:, wrows, :own_gains], far[:, wrows, :own_gains], 1).reshape(1, -1)
    with jax.named_scope("output_down_tensor"):
        slab = [
            down_weight,
            output_weight.reshape(-1, features),
            jnp.pad(column_gain, ((0, 15), (0, features - column_gain.shape[1]))),
        ]
        slabs = spread_tensor(jnp.concatenate(slab, axis=0))

    x_far, far, slabs, column = together(x_far, far, slabs, column)

    slab = by_index(slabs)
    with jax.named_scope("down_z"):
        down = lax.all_gather(slab[:, :drows].reshape(-1, features), "z", tiled=True)
    with jax.named_scope("output_weight_z"):
        out_near = send_z(slab[:, drows:brows].reshape(n_t, wrows, cols))
    gain = slab[:, brows, : column_gain.shape[1]].reshape(n_t, 2 * n_z, own_gains)
    gain = gain.transpose(1, 0, 2).astype(f32)
    gain_rows = lax.dynamic_index_in_dim(gain, place[0] * 2 + core, 0, False).reshape(-1, 1)
    gain = gain.reshape(1, features)
    with jax.named_scope("gate_up_tensor"):
        gu_near = gather_near(column)
    x_pieces = []
    for mask, parts in x_far.items():
        offset = 0
        for part in parts:
            x_pieces.append((mask, offset, part))
            offset += part.shape[0]
    qt, kt, kn, vn, ot, lse, x_full, joint_weight, *attended = attend_forward(
        heads, n_t, place, lo, full, x_pieces, near, far, first_values, cosine, sine, start, gain
    )

    attended, gu_near = together(attended, gu_near)

    with jax.named_scope("attended"):
        att = swap_all(attended)
    att, out_near, passed = together(att, out_near, pass_on(gu_near))
    with jax.named_scope("output_weight_core"):
        out_far = swap_core(out_near)
    with jax.named_scope("gate_up_tensor"):
        gathered = gather_far(column, gu_near, passed)
    hidden, unit_mid = project_out(place, tokens, att, out_near, out_far)
    unit_mid, gathered = together(unit_mid, gathered)
    with jax.named_scope("core_tokens"):
        unit_far = swap_core(unit_mid)

    inner, gvu, u_own, u_give = feed_forward(
        n_z, n_t, place, unit_mid, unit_far, out_cotangent, grad_far, down, gathered
    )
    with jax.named_scope("u_core"):
        u_got = swap_core(u_give)
    grad_both = jnp.concatenate([out_cotangent, grad_far], axis=0)
    grad_dn = mm(inner, grad_both, TN).astype(bf16).reshape(n_z, -1, features)

    u_got, grad_dn = together(u_got, grad_dn)

    with jax.named_scope("grad_down_z"):
        dn = lax.psum_scatter(grad_dn.reshape(-1, features), "z", scatter_dimension=0, tiled=True)
    grad_hidden, branch, grad_att = branch_grad(
        place, hidden, u_own, u_got, out_cotangent, out_near, out_far
    )
    with jax.named_scope("grad_attended"):
        grad_att = swap_all(grad_att)
    gu_parts = gate_up_grad(n_z, n_t, place, unit_mid, unit_far, gvu)
    keep_ow, give_ow = output_grad(n_z, place, branch, att)
    with jax.named_scope("grad_output_core"):
        got_ow = swap_core(give_ow)

    grad_att, gu_parts, got_ow = together(grad_att, gu_parts, got_ow)

    with jax.named_scope("grad_gate_up_tensor"):
        gu_terms = exchange(gu_parts, "tensor")
    with jax.named_scope("grad_output_z"):
        ow_terms = scatter_z(sums_z([keep_ow, got_ow]))
    gt, grad_first, in_parts = attend_backward(
        heads, n_t, place, lo, full, (qt, kt, kn, vn, ot, lse), grad_att, cosine, sine, start,
        joint_weight, gain,
    )

    in_parts, gt, ow_terms = together(in_parts, gt, ow_terms)

    with jax.named_scope("grad_normed"):
        in_far = scatter_far(in_parts)
    keep_jw, give_jw = projection_grad(n_z, place, gt, x_full)
    with jax.named_scope("grad_projection_core"):
        got_jw = swap_core(give_jw)
    jw_sums, inner = together(sums_z([keep_jw, got_jw]), inner)
    with jax.named_scope("grad_projection_z"):
        jw_terms = scatter_z(jw_sums)
    out_part = mm(inner, down)
    out_give = out_part[count:].astype(bf16)

    jw_own, ow_terms = together(jw_sums[0], ow_terms)
    jw_terms[0] = jw_own
    ow = total(ow_terms).astype(bf16).reshape(n_t, -1, features)
    both = jnp.concatenate([dn.reshape(n_t, -1, features), ow], axis=1)
    both = [lax.dynamic_index_in_dim(both, t ^ m, 0, False) for m in masks]

    in_far, gu_terms, jw_terms, out_give, both = together(
        in_far, gu_terms, jw_terms, out_give, both
    )
    with jax.named_scope("grad_output_down_tensor"):
        both_terms = swap_all(both)

    gu_sum = total(gu_terms).astype(bf16)
    in_joined = scatter_join(in_parts, in_far)
    with jax.named_scope("grad_gate_up_z"):
        gu_terms = exchange(gu_sum, "z")
    in_joined, jw_terms, both_terms = together(in_joined, jw_terms, both_terms)
    with jax.named_scope("grad_normed"):
        in_terms = scatter_near(in_parts, in_joined)
    with jax.named_scope("layer_out"):
        out_got = swap_core(out_give)
    layer_out = (hidden + out_part[:count] + out_got.astype(f32)).astype(bf16)

    grad_jw = total(jw_terms)
    gain_part = jnp.sum(grad_jw * own_joint.astype(f32), axis=1).reshape(n_t, -1)
    with jax.named_scope("grad_gain"):
        gain_terms = swap_all([lax.dynamic_index_in_dim(gain_part, t ^ m, 0) for m in masks])
    grad_jw = grad_jw * gain_rows

    in_terms, gu_terms, both_terms, grad_jw, gain_terms, layer_out = together(
        in_terms, gu_terms, both_terms, grad_jw, gain_terms, layer_out
    )
    grad_attn_gain = total(gain_terms)
    grad_down = total(both_terms)
    grad_output = grad_down[drows:].reshape(wrows, cols)
    grad_down = grad_down[:drows]

    gu = total(gu_terms)
    gu_mine = lax.dynamic_index_in_dim(gu, core, 0, False)
    with jax.named_scope("grad_gate_up_core"):
        gu_other = swap_core(lax.dynamic_index_in_dim(gu, 1 - core, 0, False))

    grad_input = grad_hidden + norm_backward(token_f, total(in_terms), inverse_in)

    gu = by_core(gu_mine, gu_other, 0)
    grad_gate = join_cols(gu[:, :, :ff_core], n_z)
    grad_up = join_cols(gu[:, :, ff_core:], n_z)
    grad_mlp_gain = jnp.sum(
        grad_gate * gate_weight.astype(f32) + grad_up * up_weight.astype(f32), axis=1
    )
    grad_gate = grad_gate * gain_mid
    grad_up = grad_up * gain_mid

    return (
        layer_out,
        grad_input,
        grad_first,
        grad_attn_gain[0],
        grad_jw[:, :cols],
        grad_jw[:, cols : 2 * cols],
        grad_jw[:, 2 * cols :],
        grad_output,
        grad_mlp_gain,
        grad_gate,
        grad_up,
        grad_down,
    )


def solution(mesh):
    n_dp, n_t = mesh.shape["dp"], mesh.shape["tensor"]
    mesh = Mesh(mesh.devices.reshape(n_dp // 2, 2, n_t), ("z", "core", "tensor"))
    dp = ("z", "core")
    both = ("z", "core", "tensor")
    in_specs = (
        P(both, None),
        P(dp, None),
        P(dp, "tensor"),
        P(both),
        P(dp, "tensor"),
        P(dp, "tensor"),
        P(dp, "tensor"),
        P(dp, "tensor"),
        P(both),
        P(both, None),
        P(both, None),
        P(both, None),
        P(both, None),
    )
    out_specs = (
        P(both, None),
        P(both, None),
        P(dp, "tensor"),
        P(both),
        P(dp, "tensor"),
        P(dp, "tensor"),
        P(dp, "tensor"),
        P(dp, "tensor"),
        P(both),
        P(both, None),
        P(both, None),
        P(both, None),
    )
    return jax.shard_map(body, mesh=mesh, in_specs=in_specs, out_specs=out_specs, check_vma=False)
```

```python
import functools

import jax
import jax.numpy as jnp
from jax import lax
from jax.experimental import pallas as pl
from jax.experimental.pallas import tpu as pltpu
from jax.sharding import Mesh, PartitionSpec as P

HEAD_DIM = 64
HALF = HEAD_DIM // 2
BLOCK = 256
VMEM_LIMIT = 60 * 1024 * 1024

eps = 1e-06
rope_base = 10000.0
bf16 = jnp.bfloat16
f32 = jnp.float32

NN = (((1,), (0,)), ((), ()))
NT = (((1,), (1,)), ((), ()))
TN = (((0,), (0,)), ((), ()))


def mm(left, right, dims=NN):
    return lax.dot_general(left, right, dims, preferred_element_type=f32)


def swap_tensor(value, mask):
    size = lax.axis_size("tensor")
    return lax.ppermute(value, "tensor", [(i, i ^ mask) for i in range(size)])


def swap_core(value):
    return lax.ppermute(value, "core", [(0, 1), (1, 0)])


def shift_z(value, step):
    size = lax.axis_size("z")
    return lax.ppermute(value, "z", [(i, (i + step) % size) for i in range(size)])


def bit_orders():
    bits = [1 << b for b in range(lax.axis_size("tensor").bit_length() - 1)]
    return bits, bits[1:] + bits[:1]


def together(*values):
    return lax.optimization_barrier(values)


def halves(value):
    middle = value.shape[0] // 2
    return value[:middle], value[middle:]


def gather_near(value):
    if lax.axis_size("tensor") != 4:
        return []
    return [swap_tensor(value, 1), swap_tensor(value, 2)]


def pass_on(near):
    return [halves(near[0])[0], halves(near[1])[1]] if near else []


def gather_far(value, near, passed=()):
    if near:
        if not passed:
            passed = pass_on(near)
        far = [swap_tensor(passed[0], 2), swap_tensor(passed[1], 1)]
        return {0: [value], 1: [near[0]], 2: [near[1]], 3: far}
    parts = []
    for piece, bits in zip(halves(value), bit_orders()):
        have = {0: piece}
        for bit in bits:
            have.update({m ^ bit: swap_tensor(got, bit) for m, got in list(have.items())})
        parts.append(have)
    return {mask: [part[mask] for part in parts] for mask in parts[0]}


def add(left, right):
    return (left.astype(f32) + right.astype(f32)).astype(bf16)


def scatter_far(parts):
    if lax.axis_size("tensor") != 4:
        return []
    upper, lower = parts[3]
    return [swap_tensor(upper, 1), swap_tensor(lower, 2)]


def scatter_join(parts, far):
    if not far:
        return []
    to_x, to_y = parts[1][0], parts[2][0]
    middle = to_y.shape[0] // 2
    return [
        lax.dynamic_update_slice_in_dim(to_x, add(to_x[middle:], far[1]), middle, 0),
        lax.dynamic_update_slice_in_dim(to_y, add(to_y[:middle], far[0]), 0, 0),
    ]


def scatter_near(parts, joined):
    if joined:
        return [parts[0][0], swap_tensor(joined[0], 1), swap_tensor(joined[1], 2)]
    parts = {mask: jnp.concatenate(part, axis=0) for mask, part in parts.items()}
    sums = []
    for which, bits in enumerate(bit_orders()):
        left = {mask: halves(part)[which] for mask, part in parts.items()}
        for bit in bits:
            for mask in [m for m in left if not m & bit]:
                left[mask] = add(left[mask], swap_tensor(left.pop(mask | bit), bit))
        sums.append(left[0])
    return [jnp.concatenate(sums, axis=0)]


def spread_tensor(value):
    return swap_all([value] * lax.axis_size("tensor"))


def swap_all(pieces):
    return [swap_tensor(piece, mask) if mask else piece for mask, piece in enumerate(pieces)]


def by_index(pieces):
    here = lax.axis_index("tensor")
    order = []
    for place in range(len(pieces)):
        piece = pieces[0]
        for mask in range(1, len(pieces)):
            piece = jnp.where(here ^ place == mask, pieces[mask], piece)
        order.append(piece)
    return jnp.stack(order)


def send_z(value):
    return jnp.stack([value] + [shift_z(value, i) for i in range(1, lax.axis_size("z"))])


def sums_z(terms):
    depth = lax.axis_size("z")
    here = lax.axis_index("z")
    take = lambda term, i: lax.dynamic_index_in_dim(term, (here + i) % depth, 0, False)
    sums = [total([take(term, i) for term in terms]) for i in range(depth)]
    return [sums[0]] + [part.astype(bf16) for part in sums[1:]]


def scatter_z(sums):
    return [sums[0]] + [shift_z(part, i + 1) for i, part in enumerate(sums[1:])]


def exchange(value, axis):
    return lax.all_to_all(value, axis, 0, 0)


def spread(value, axis):
    return exchange(jnp.broadcast_to(value[None], (lax.axis_size(axis),) + value.shape), axis)


def piece_rows(mask, height, n_t):
    return [height // 2] * 2 if mask == 3 and n_t == 4 else [height]


def total(terms):
    terms = [terms[i].astype(f32) for i in range(len(terms))]
    return sum(terms[1:], terms[0])


def attend_forward_kernel(
    heads, n_t, x_at, place_ref, lo_ref, full_ref, fv_ref, cos_ref, sin_ref, start_ref, gain_ref, *rest
):
    x_in, w_in, rest = rest[: len(x_at)], rest[len(x_at) : len(x_at) + 2], rest[len(x_at) + 2 :]
    outs, (ot_ref, lse_ref, x_out, w_out) = rest[:4], rest[4:8]
    o_out, rest = rest[8 : 8 + n_t], rest[8 + n_t :]
    qt_ref, kt_ref, kn_ref, vn_ref, x_ref, w_ref, wt, vt, o_ref, acc, sems, out_sems = rest
    core, t = place_ref[1], place_ref[2]
    n_z = w_in[0].shape[0]
    height = w_ref.shape[0] // (2 * n_z)
    cols = heads * HEAD_DIM
    blocks = x_ref.shape[0] // BLOCK
    count = x_ref.shape[0] // n_t
    copies = []
    for other, ref in enumerate(w_in):
        for z in range(n_z):
            row = pl.multiple_of((2 * z + jnp.bitwise_xor(core, other)) * height, height)
            copies.append((ref.at[z, pl.ds(0, height)], w_ref.at[pl.ds(row, height)]))
    for ref, (mask, offset) in zip(x_in, x_at):
        row = jnp.bitwise_xor(t, mask) * count + offset
        size = ref.shape[0]
        copies.append((ref, x_ref.at[pl.ds(pl.multiple_of(row, size), size)]))
    copies = [pltpu.make_async_copy(a, b, sems.at[i]) for i, (a, b) in enumerate(copies)]
    for copy in copies:
        copy.start()
    for copy in copies[: 2 * n_z]:
        copy.wait()
    wt[...] = (w_ref[...].astype(f32).T * gain_ref[...]).astype(bf16)

    def project(i, carry):
        at = pl.ds(pl.multiple_of(i * BLOCK, BLOCK), BLOCK)
        joint = mm(wt[...], x_ref[at, :], NT)
        cosine, sine = cos_ref[:, at], sin_ref[:, at]
        first = fv_ref[at, :].astype(f32).T
        for h in range(heads):
            lo, mid, hi = h * HEAD_DIM, h * HEAD_DIM + HALF, (h + 1) * HEAD_DIM
            qa, qb = joint[lo:mid], joint[mid:hi]
            q = jnp.concatenate([qa * cosine - qb * sine, qb * cosine + qa * sine], axis=0)
            qt_ref[lo:hi, at] = (q * HEAD_DIM ** (-0.5)).astype(bf16)
            ka, kb = joint[cols + lo : cols + mid], joint[cols + mid : cols + hi]
            k = jnp.concatenate([ka * cosine - kb * sine, kb * cosine + ka * sine], axis=0)
            kt_ref[lo:hi, at] = k.astype(bf16)
            kn_ref[h, at, :] = k.T.astype(bf16)
            v = 0.5 * joint[2 * cols + lo : 2 * cols + hi] + 0.5 * first[lo:hi]
            vt[lo:hi, at] = v.astype(bf16)
            vn_ref[h, at, :] = v.T.astype(bf16)
        return carry

    for copy in copies[2 * n_z :]:
        copy.wait()
    lax.fori_loop(0, blocks, project, 0)
    pairs = [(x_ref, x_out), (w_ref, w_out)]
    pairs += list(zip((qt_ref, kt_ref, kn_ref, vn_ref), outs))
    keep = [pltpu.make_async_copy(a, b, out_sems.at[i]) for i, (a, b) in enumerate(pairs)]
    for copy in keep:
        copy.start()

    def query_block(i, carry):
        qs = pl.ds(pl.multiple_of(i * BLOCK, BLOCK), BLOCK)
        start = start_ref[:, qs]
        key_iota = lax.broadcasted_iota(jnp.int32, (BLOCK, BLOCK), 0)
        query_pos = lax.broadcasted_iota(jnp.int32, (BLOCK, BLOCK), 1) + i * BLOCK

        def tile(j, state, masked, opening):
            ks = pl.ds(pl.multiple_of(j * BLOCK, BLOCK), BLOCK)
            if masked:
                key_pos = key_iota + j * BLOCK
                allowed = (key_pos <= query_pos) & (key_pos >= start)
            result = []
            all_scores = [
                mm(kn_ref[h, ks, :], qt_ref[h * HEAD_DIM : (h + 1) * HEAD_DIM, qs])
                for h in range(heads)
            ]
            if masked:
                all_scores = [jnp.where(allowed, sc, -1e30) for sc in all_scores]
            peaks = [jnp.max(sc, axis=0, keepdims=True) for sc in all_scores]
            if not opening:
                shrinks = []
                for h in range(heads):
                    peaks[h] = jnp.maximum(state[h][0], peaks[h])
                    shrinks.append(jnp.exp(state[h][0] - peaks[h]))
            all_probs = [jnp.exp(sc - pk) for sc, pk in zip(all_scores, peaks)]
            for h in range(heads):
                rows = slice(h * HEAD_DIM, (h + 1) * HEAD_DIM)
                total = jnp.sum(all_probs[h], axis=0, keepdims=True)
                out = mm(vt[rows, ks], all_probs[h].astype(bf16))
                if not opening:
                    total = total + state[h][1] * shrinks[h]
                    out = out + acc[rows, :] * shrinks[h]
                acc[rows, :] = out
                result.append((peaks[h], total))
            return tuple(result)

        lo, full = lo_ref[i], full_ref[i]
        state = tile(i, None, True, True)
        state = lax.fori_loop(full, i, lambda j, s: tile(j, s, False, False), state)
        state = lax.fori_loop(lo, full, lambda j, s: tile(j, s, True, False), state)
        for h in range(heads):
            rows = slice(h * HEAD_DIM, (h + 1) * HEAD_DIM)
            peak, total = state[h]
            acc[rows, :] = acc[rows, :] * (1.0 / total)
            lse_ref[h : h + 1, qs] = peak + jnp.log(total)
        out = acc[...]
        ot_ref[:, qs] = out.astype(bf16)
        o_ref[qs, :] = out.T.astype(bf16)
        return carry

    lax.fori_loop(0, blocks, query_block, 0)
    for mask in range(n_t):
        row = pl.multiple_of(jnp.bitwise_xor(t, mask) * count, count)
        copy = pltpu.make_async_copy(o_ref.at[pl.ds(row, count)], o_out[mask], sems.at[mask])
        copy.start()
        keep.append(copy)
    for copy in keep:
        copy.wait()


def attend_backward_kernel(
    heads, n_t, place_ref, lo_ref, full_ref, qt_ref, kt_ref, kn_ref, vn_ref, ot_ref, lse_ref,
    cos_ref, sin_ref, start_ref, w_ref, gain_ref, *rest
):
    do_in, rest = rest[:n_t], rest[n_t:]
    gt_out, gf_out, *gn_out = rest[:-11]
    gt_ref, gf_ref, do_ref, gn_ref, dot_, delta, dq, dk, dv, sems, out_sems = rest[-11:]
    t = place_ref[2]
    cols = heads * HEAD_DIM
    blocks = do_ref.shape[0] // BLOCK
    count = do_ref.shape[0] // n_t
    copies = []
    for mask in range(n_t):
        row = pl.multiple_of(jnp.bitwise_xor(t, mask) * count, count)
        copies.append(
            pltpu.make_async_copy(do_in[mask], do_ref.at[pl.ds(row, count)], sems.at[mask])
        )
        copies[-1].start()
    for copy in copies:
        copy.wait()
    dk[...] = jnp.zeros_like(dk)
    dv[...] = jnp.zeros_like(dv)

    def prepare(i, carry):
        at = pl.ds(pl.multiple_of(i * BLOCK, BLOCK), BLOCK)
        grads = do_ref[at, :].astype(f32).T
        dot_[:, at] = grads.astype(bf16)
        prod = grads * ot_ref[:, at].astype(f32)
        for h in range(heads):
            delta[h : h + 1, at] = jnp.sum(
                prod[h * HEAD_DIM : (h + 1) * HEAD_DIM], axis=0, keepdims=True
            )
        return carry

    lax.fori_loop(0, blocks, prepare, 0)

    def give(i):
        at = pl.ds(pl.multiple_of(i * BLOCK, BLOCK), BLOCK)
        return [
            pltpu.make_async_copy(gt_ref.at[:, at], gt_out.at[:, at], out_sems.at[2 * i]),
            pltpu.make_async_copy(gf_ref.at[at], gf_out.at[at], out_sems.at[2 * i + 1]),
        ]

    def query_block(step, carry):
        i = blocks - 1 - step
        qs = pl.ds(pl.multiple_of(i * BLOCK, BLOCK), BLOCK)
        start = start_ref[:, qs]
        key_iota = lax.broadcasted_iota(jnp.int32, (BLOCK, BLOCK), 0)
        query_pos = lax.broadcasted_iota(jnp.int32, (BLOCK, BLOCK), 1) + i * BLOCK
        dq[...] = jnp.zeros_like(dq)

        def tile(j, carry, masked):
            ks = pl.ds(pl.multiple_of(j * BLOCK, BLOCK), BLOCK)
            if masked:
                key_pos = key_iota + j * BLOCK
                allowed = (key_pos <= query_pos) & (key_pos >= start)
            hs = range(heads)
            rows = [slice(h * HEAD_DIM, (h + 1) * HEAD_DIM) for h in hs]
            q_h = [qt_ref[rows[h], qs] for h in hs]
            do_h = [dot_[rows[h], qs] for h in hs]
            scores = [mm(kn_ref[h, ks, :], q_h[h]) for h in hs]
            gp = [mm(vn_ref[h, ks, :], do_h[h]) for h in hs]
            for h in hs:
                s = scores[h]
                if masked:
                    s = jnp.where(allowed, s, -1e30)
                probs = jnp.exp(s - lse_ref[h : h + 1, qs])
                grad_scores = (probs * (gp[h] - delta[h : h + 1, qs])).astype(bf16)
                dv[rows[h], ks] += mm(do_h[h], probs.astype(bf16), NT)
                dk[rows[h], ks] += mm(q_h[h], grad_scores, NT)
                dq[rows[h], :] += mm(kt_ref[rows[h], ks], grad_scores)
            return carry

        lo, full = lo_ref[i], full_ref[i]
        tile(i, 0, True)
        lax.fori_loop(full, i, lambda j, s: tile(j, s, False), 0)
        lax.fori_loop(lo, full, lambda j, s: tile(j, s, True), 0)

        cosine, sine = cos_ref[:, qs], sin_ref[:, qs]
        pieces = []
        for source, factor in ((dq, HEAD_DIM ** (-0.5)), (dk, 1.0)):
            for h in range(heads):
                lo_row, mid, hi = h * HEAD_DIM, h * HEAD_DIM + HALF, (h + 1) * HEAD_DIM
                where = slice(None) if source is dq else qs
                a, b = source[lo_row:mid, where] * factor, source[mid:hi, where] * factor
                pieces += [a * cosine + b * sine, b * cosine - a * sine]
        half_v = 0.5 * dv[:, qs]
        gf_ref[qs, :] = half_v.T
        grads = jnp.concatenate(pieces + [half_v], axis=0)
        gt_ref[:, qs] = grads.astype(bf16)
        for copy in give(i):
            copy.start()
        gn_ref[qs, :] = (mm(grads.T.astype(bf16), w_ref[...], NT) * gain_ref[...]).astype(bf16)
        return carry

    lax.fori_loop(0, blocks, query_block, 0)
    copies, outs = [], list(gn_out)
    for mask in range(n_t):
        row = jnp.bitwise_xor(t, mask) * count
        for size in piece_rows(mask, count, n_t):
            copies.append(
                pltpu.make_async_copy(
                    gn_ref.at[pl.ds(pl.multiple_of(row, size), size)],
                    outs.pop(0),
                    sems.at[len(copies)],
                )
            )
            row = row + size
    for copy in copies:
        copy.start()
    for i in range(blocks):
        copies += give(i)
    for copy in copies:
        copy.wait()


def feed_forward_kernel(masks, place_ref, *rest):
    count = len(masks)
    sources, pieces, rest = rest[:5], rest[5 : 5 + count], rest[5 + count :]
    inner_out, gvu_out, *u_outs = rest[:4]
    held, (w, inner_ref, gvu_ref, *u_refs, in_sems, out_sems) = rest[4:9], rest[9:]
    xa_ref, xb_ref, ga_ref, gb_ref, wd_ref = held
    t = place_ref[2]
    first = [pltpu.make_async_copy(sources[0], xa_ref, in_sems.at[0])]
    for i, (piece, (mask, row)) in enumerate(zip(pieces, masks)):
        at = w.at[pl.ds(row, piece.shape[0]), :, jnp.bitwise_xor(t, mask)]
        first.append(pltpu.make_async_copy(piece, at, in_sems.at[5 + i]))
    first.append(pltpu.make_async_copy(sources[2], ga_ref, in_sems.at[2]))
    first.append(pltpu.make_async_copy(sources[4], wd_ref, in_sems.at[4]))
    second = [
        pltpu.make_async_copy(sources[1], xb_ref, in_sems.at[1]),
        pltpu.make_async_copy(sources[3], gb_ref, in_sems.at[3]),
    ]
    for copy in first + second:
        copy.start()
    features = xa_ref.shape[1]
    tokens = xa_ref.shape[0]
    ff = wd_ref.shape[0]
    step, high = 256, min(512, tokens)
    edges = list(range(0, ff, step)) + [ff]
    results = []

    def give(ref, out):
        copy = pltpu.make_async_copy(ref, out, out_sems.at[len(results)])
        copy.start()
        results.append(copy)

    def weight(lo, hi):
        return w[:, :, :, :, lo:hi].reshape(features, hi - lo)

    for source, (x_ref, g_ref) in enumerate(((xa_ref, ga_ref), (xb_ref, gb_ref))):
        for copy in (first, second)[source]:
            copy.wait()
        for row in range(0, tokens, high):
            rows = pl.ds(row, high)
            outs = pl.ds(source * tokens + row, high)
            x, g = x_ref[rows, :], g_ref[rows, :]
            for lo, hi in zip(edges[:-1], edges[1:]):
                gate = mm(x, weight(lo, hi))
                up = mm(x, weight(ff + lo, ff + hi))
                grad_inner = mm(g, wd_ref[lo:hi, :], NT)
                sig = jax.nn.sigmoid(gate)
                act = gate * sig
                inner_ref[outs, lo:hi] = (act * up).astype(bf16)
                gvu_ref[outs, lo:hi] = (
                    grad_inner * up * (sig * (1.0 + gate * (1.0 - sig)))
                ).astype(bf16)
                gvu_ref[outs, ff + lo : ff + hi] = (grad_inner * act).astype(bf16)
            give(inner_ref.at[outs], inner_out.at[outs])
            give(gvu_ref.at[outs], gvu_out.at[outs])
            u = mm(gvu_ref[outs, :], weight(0, 2 * ff), NT)
            u_refs[source][rows, :] = u.astype(u_refs[source].dtype)
            give(u_refs[source].at[rows], u_outs[source].at[rows])
    for copy in results:
        copy.wait()


def gate_up_grad_kernel(n_t, place_ref, xa_ref, xb_ref, gvu_in, out_ref, xt, gvu, grads, sems, out_sems):
    tokens, features = xa_ref.shape
    n_z = grads.shape[0]
    own = grads.shape[3]
    step = gvu.shape[2]
    blocks = gvu.shape[0]

    def fetch(i):
        at = pl.ds(pl.multiple_of(i * step, step), step)
        return pltpu.make_async_copy(gvu_in.at[:, at], gvu.at[i], sems.at[i])

    def give(i):
        at = pl.ds(pl.multiple_of(i * step, step), step)
        return [
            pltpu.make_async_copy(
                grads.at[:, :, j, :, at], out_ref.at[j, :, :, :, at], out_sems.at[n_t * i + j]
            )
            for j in range(n_t)
        ]

    for i in range(blocks):
        fetch(i).start()
    for i in range(0, tokens, 256):
        xt[:, i : i + 256] = xa_ref[i : i + 256, :].T
        xt[:, tokens + i : tokens + i + 256] = xb_ref[i : i + 256, :].T

    def columns(i, carry):
        fetch(i).wait()
        part = mm(xt[...], gvu[i]).astype(bf16)
        at = pl.ds(pl.multiple_of(i * step, step), step)
        grads[:, :, :, :, at] = part.reshape(n_z, 2, n_t, own, step)
        for copy in give(i):
            copy.start()
        return carry

    lax.fori_loop(0, blocks, columns, 0)
    for i in range(blocks):
        for copy in give(i):
            copy.wait()


def load_output_weight(place_ref, near, far, wo, sems):
    z, core = place_ref[0], place_ref[1]
    n_z = near.shape[0]
    copies = []
    for other, ref in enumerate((near, far)):
        for i in range(n_z):
            at = wo.at[2 * lax.rem(z - i + n_z, n_z) + jnp.bitwise_xor(core, other)]
            copies.append(pltpu.make_async_copy(ref.at[i], at, sems.at[len(copies)]))
            copies[-1].start()
    for copy in copies:
        copy.wait()


def project_out_kernel(n_t, place_ref, token_ref, near, far, *rest):
    *att, hidden_ref, unit_ref, wo, sems = rest

    @pl.when(pl.program_id(0) == 0)
    def _():
        load_output_weight(place_ref, near, far, wo, sems)

    t = place_ref[2]
    n_dp, _, height, cols = wo.shape
    hidden = token_ref[...].astype(f32)
    for mask, ref in enumerate(att):
        weight = wo[:, jnp.bitwise_xor(t, mask)].reshape(n_dp * height, cols)
        hidden = hidden + mm(ref[...], weight, NT)
    hidden_ref[...] = hidden
    mean = jnp.mean(hidden * hidden, axis=-1, keepdims=True)
    unit_ref[...] = (hidden * lax.rsqrt(mean + eps)).astype(bf16)


def norm_backward(values, scaled, inverse):
    dot = jnp.sum(scaled * values, axis=-1, keepdims=True) / values.shape[-1]
    return inverse * scaled - values * (inverse * inverse * inverse * dot)


def branch_grad_kernel(
    place_ref, hidden_ref, u_ref, u_got_ref, g_ref, near, far, grad_ref, branch_ref, *rest
):
    *outs, wo, sems = rest

    @pl.when(pl.program_id(0) == 0)
    def _():
        load_output_weight(place_ref, near, far, wo, sems)

    t = place_ref[2]
    n_dp, _, height, cols = wo.shape
    hidden = hidden_ref[...]
    scaled = u_ref[...] + u_got_ref[...].astype(f32)
    inverse = lax.rsqrt(jnp.mean(hidden * hidden, axis=-1, keepdims=True) + eps)
    grad = g_ref[...].astype(f32) + norm_backward(hidden, scaled, inverse)
    grad_ref[...] = grad
    branch = grad.astype(bf16)
    branch_ref[...] = branch
    for mask, out in enumerate(outs):
        weight = wo[:, jnp.bitwise_xor(t, mask)].reshape(n_dp * height, cols)
        out[...] = mm(branch, weight).astype(bf16)


def output_grad_kernel(place_ref, branch_ref, *rest):
    *att, keep_ref, give_ref, turned, grads = rest
    core, t = place_ref[1], place_ref[2]
    n_z, n_t, height, cols = keep_ref.shape
    turned[...] = branch_ref[...].T
    for mask, ref in enumerate(att):
        part = mm(turned[...], ref[...]).astype(bf16).reshape(n_z, 2, height, cols)
        for which in range(2):
            grads[which, :, jnp.bitwise_xor(t, mask)] = part[:, which]
    keep_ref[...] = grads[core]
    give_ref[...] = grads[1 - core]


def projection_grad_kernel(
    place_ref, gt_in, x_in, keep_ref, give_ref, gt_ref, x_ref, grads, sems, out_sems
):
    core = place_ref[1]
    _, n_z, height, _ = grads.shape
    wide = 2 * height

    def fetch(i):
        at = pl.ds(pl.multiple_of(i * wide, wide), wide)
        return pltpu.make_async_copy(x_in.at[:, at], x_ref.at[i], sems.at[1 + i])

    load = pltpu.make_async_copy(gt_in, gt_ref, sems.at[0])
    load.start()
    for i in range(n_z):
        fetch(i).start()
    load.wait()

    def give(i):
        return [
            pltpu.make_async_copy(grads.at[core, i], keep_ref.at[i], out_sems.at[2 * i]),
            pltpu.make_async_copy(grads.at[1 - core, i], give_ref.at[i], out_sems.at[2 * i + 1]),
        ]

    def columns(i, carry):
        fetch(i).wait()
        part = mm(gt_ref[...], x_ref[i]).T.astype(bf16)
        grads[0, i] = part[:height]
        grads[1, i] = part[height:]
        for copy in give(i):
            copy.start()
        return carry

    lax.fori_loop(0, n_z, columns, 0)
    for i in range(n_z):
        for copy in give(i):
            copy.wait()


def vmem(n):
    return [pl.BlockSpec(memory_space=pltpu.VMEM)] * n


def smem(n):
    return [pl.BlockSpec(memory_space=pltpu.SMEM)] * n


def hbm(n):
    return [pl.BlockSpec(memory_space=pl.ANY)] * n


sds = jax.ShapeDtypeStruct


def row_blocks(arrays):
    return [pl.BlockSpec((BLOCK, a.shape[1]), lambda i: (i, 0)) for a in arrays]


def call(kernel, name, gflops, in_specs, out_specs, out_shape, scratch, args, grid=()):
    return pl.pallas_call(
        kernel,
        grid=grid,
        out_shape=tuple(out_shape),
        in_specs=in_specs,
        out_specs=tuple(out_specs),
        scratch_shapes=scratch,
        compiler_params=pltpu.CompilerParams(vmem_limit_bytes=VMEM_LIMIT),
        cost_estimate=pl.CostEstimate(
            flops=int(gflops * 1e9), bytes_accessed=1000, transcendentals=0
        ),
        name=name,
    )(*args)


def attend_forward(
    heads, n_t, place, lo, full, x_pieces, near, far, fv, cosine, sine, start, gain
):
    rows, cols = fv.shape
    x_at = [(mask, offset) for mask, offset, _ in x_pieces]
    pieces = [piece for _, _, piece in x_pieces]
    features, width = pieces[0].shape[1], near.shape[2]
    return call(
        functools.partial(attend_forward_kernel, heads, n_t, x_at),
        "attend_forward",
        5,
        smem(3) + vmem(5) + hbm(len(pieces) + 2),
        hbm(4) + vmem(2) + hbm(2 + n_t),
        [
            sds((cols, rows), bf16),
            sds((cols, rows), bf16),
            sds((heads, rows, HEAD_DIM), bf16),
            sds((heads, rows, HEAD_DIM), bf16),
            sds((cols, rows), bf16),
            sds((heads, rows), f32),
            sds((rows, features), bf16),
            sds((features, width), bf16),
        ]
        + [sds((rows // n_t, cols), bf16)] * n_t,
        [
            pltpu.VMEM((cols, rows), bf16),
            pltpu.VMEM((cols, rows), bf16),
            pltpu.VMEM((heads, rows, HEAD_DIM), bf16),
            pltpu.VMEM((heads, rows, HEAD_DIM), bf16),
            pltpu.VMEM((rows, features), bf16),
            pltpu.VMEM((features, width), bf16),
            pltpu.VMEM((width, features), bf16),
            pltpu.VMEM((cols, rows), bf16),
            pltpu.VMEM((rows, cols), bf16),
            pltpu.VMEM((cols, BLOCK), f32),
            pltpu.SemaphoreType.DMA((len(pieces) + 2 * near.shape[0],)),
            pltpu.SemaphoreType.DMA((6,)),
        ],
        (place, lo, full, fv, cosine, sine, start, gain, *pieces, near, far),
    )


def attend_backward(
    heads, n_t, place, lo, full, saved, grads, cosine, sine, start, w, gain
):
    rows, cols = start.shape[1], heads * HEAD_DIM
    count = rows // n_t
    features = w.shape[0]
    sizes = {mask: piece_rows(mask, count, n_t) for mask in range(n_t)}
    flat = [size for mask in range(n_t) for size in sizes[mask]]
    outs = call(
        functools.partial(attend_backward_kernel, heads, n_t),
        "attend_backward",
        10,
        smem(3) + vmem(11) + hbm(n_t),
        hbm(2 + len(flat)),
        [sds((3 * cols, rows), bf16), sds((rows, cols), f32)]
        + [sds((size, features), bf16) for size in flat],
        [
            pltpu.VMEM((3 * cols, rows), bf16),
            pltpu.VMEM((rows, cols), f32),
            pltpu.VMEM((rows, cols), bf16),
            pltpu.VMEM((rows, features), bf16),
            pltpu.VMEM((cols, rows), bf16),
            pltpu.VMEM((heads, rows), f32),
            pltpu.VMEM((cols, BLOCK), f32),
            pltpu.VMEM((cols, rows), f32),
            pltpu.VMEM((cols, rows), f32),
            pltpu.SemaphoreType.DMA((len(flat),)),
            pltpu.SemaphoreType.DMA((2 * (rows // BLOCK),)),
        ],
        (place, lo, full, *saved, cosine, sine, start, w, gain, *grads),
    )
    pieces = list(outs[2:])
    return outs[0], outs[1], {m: [pieces.pop(0) for _ in sizes[m]] for m in range(n_t)}


def feed_forward(n_z, n_t, place, xa, xb, ga, gb, wd, gathered):
    tokens, features = xa.shape
    ff = wd.shape[0]
    pieces, masks = [], []
    for mask, parts in gathered.items():
        first = 0
        for part in parts:
            pieces.append(part)
            masks.append((mask, first))
            first += part.shape[0]
    return call(
        functools.partial(feed_forward_kernel, masks),
        "feed_forward",
        0,
        smem(1) + hbm(5 + len(pieces)),
        hbm(4),
        [
            sds((2 * tokens, ff), bf16),
            sds((2 * tokens, 2 * ff), bf16),
            sds((tokens, features), f32),
            sds((tokens, features), bf16),
        ],
        [
            *[pltpu.VMEM((tokens, features), bf16)] * 4,
            pltpu.VMEM((ff, features), bf16),
            pltpu.VMEM((n_z, 2, n_t, features // (2 * n_z * n_t), 2 * ff), bf16),
            pltpu.VMEM((2 * tokens, ff), bf16),
            pltpu.VMEM((2 * tokens, 2 * ff), bf16),
            pltpu.VMEM((tokens, features), f32),
            pltpu.VMEM((tokens, features), bf16),
            pltpu.SemaphoreType.DMA((5 + len(pieces),)),
            pltpu.SemaphoreType.DMA((6 * max(1, tokens // 512),)),
        ],
        (place, xa, xb, ga, gb, wd, *pieces),
    )


def gate_up_grad(n_z, n_t, place, xa, xb, gvu):
    tokens, features = xa.shape
    own = features // (2 * n_z * n_t)
    return call(
        functools.partial(gate_up_grad_kernel, n_t),
        "gate_up_grad",
        0,
        smem(1) + vmem(2) + hbm(1),
        hbm(1),
        [sds((n_t, n_z, 2, own, gvu.shape[1]), bf16)],
        [
            pltpu.VMEM((features, 2 * tokens), bf16),
            pltpu.VMEM((gvu.shape[1] // 256, 2 * tokens, 256), bf16),
            pltpu.VMEM((n_z, 2, n_t, own, gvu.shape[1]), bf16),
            pltpu.SemaphoreType.DMA((gvu.shape[1] // 256,)),
            pltpu.SemaphoreType.DMA((n_t * (gvu.shape[1] // 256),)),
        ],
        (place, xa, xb, gvu),
    )[0]


def output_weight_scratch(near):
    n_z, n_t, height, cols = near.shape
    return [
        pltpu.VMEM((2 * n_z, n_t, height, cols), bf16),
        pltpu.SemaphoreType.DMA((2 * n_z,)),
    ]


def project_out(place, tokens, att, near, far):
    shapes = [sds(tokens.shape, f32), sds(tokens.shape, bf16)]
    return call(
        functools.partial(project_out_kernel, len(att)),
        "project_out",
        20,
        smem(1) + row_blocks([tokens]) + hbm(2) + row_blocks(att),
        row_blocks(shapes),
        shapes,
        output_weight_scratch(near),
        (place, tokens, near, far, *att),
        (tokens.shape[0] // BLOCK,),
    )


def branch_grad(place, hidden, u, u_got, g, near, far):
    _, n_t, _, cols = near.shape
    shapes = [sds(hidden.shape, f32), sds(hidden.shape, bf16)]
    shapes += [sds((hidden.shape[0], cols), bf16)] * n_t
    outs = call(
        branch_grad_kernel,
        "branch_grad",
        0,
        smem(1) + row_blocks([hidden, u, u_got, g]) + hbm(2),
        row_blocks(shapes),
        shapes,
        output_weight_scratch(near),
        (place, hidden, u, u_got, g, near, far),
        (hidden.shape[0] // BLOCK,),
    )
    return outs[0], outs[1], list(outs[2:])


def output_grad(n_z, place, branch, att):
    n_t, cols = len(att), att[0].shape[1]
    shape = (n_z, n_t, branch.shape[1] // (2 * n_z), cols)
    return call(
        output_grad_kernel,
        "output_grad",
        0,
        smem(1) + vmem(1 + n_t),
        vmem(2),
        [sds(shape, bf16)] * 2,
        [pltpu.VMEM(branch.shape[::-1], bf16), pltpu.VMEM((2,) + shape, bf16)],
        (place, branch, *att),
    )


def projection_grad(n_z, place, gt, x):
    height = x.shape[1] // (2 * n_z)
    return call(
        projection_grad_kernel,
        "projection_grad",
        0,
        smem(1) + hbm(2),
        hbm(2),
        [sds((n_z, height, gt.shape[0]), bf16)] * 2,
        [
            pltpu.VMEM(gt.shape, bf16),
            pltpu.VMEM((n_z, x.shape[0], 2 * height), bf16),
            pltpu.VMEM((2, n_z, height, gt.shape[0]), bf16),
            pltpu.SemaphoreType.DMA((1 + n_z,)),
            pltpu.SemaphoreType.DMA((2 * n_z,)),
        ],
        (place, gt, x),
    )


def doc_layout(doc_lengths, total):
    doc_ends = jnp.cumsum(doc_lengths)
    index = jnp.arange(total, dtype=jnp.int32)
    passed = (index[:, None] >= doc_ends[None, :]).astype(jnp.int32)
    return jnp.sum(passed * doc_lengths[None, :], axis=1)


def split_cols(weight, n_z):
    rows = weight.shape[0]
    return weight.reshape(rows, n_z, 2, -1).transpose(2, 0, 1, 3).reshape(2, rows, -1)


def join_cols(parts, n_z):
    rows = parts.shape[1]
    return parts.reshape(2, rows, n_z, -1).transpose(1, 2, 0, 3).reshape(rows, -1)


def body(
    tokens, lengths, first_values, attn_gain, query_weight, key_weight, value_weight,
    output_weight, mlp_gain, gate_weight, up_weight, down_weight, out_cotangent,
):
    n_t = lax.axis_size("tensor")
    n_z = lax.axis_size("z")
    t = lax.axis_index("tensor")
    core = lax.axis_index("core")
    place = jnp.stack([lax.axis_index("z"), core, t]).astype(jnp.int32)
    masks = range(n_t)
    count, features = tokens.shape
    rows = count * n_t
    wrows, cols = query_weight.shape
    heads = cols // HEAD_DIM
    ff_core = gate_weight.shape[1] // 2

    def by_core(near, far, axis):
        return jnp.where(
            core == 0, jnp.stack([near, far], axis=axis), jnp.stack([far, near], axis=axis)
        )

    token_f = tokens.astype(f32)
    inverse_in = lax.rsqrt(jnp.mean(token_f * token_f, axis=-1, keepdims=True) + eps)
    unit_in = (token_f * inverse_in).astype(bf16)
    with jax.named_scope("normed_tokens"):
        x_near = gather_near(unit_in)

    own_joint = jnp.concatenate([query_weight, key_weight, value_weight], axis=1)
    own_gains = attn_gain.shape[0]
    gain_rows = jnp.pad(attn_gain[None], ((0, 15), (0, 3 * cols - own_gains)))
    with jax.named_scope("attention_weights_z"):
        near = spread(jnp.concatenate([own_joint, gain_rows]), "z")

    gain_mid = mlp_gain.astype(f32)[:, None]
    both = jnp.concatenate(
        [split_cols(gate_weight, n_z), split_cols(up_weight, n_z)], axis=2
    ).astype(f32)
    both = (both * gain_mid[None]).astype(bf16)
    mine = lax.dynamic_index_in_dim(both, core, 0, False)
    with jax.named_scope("gate_up_core"):
        theirs = swap_core(lax.dynamic_index_in_dim(both, 1 - core, 0, False))
    with jax.named_scope("core_tokens"):
        grad_far = swap_core(out_cotangent)
    pair = by_core(mine, theirs, 0)

    start = doc_layout(lengths[0], rows)
    position = (jnp.arange(rows, dtype=jnp.int32) - start).astype(f32)
    freqs = rope_base ** (-jnp.arange(HALF, dtype=f32) * 2.0 / HEAD_DIM)
    angles = freqs[:, None] * position[None, :]
    cosine, sine = jnp.cos(angles), jnp.sin(angles)
    block_starts = start.reshape(-1, BLOCK)
    lo = block_starts[:, 0] // BLOCK
    full = jnp.minimum(
        (block_starts[:, -1] + BLOCK - 1) // BLOCK,
        jnp.arange(rows // BLOCK, dtype=jnp.int32),
    )
    start = start[None]

    x_near, near, pair, grad_far, output_weight, down_weight = together(
        x_near, near, pair, grad_far, output_weight, down_weight
    )

    with jax.named_scope("gate_up_z"):
        column = spread(pair, "z")
    with jax.named_scope("normed_tokens"):
        x_far = gather_far(unit_in, x_near)
    with jax.named_scope("attention_weights_core"):
        far = swap_core(near)
    drows = down_weight.shape[0]
    brows = drows + output_weight.size // features
    column_gain = by_core(near[:, wrows, :own_gains], far[:, wrows, :own_gains], 1).reshape(1, -1)
    with jax.named_scope("output_down_tensor"):
        slab = [
            down_weight,
            output_weight.reshape(-1, features),
            jnp.pad(column_gain, ((0, 15), (0, features - column_gain.shape[1]))),
        ]
        slabs = spread_tensor(jnp.concatenate(slab, axis=0))

    x_far, far, slab, column, cosine, sine, start, lo, full = together(
        x_far, far, by_index(slabs), column, cosine, sine, start, lo, full
    )

    with jax.named_scope("down_z"):
        down = lax.all_gather(slab[:, :drows].reshape(-1, features), "z", tiled=True)
    with jax.named_scope("output_weight_z"):
        out_near = send_z(slab[:, drows:brows].reshape(n_t, wrows, cols))
    gain = slab[:, brows, : column_gain.shape[1]].reshape(n_t, 2 * n_z, own_gains)
    gain = gain.transpose(1, 0, 2).astype(f32)
    gain_rows = lax.dynamic_index_in_dim(gain, place[0] * 2 + core, 0, False).reshape(-1, 1)
    gain = gain.reshape(1, features)
    with jax.named_scope("gate_up_tensor"):
        gu_near = gather_near(column)
    x_pieces = []
    for mask, parts in x_far.items():
        offset = 0
        for part in parts:
            x_pieces.append((mask, offset, part))
            offset += part.shape[0]
    qt, kt, kn, vn, ot, lse, x_full, joint_weight, *attended = attend_forward(
        heads, n_t, place, lo, full, x_pieces, near, far, first_values, cosine, sine, start, gain
    )

    attended, gu_near = together(attended, gu_near)

    with jax.named_scope("attended"):
        att = swap_all(attended)
    att, out_near, passed = together(att, out_near, pass_on(gu_near))
    with jax.named_scope("output_weight_core"):
        out_far = swap_core(out_near)
    with jax.named_scope("gate_up_tensor"):
        gathered = gather_far(column, gu_near, passed)
    hidden, unit_mid = project_out(place, tokens, att, out_near, out_far)
    unit_mid, gathered = together(unit_mid, gathered)
    with jax.named_scope("core_tokens"):
        unit_far = swap_core(unit_mid)

    inner, gvu, u_own, u_give = feed_forward(
        n_z, n_t, place, unit_mid, unit_far, out_cotangent, grad_far, down, gathered
    )
    with jax.named_scope("u_core"):
        u_got = swap_core(u_give)
    grad_both = jnp.concatenate([out_cotangent, grad_far], axis=0)
    grad_dn = mm(inner, grad_both, TN).astype(bf16).reshape(n_z, -1, features)

    u_got, grad_dn = together(u_got, grad_dn)

    with jax.named_scope("grad_down_z"):
        dn = lax.psum_scatter(grad_dn.reshape(-1, features), "z", scatter_dimension=0, tiled=True)
    grad_hidden, branch, grad_att = branch_grad(
        place, hidden, u_own, u_got, out_cotangent, out_near, out_far
    )
    with jax.named_scope("grad_attended"):
        grad_att = swap_all(grad_att)
    gu_parts = gate_up_grad(n_z, n_t, place, unit_mid, unit_far, gvu)
    keep_ow, give_ow = output_grad(n_z, place, branch, att)
    with jax.named_scope("grad_output_core"):
        got_ow = swap_core(give_ow)

    grad_att, gu_parts, got_ow = together(grad_att, gu_parts, got_ow)

    with jax.named_scope("grad_gate_up_tensor"):
        gu_terms = exchange(gu_parts, "tensor")
    with jax.named_scope("grad_output_z"):
        ow_terms = scatter_z(sums_z([keep_ow, got_ow]))
    gt, grad_first, in_parts = attend_backward(
        heads, n_t, place, lo, full, (qt, kt, kn, vn, ot, lse), grad_att, cosine, sine, start,
        joint_weight, gain,
    )

    in_parts, gt, ow_terms, dn = together(in_parts, gt, ow_terms, dn)

    with jax.named_scope("grad_normed"):
        in_far = scatter_far(in_parts)
    keep_jw, give_jw = projection_grad(n_z, place, gt, x_full)
    with jax.named_scope("grad_projection_core"):
        got_jw = swap_core(give_jw)
    jw_sums, inner = together(sums_z([keep_jw, got_jw]), inner)
    with jax.named_scope("grad_projection_z"):
        jw_terms = scatter_z(jw_sums)
    out_part = mm(inner, down)
    out_give = out_part[count:].astype(bf16)

    jw_own, ow_terms = together(jw_sums[0], ow_terms)
    jw_terms[0] = jw_own
    ow = total(ow_terms).astype(bf16).reshape(n_t, -1, features)
    both = jnp.concatenate([dn.reshape(n_t, -1, features), ow], axis=1)
    both = [lax.dynamic_index_in_dim(both, t ^ m, 0, False) for m in masks]

    in_far, gu_terms, jw_terms, out_give, both = together(
        in_far, gu_terms, jw_terms, out_give, both
    )
    with jax.named_scope("grad_output_down_tensor"):
        both_terms = swap_all(both)

    gu_sum = total(gu_terms).astype(bf16)
    in_joined = scatter_join(in_parts, in_far)
    with jax.named_scope("grad_gate_up_z"):
        gu_terms = exchange(gu_sum, "z")
    in_joined, jw_terms, both_terms = together(in_joined, jw_terms, both_terms)
    with jax.named_scope("grad_normed"):
        in_terms = scatter_near(in_parts, in_joined)
    with jax.named_scope("layer_out"):
        out_got = swap_core(out_give)
    layer_out = (hidden + out_part[:count] + out_got.astype(f32)).astype(bf16)

    grad_jw = total(jw_terms)
    gain_part = jnp.sum(grad_jw * own_joint.astype(f32), axis=1).reshape(n_t, -1)
    with jax.named_scope("grad_gain"):
        gain_terms = swap_all([lax.dynamic_index_in_dim(gain_part, t ^ m, 0) for m in masks])
    grad_jw = grad_jw * gain_rows

    in_terms, gu_terms, both_terms, grad_jw, gain_terms, layer_out = together(
        in_terms, gu_terms, both_terms, grad_jw, gain_terms, layer_out
    )
    grad_attn_gain = total(gain_terms)
    grad_down = total(both_terms)
    grad_output = grad_down[drows:].reshape(wrows, cols)
    grad_down = grad_down[:drows]

    gu = total(gu_terms)
    gu_mine = lax.dynamic_index_in_dim(gu, core, 0, False)
    with jax.named_scope("grad_gate_up_core"):
        gu_other = swap_core(lax.dynamic_index_in_dim(gu, 1 - core, 0, False))

    grad_input = grad_hidden + norm_backward(token_f, total(in_terms), inverse_in)

    gu = by_core(gu_mine, gu_other, 0)
    grad_gate = join_cols(gu[:, :, :ff_core], n_z)
    grad_up = join_cols(gu[:, :, ff_core:], n_z)
    grad_mlp_gain = jnp.sum(
        grad_gate * gate_weight.astype(f32) + grad_up * up_weight.astype(f32), axis=1
    )
    grad_gate = grad_gate * gain_mid
    grad_up = grad_up * gain_mid

    return (
        layer_out,
        grad_input,
        grad_first,
        grad_attn_gain[0],
        grad_jw[:, :cols],
        grad_jw[:, cols : 2 * cols],
        grad_jw[:, 2 * cols :],
        grad_output,
        grad_mlp_gain,
        grad_gate,
        grad_up,
        grad_down,
    )


def solution(mesh):
    n_dp, n_t = mesh.shape["dp"], mesh.shape["tensor"]
    mesh = Mesh(mesh.devices.reshape(n_dp // 2, 2, n_t), ("z", "core", "tensor"))
    dp = ("z", "core")
    both = ("z", "core", "tensor")
    in_specs = (
        P(both, None),
        P(dp, None),
        P(dp, "tensor"),
        P(both),
        P(dp, "tensor"),
        P(dp, "tensor"),
        P(dp, "tensor"),
        P(dp, "tensor"),
        P(both),
        P(both, None),
        P(both, None),
        P(both, None),
        P(both, None),
    )
    out_specs = (
        P(both, None),
        P(both, None),
        P(dp, "tensor"),
        P(both),
        P(dp, "tensor"),
        P(dp, "tensor"),
        P(dp, "tensor"),
        P(dp, "tensor"),
        P(both),
        P(both, None),
        P(both, None),
        P(both, None),
    )
    return jax.shard_map(body, mesh=mesh, in_specs=in_specs, out_specs=out_specs, check_vma=False)
```

```python
import functools

import jax
import jax.numpy as jnp
from jax import lax
from jax.experimental import pallas as pl
from jax.experimental.pallas import tpu as pltpu
from jax.sharding import Mesh, PartitionSpec as P

HEAD_DIM = 64
HALF = HEAD_DIM // 2
BLOCK = 256
VMEM_LIMIT = 60 * 1024 * 1024

eps = 1e-06
rope_base = 10000.0
bf16 = jnp.bfloat16
f32 = jnp.float32

NN = (((1,), (0,)), ((), ()))
NT = (((1,), (1,)), ((), ()))
TN = (((0,), (0,)), ((), ()))


def mm(left, right, dims=NN):
    return lax.dot_general(left, right, dims, preferred_element_type=f32)


def swap_tensor(value, mask):
    size = lax.axis_size("tensor")
    return lax.ppermute(value, "tensor", [(i, i ^ mask) for i in range(size)])


def swap_core(value):
    return lax.ppermute(value, "core", [(0, 1), (1, 0)])


def shift_z(value, step):
    size = lax.axis_size("z")
    return lax.ppermute(value, "z", [(i, (i + step) % size) for i in range(size)])


def bit_orders():
    bits = [1 << b for b in range(lax.axis_size("tensor").bit_length() - 1)]
    return bits, bits[1:] + bits[:1]


def together(*values):
    return lax.optimization_barrier(values)


def halves(value):
    middle = value.shape[0] // 2
    return value[:middle], value[middle:]


def gather_near(value):
    if lax.axis_size("tensor") != 4:
        return []
    return [swap_tensor(value, 1), swap_tensor(value, 2)]


def pass_on(near):
    return [halves(near[0])[0], halves(near[1])[1]] if near else []


def gather_far(value, near, passed=()):
    if near:
        if not passed:
            passed = pass_on(near)
        far = [swap_tensor(passed[0], 2), swap_tensor(passed[1], 1)]
        return {0: [value], 1: [near[0]], 2: [near[1]], 3: far}
    parts = []
    for piece, bits in zip(halves(value), bit_orders()):
        have = {0: piece}
        for bit in bits:
            have.update({m ^ bit: swap_tensor(got, bit) for m, got in list(have.items())})
        parts.append(have)
    return {mask: [part[mask] for part in parts] for mask in parts[0]}


def add(left, right):
    return (left.astype(f32) + right.astype(f32)).astype(bf16)


def scatter_far(parts):
    if lax.axis_size("tensor") != 4:
        return []
    upper, lower = parts[3]
    return [swap_tensor(upper, 1), swap_tensor(lower, 2)]


def scatter_join(parts, far):
    if not far:
        return []
    to_x, to_y = parts[1][0], parts[2][0]
    middle = to_y.shape[0] // 2
    return [
        lax.dynamic_update_slice_in_dim(to_x, add(to_x[middle:], far[1]), middle, 0),
        lax.dynamic_update_slice_in_dim(to_y, add(to_y[:middle], far[0]), 0, 0),
    ]


def scatter_near(parts, joined):
    if joined:
        return [parts[0][0], swap_tensor(joined[0], 1), swap_tensor(joined[1], 2)]
    parts = {mask: jnp.concatenate(part, axis=0) for mask, part in parts.items()}
    sums = []
    for which, bits in enumerate(bit_orders()):
        left = {mask: halves(part)[which] for mask, part in parts.items()}
        for bit in bits:
            for mask in [m for m in left if not m & bit]:
                left[mask] = add(left[mask], swap_tensor(left.pop(mask | bit), bit))
        sums.append(left[0])
    return [jnp.concatenate(sums, axis=0)]


def spread_tensor(value):
    return swap_all([value] * lax.axis_size("tensor"))


def swap_all(pieces):
    return [swap_tensor(piece, mask) if mask else piece for mask, piece in enumerate(pieces)]


def by_index(pieces):
    here = lax.axis_index("tensor")
    order = []
    for place in range(len(pieces)):
        piece = pieces[0]
        for mask in range(1, len(pieces)):
            piece = jnp.where(here ^ place == mask, pieces[mask], piece)
        order.append(piece)
    return jnp.stack(order)


def send_z(value):
    return jnp.stack([value] + [shift_z(value, i) for i in range(1, lax.axis_size("z"))])


def sums_z(terms):
    depth = lax.axis_size("z")
    here = lax.axis_index("z")
    take = lambda term, i: lax.dynamic_index_in_dim(term, (here + i) % depth, 0, False)
    sums = [total([take(term, i) for term in terms]) for i in range(depth)]
    return [sums[0]] + [part.astype(bf16) for part in sums[1:]]


def scatter_z(sums):
    return [sums[0]] + [shift_z(part, i + 1) for i, part in enumerate(sums[1:])]


def exchange(value, axis):
    return lax.all_to_all(value, axis, 0, 0)


def spread(value, axis):
    return exchange(jnp.broadcast_to(value[None], (lax.axis_size(axis),) + value.shape), axis)


def piece_rows(mask, height, n_t):
    return [height // 2] * 2 if mask == 3 and n_t == 4 else [height]


def total(terms):
    terms = [terms[i].astype(f32) for i in range(len(terms))]
    return sum(terms[1:], terms[0])


def attend_forward_kernel(
    heads, n_t, x_at, place_ref, lo_ref, full_ref, fv_ref, cos_ref, sin_ref, start_ref, gain_ref, *rest
):
    x_in, w_in, rest = rest[: len(x_at)], rest[len(x_at) : len(x_at) + 2], rest[len(x_at) + 2 :]
    outs, (ot_ref, lse_ref, x_out, w_out) = rest[:4], rest[4:8]
    o_out, rest = rest[8 : 8 + n_t], rest[8 + n_t :]
    qt_ref, kt_ref, kn_ref, vn_ref, x_ref, w_ref, wt, vt, o_ref, acc, sems, out_sems = rest
    core, t = place_ref[1], place_ref[2]
    n_z = w_in[0].shape[0]
    height = w_ref.shape[0] // (2 * n_z)
    cols = heads * HEAD_DIM
    blocks = x_ref.shape[0] // BLOCK
    count = x_ref.shape[0] // n_t
    copies = []
    for other, ref in enumerate(w_in):
        for z in range(n_z):
            row = pl.multiple_of((2 * z + jnp.bitwise_xor(core, other)) * height, height)
            copies.append((ref.at[z, pl.ds(0, height)], w_ref.at[pl.ds(row, height)]))
    for ref, (mask, offset) in zip(x_in, x_at):
        row = jnp.bitwise_xor(t, mask) * count + offset
        size = ref.shape[0]
        copies.append((ref, x_ref.at[pl.ds(pl.multiple_of(row, size), size)]))
    copies = [pltpu.make_async_copy(a, b, sems.at[i]) for i, (a, b) in enumerate(copies)]
    for copy in copies:
        copy.start()
    for copy in copies[: 2 * n_z]:
        copy.wait()
    wt[...] = (w_ref[...].astype(f32).T * gain_ref[...]).astype(bf16)

    def project(i, carry):
        at = pl.ds(pl.multiple_of(i * BLOCK, BLOCK), BLOCK)
        joint = mm(wt[...], x_ref[at, :], NT)
        cosine, sine = cos_ref[:, at], sin_ref[:, at]
        first = fv_ref[at, :].astype(f32).T
        for h in range(heads):
            lo, mid, hi = h * HEAD_DIM, h * HEAD_DIM + HALF, (h + 1) * HEAD_DIM
            qa, qb = joint[lo:mid], joint[mid:hi]
            q = jnp.concatenate([qa * cosine - qb * sine, qb * cosine + qa * sine], axis=0)
            qt_ref[lo:hi, at] = (q * HEAD_DIM ** (-0.5)).astype(bf16)
            ka, kb = joint[cols + lo : cols + mid], joint[cols + mid : cols + hi]
            k = jnp.concatenate([ka * cosine - kb * sine, kb * cosine + ka * sine], axis=0)
            kt_ref[lo:hi, at] = k.astype(bf16)
            kn_ref[h, at, :] = k.T.astype(bf16)
            v = 0.5 * joint[2 * cols + lo : 2 * cols + hi] + 0.5 * first[lo:hi]
            vt[lo:hi, at] = v.astype(bf16)
            vn_ref[h, at, :] = v.T.astype(bf16)
        return carry

    for copy in copies[2 * n_z :]:
        copy.wait()
    lax.fori_loop(0, blocks, project, 0)
    pairs = [(x_ref, x_out), (w_ref, w_out)]
    pairs += list(zip((qt_ref, kt_ref, kn_ref, vn_ref), outs))
    keep = [pltpu.make_async_copy(a, b, out_sems.at[i]) for i, (a, b) in enumerate(pairs)]
    for copy in keep:
        copy.start()

    def query_block(i, carry):
        qs = pl.ds(pl.multiple_of(i * BLOCK, BLOCK), BLOCK)
        start = start_ref[:, qs]
        key_iota = lax.broadcasted_iota(jnp.int32, (BLOCK, BLOCK), 0)
        query_pos = lax.broadcasted_iota(jnp.int32, (BLOCK, BLOCK), 1) + i * BLOCK

        def tile(j, state, masked, opening):
            ks = pl.ds(pl.multiple_of(j * BLOCK, BLOCK), BLOCK)
            if masked:
                key_pos = key_iota + j * BLOCK
                allowed = (key_pos <= query_pos) & (key_pos >= start)
            result = []
            all_scores = [
                mm(kn_ref[h, ks, :], qt_ref[h * HEAD_DIM : (h + 1) * HEAD_DIM, qs])
                for h in range(heads)
            ]
            if masked:
                all_scores = [jnp.where(allowed, sc, -1e30) for sc in all_scores]
            peaks = [jnp.max(sc, axis=0, keepdims=True) for sc in all_scores]
            if not opening:
                shrinks = []
                for h in range(heads):
                    peaks[h] = jnp.maximum(state[h][0], peaks[h])
                    shrinks.append(jnp.exp(state[h][0] - peaks[h]))
            all_probs = [jnp.exp(sc - pk) for sc, pk in zip(all_scores, peaks)]
            for h in range(heads):
                rows = slice(h * HEAD_DIM, (h + 1) * HEAD_DIM)
                total = jnp.sum(all_probs[h], axis=0, keepdims=True)
                out = mm(vt[rows, ks], all_probs[h].astype(bf16))
                if not opening:
                    total = total + state[h][1] * shrinks[h]
                    out = out + acc[rows, :] * shrinks[h]
                acc[rows, :] = out
                result.append((peaks[h], total))
            return tuple(result)

        lo, full = lo_ref[i], full_ref[i]
        state = tile(i, None, True, True)
        state = lax.fori_loop(full, i, lambda j, s: tile(j, s, False, False), state)
        state = lax.fori_loop(lo, full, lambda j, s: tile(j, s, True, False), state)
        for h in range(heads):
            rows = slice(h * HEAD_DIM, (h + 1) * HEAD_DIM)
            peak, total = state[h]
            acc[rows, :] = acc[rows, :] * (1.0 / total)
            lse_ref[h : h + 1, qs] = peak + jnp.log(total)
        out = acc[...]
        ot_ref[:, qs] = out.astype(bf16)
        o_ref[qs, :] = out.T.astype(bf16)
        return carry

    lax.fori_loop(0, blocks, query_block, 0)
    for mask in range(n_t):
        row = pl.multiple_of(jnp.bitwise_xor(t, mask) * count, count)
        copy = pltpu.make_async_copy(o_ref.at[pl.ds(row, count)], o_out[mask], sems.at[mask])
        copy.start()
        keep.append(copy)
    for copy in keep:
        copy.wait()


def attend_backward_kernel(
    heads, n_t, place_ref, lo_ref, full_ref, qt_ref, kt_ref, kn_ref, vn_ref, ot_ref, lse_ref,
    cos_ref, sin_ref, start_ref, w_ref, gain_ref, *rest
):
    do_in, rest = rest[:n_t], rest[n_t:]
    gt_out, gf_out, *gn_out = rest[:-11]
    gt_ref, gf_ref, do_ref, gn_ref, dot_, delta, dq, dk, dv, sems, out_sems = rest[-11:]
    t = place_ref[2]
    cols = heads * HEAD_DIM
    blocks = do_ref.shape[0] // BLOCK
    count = do_ref.shape[0] // n_t
    copies = []
    for mask in range(n_t):
        row = pl.multiple_of(jnp.bitwise_xor(t, mask) * count, count)
        copies.append(
            pltpu.make_async_copy(do_in[mask], do_ref.at[pl.ds(row, count)], sems.at[mask])
        )
        copies[-1].start()
    for copy in copies:
        copy.wait()
    dk[...] = jnp.zeros_like(dk)
    dv[...] = jnp.zeros_like(dv)

    def prepare(i, carry):
        at = pl.ds(pl.multiple_of(i * BLOCK, BLOCK), BLOCK)
        grads = do_ref[at, :].astype(f32).T
        dot_[:, at] = grads.astype(bf16)
        prod = grads * ot_ref[:, at].astype(f32)
        for h in range(heads):
            delta[h : h + 1, at] = jnp.sum(
                prod[h * HEAD_DIM : (h + 1) * HEAD_DIM], axis=0, keepdims=True
            )
        return carry

    lax.fori_loop(0, blocks, prepare, 0)

    def give(i):
        at = pl.ds(pl.multiple_of(i * BLOCK, BLOCK), BLOCK)
        return [
            pltpu.make_async_copy(gt_ref.at[:, at], gt_out.at[:, at], out_sems.at[2 * i]),
            pltpu.make_async_copy(gf_ref.at[at], gf_out.at[at], out_sems.at[2 * i + 1]),
        ]

    def query_block(step, carry):
        i = blocks - 1 - step
        qs = pl.ds(pl.multiple_of(i * BLOCK, BLOCK), BLOCK)
        start = start_ref[:, qs]
        key_iota = lax.broadcasted_iota(jnp.int32, (BLOCK, BLOCK), 0)
        query_pos = lax.broadcasted_iota(jnp.int32, (BLOCK, BLOCK), 1) + i * BLOCK
        dq[...] = jnp.zeros_like(dq)

        def tile(j, carry, masked):
            ks = pl.ds(pl.multiple_of(j * BLOCK, BLOCK), BLOCK)
            if masked:
                key_pos = key_iota + j * BLOCK
                allowed = (key_pos <= query_pos) & (key_pos >= start)
            hs = range(heads)
            rows = [slice(h * HEAD_DIM, (h + 1) * HEAD_DIM) for h in hs]
            q_h = [qt_ref[rows[h], qs] for h in hs]
            do_h = [dot_[rows[h], qs] for h in hs]
            scores = [mm(kn_ref[h, ks, :], q_h[h]) for h in hs]
            gp = [mm(vn_ref[h, ks, :], do_h[h]) for h in hs]
            for h in hs:
                s = scores[h]
                if masked:
                    s = jnp.where(allowed, s, -1e30)
                probs = jnp.exp(s - lse_ref[h : h + 1, qs])
                grad_scores = (probs * (gp[h] - delta[h : h + 1, qs])).astype(bf16)
                dv[rows[h], ks] += mm(do_h[h], probs.astype(bf16), NT)
                dk[rows[h], ks] += mm(q_h[h], grad_scores, NT)
                dq[rows[h], :] += mm(kt_ref[rows[h], ks], grad_scores)
            return carry

        lo, full = lo_ref[i], full_ref[i]
        tile(i, 0, True)
        lax.fori_loop(full, i, lambda j, s: tile(j, s, False), 0)
        lax.fori_loop(lo, full, lambda j, s: tile(j, s, True), 0)

        cosine, sine = cos_ref[:, qs], sin_ref[:, qs]
        pieces = []
        for source, factor in ((dq, HEAD_DIM ** (-0.5)), (dk, 1.0)):
            for h in range(heads):
                lo_row, mid, hi = h * HEAD_DIM, h * HEAD_DIM + HALF, (h + 1) * HEAD_DIM
                where = slice(None) if source is dq else qs
                a, b = source[lo_row:mid, where] * factor, source[mid:hi, where] * factor
                pieces += [a * cosine + b * sine, b * cosine - a * sine]
        half_v = 0.5 * dv[:, qs]
        gf_ref[qs, :] = half_v.T
        grads = jnp.concatenate(pieces + [half_v], axis=0)
        gt_ref[:, qs] = grads.astype(bf16)
        for copy in give(i):
            copy.start()
        gn_ref[qs, :] = (mm(grads.T.astype(bf16), w_ref[...], NT) * gain_ref[...]).astype(bf16)
        return carry

    lax.fori_loop(0, blocks, query_block, 0)
    copies, outs = [], list(gn_out)
    for mask in range(n_t):
        row = jnp.bitwise_xor(t, mask) * count
        for size in piece_rows(mask, count, n_t):
            copies.append(
                pltpu.make_async_copy(
                    gn_ref.at[pl.ds(pl.multiple_of(row, size), size)],
                    outs.pop(0),
                    sems.at[len(copies)],
                )
            )
            row = row + size
    for copy in copies:
        copy.start()
    for i in range(blocks):
        copies += give(i)
    for copy in copies:
        copy.wait()


def feed_forward_kernel(masks, place_ref, *rest):
    count = len(masks)
    sources, pieces, rest = rest[:5], rest[5 : 5 + count], rest[5 + count :]
    inner_out, gvu_out, *u_outs = rest[:4]
    held, (w, inner_ref, gvu_ref, *u_refs, in_sems, out_sems) = rest[4:9], rest[9:]
    xa_ref, xb_ref, ga_ref, gb_ref, wd_ref = held
    t = place_ref[2]
    first = [pltpu.make_async_copy(sources[0], xa_ref, in_sems.at[0])]
    for i, (piece, (mask, row)) in enumerate(zip(pieces, masks)):
        at = w.at[pl.ds(row, piece.shape[0]), :, jnp.bitwise_xor(t, mask)]
        first.append(pltpu.make_async_copy(piece, at, in_sems.at[5 + i]))
    first.append(pltpu.make_async_copy(sources[2], ga_ref, in_sems.at[2]))
    first.append(pltpu.make_async_copy(sources[4], wd_ref, in_sems.at[4]))
    second = [
        pltpu.make_async_copy(sources[1], xb_ref, in_sems.at[1]),
        pltpu.make_async_copy(sources[3], gb_ref, in_sems.at[3]),
    ]
    for copy in first + second:
        copy.start()
    features = xa_ref.shape[1]
    tokens = xa_ref.shape[0]
    ff = wd_ref.shape[0]
    step, high = 256, min(512, tokens)
    edges = list(range(0, ff, step)) + [ff]
    results = []

    def give(ref, out):
        copy = pltpu.make_async_copy(ref, out, out_sems.at[len(results)])
        copy.start()
        results.append(copy)

    def weight(lo, hi):
        return w[:, :, :, :, lo:hi].reshape(features, hi - lo)

    for source, (x_ref, g_ref) in enumerate(((xa_ref, ga_ref), (xb_ref, gb_ref))):
        for copy in (first, second)[source]:
            copy.wait()
        for row in range(0, tokens, high):
            rows = pl.ds(row, high)
            outs = pl.ds(source * tokens + row, high)
            x, g = x_ref[rows, :], g_ref[rows, :]
            for lo, hi in zip(edges[:-1], edges[1:]):
                gate = mm(x, weight(lo, hi))
                up = mm(x, weight(ff + lo, ff + hi))
                grad_inner = mm(g, wd_ref[lo:hi, :], NT)
                sig = jax.nn.sigmoid(gate)
                act = gate * sig
                inner_ref[outs, lo:hi] = (act * up).astype(bf16)
                gvu_ref[outs, lo:hi] = (
                    grad_inner * up * (sig * (1.0 + gate * (1.0 - sig)))
                ).astype(bf16)
                gvu_ref[outs, ff + lo : ff + hi] = (grad_inner * act).astype(bf16)
            give(inner_ref.at[outs], inner_out.at[outs])
            give(gvu_ref.at[outs], gvu_out.at[outs])
            u = mm(gvu_ref[outs, :], weight(0, 2 * ff), NT)
            u_refs[source][rows, :] = u.astype(u_refs[source].dtype)
            give(u_refs[source].at[rows], u_outs[source].at[rows])
    for copy in results:
        copy.wait()


def gate_up_grad_kernel(n_t, place_ref, xa_ref, xb_ref, gvu_in, out_ref, xt, gvu, grads, sems, out_sems):
    tokens, features = xa_ref.shape
    n_z = grads.shape[0]
    own = grads.shape[3]
    step = gvu.shape[2]
    blocks = gvu.shape[0]

    def fetch(i):
        at = pl.ds(pl.multiple_of(i * step, step), step)
        return pltpu.make_async_copy(gvu_in.at[:, at], gvu.at[i], sems.at[i])

    def give(i):
        at = pl.ds(pl.multiple_of(i * step, step), step)
        return [
            pltpu.make_async_copy(
                grads.at[:, :, j, :, at], out_ref.at[j, :, :, :, at], out_sems.at[n_t * i + j]
            )
            for j in range(n_t)
        ]

    for i in range(blocks):
        fetch(i).start()
    for i in range(0, tokens, 256):
        xt[:, i : i + 256] = xa_ref[i : i + 256, :].T
        xt[:, tokens + i : tokens + i + 256] = xb_ref[i : i + 256, :].T

    def columns(i, carry):
        fetch(i).wait()
        part = mm(xt[...], gvu[i]).astype(bf16)
        at = pl.ds(pl.multiple_of(i * step, step), step)
        grads[:, :, :, :, at] = part.reshape(n_z, 2, n_t, own, step)
        for copy in give(i):
            copy.start()
        return carry

    lax.fori_loop(0, blocks, columns, 0)
    for i in range(blocks):
        for copy in give(i):
            copy.wait()


def load_output_weight(place_ref, near, far, wo, sems):
    z, core = place_ref[0], place_ref[1]
    n_z = near.shape[0]
    copies = []
    for other, ref in enumerate((near, far)):
        for i in range(n_z):
            at = wo.at[2 * lax.rem(z - i + n_z, n_z) + jnp.bitwise_xor(core, other)]
            copies.append(pltpu.make_async_copy(ref.at[i], at, sems.at[len(copies)]))
            copies[-1].start()
    for copy in copies:
        copy.wait()


def project_out_kernel(n_t, place_ref, token_ref, near, far, *rest):
    *att, hidden_ref, unit_ref, wo, sems = rest

    @pl.when(pl.program_id(0) == 0)
    def _():
        load_output_weight(place_ref, near, far, wo, sems)

    t = place_ref[2]
    n_dp, _, height, cols = wo.shape
    hidden = token_ref[...].astype(f32)
    for mask, ref in enumerate(att):
        weight = wo[:, jnp.bitwise_xor(t, mask)].reshape(n_dp * height, cols)
        hidden = hidden + mm(ref[...], weight, NT)
    hidden_ref[...] = hidden
    mean = jnp.mean(hidden * hidden, axis=-1, keepdims=True)
    unit_ref[...] = (hidden * lax.rsqrt(mean + eps)).astype(bf16)


def norm_backward(values, scaled, inverse):
    dot = jnp.sum(scaled * values, axis=-1, keepdims=True) / values.shape[-1]
    return inverse * scaled - values * (inverse * inverse * inverse * dot)


def branch_grad_kernel(
    place_ref, hidden_ref, u_ref, u_got_ref, g_ref, near, far, grad_ref, branch_ref, *rest
):
    *outs, wo, sems = rest

    @pl.when(pl.program_id(0) == 0)
    def _():
        load_output_weight(place_ref, near, far, wo, sems)

    t = place_ref[2]
    n_dp, _, height, cols = wo.shape
    hidden = hidden_ref[...]
    scaled = u_ref[...] + u_got_ref[...].astype(f32)
    inverse = lax.rsqrt(jnp.mean(hidden * hidden, axis=-1, keepdims=True) + eps)
    grad = g_ref[...].astype(f32) + norm_backward(hidden, scaled, inverse)
    grad_ref[...] = grad
    branch = grad.astype(bf16)
    branch_ref[...] = branch
    for mask, out in enumerate(outs):
        weight = wo[:, jnp.bitwise_xor(t, mask)].reshape(n_dp * height, cols)
        out[...] = mm(branch, weight).astype(bf16)


def output_grad_kernel(place_ref, branch_ref, *rest):
    *att, keep_ref, give_ref, turned, grads = rest
    core, t = place_ref[1], place_ref[2]
    n_z, n_t, height, cols = keep_ref.shape
    turned[...] = branch_ref[...].T
    for mask, ref in enumerate(att):
        part = mm(turned[...], ref[...]).astype(bf16).reshape(n_z, 2, height, cols)
        for which in range(2):
            grads[which, :, jnp.bitwise_xor(t, mask)] = part[:, which]
    keep_ref[...] = grads[core]
    give_ref[...] = grads[1 - core]


def projection_grad_kernel(
    place_ref, gt_in, x_in, keep_ref, give_ref, gt_ref, x_ref, grads, sems, out_sems
):
    core = place_ref[1]
    _, n_z, height, _ = grads.shape
    wide = 2 * height

    def fetch(i):
        at = pl.ds(pl.multiple_of(i * wide, wide), wide)
        return pltpu.make_async_copy(x_in.at[:, at], x_ref.at[i], sems.at[1 + i])

    load = pltpu.make_async_copy(gt_in, gt_ref, sems.at[0])
    load.start()
    for i in range(n_z):
        fetch(i).start()
    load.wait()

    def give(i):
        return [
            pltpu.make_async_copy(grads.at[core, i], keep_ref.at[i], out_sems.at[2 * i]),
            pltpu.make_async_copy(grads.at[1 - core, i], give_ref.at[i], out_sems.at[2 * i + 1]),
        ]

    def columns(i, carry):
        fetch(i).wait()
        part = mm(gt_ref[...], x_ref[i]).T.astype(bf16)
        grads[0, i] = part[:height]
        grads[1, i] = part[height:]
        for copy in give(i):
            copy.start()
        return carry

    lax.fori_loop(0, n_z, columns, 0)
    for i in range(n_z):
        for copy in give(i):
            copy.wait()


def vmem(n):
    return [pl.BlockSpec(memory_space=pltpu.VMEM)] * n


def smem(n):
    return [pl.BlockSpec(memory_space=pltpu.SMEM)] * n


def hbm(n):
    return [pl.BlockSpec(memory_space=pl.ANY)] * n


sds = jax.ShapeDtypeStruct


def row_blocks(arrays):
    return [pl.BlockSpec((BLOCK, a.shape[1]), lambda i: (i, 0)) for a in arrays]


def call(kernel, name, gflops, in_specs, out_specs, out_shape, scratch, args, grid=()):
    return pl.pallas_call(
        kernel,
        grid=grid,
        out_shape=tuple(out_shape),
        in_specs=in_specs,
        out_specs=tuple(out_specs),
        scratch_shapes=scratch,
        compiler_params=pltpu.CompilerParams(vmem_limit_bytes=VMEM_LIMIT),
        cost_estimate=pl.CostEstimate(
            flops=int(gflops * 1e9), bytes_accessed=1000, transcendentals=0
        ),
        name=name,
    )(*args)


def attend_forward(
    heads, n_t, place, lo, full, x_pieces, near, far, fv, cosine, sine, start, gain
):
    rows, cols = fv.shape
    x_at = [(mask, offset) for mask, offset, _ in x_pieces]
    pieces = [piece for _, _, piece in x_pieces]
    features, width = pieces[0].shape[1], near.shape[2]
    return call(
        functools.partial(attend_forward_kernel, heads, n_t, x_at),
        "attend_forward",
        5,
        smem(3) + vmem(5) + hbm(len(pieces) + 2),
        hbm(4) + vmem(2) + hbm(2 + n_t),
        [
            sds((cols, rows), bf16),
            sds((cols, rows), bf16),
            sds((heads, rows, HEAD_DIM), bf16),
            sds((heads, rows, HEAD_DIM), bf16),
            sds((cols, rows), bf16),
            sds((heads, rows), f32),
            sds((rows, features), bf16),
            sds((features, width), bf16),
        ]
        + [sds((rows // n_t, cols), bf16)] * n_t,
        [
            pltpu.VMEM((cols, rows), bf16),
            pltpu.VMEM((cols, rows), bf16),
            pltpu.VMEM((heads, rows, HEAD_DIM), bf16),
            pltpu.VMEM((heads, rows, HEAD_DIM), bf16),
            pltpu.VMEM((rows, features), bf16),
            pltpu.VMEM((features, width), bf16),
            pltpu.VMEM((width, features), bf16),
            pltpu.VMEM((cols, rows), bf16),
            pltpu.VMEM((rows, cols), bf16),
            pltpu.VMEM((cols, BLOCK), f32),
            pltpu.SemaphoreType.DMA((len(pieces) + 2 * near.shape[0],)),
            pltpu.SemaphoreType.DMA((6,)),
        ],
        (place, lo, full, fv, cosine, sine, start, gain, *pieces, near, far),
    )


def attend_backward(
    heads, n_t, place, lo, full, saved, grads, cosine, sine, start, w, gain
):
    rows, cols = start.shape[1], heads * HEAD_DIM
    count = rows // n_t
    features = w.shape[0]
    sizes = {mask: piece_rows(mask, count, n_t) for mask in range(n_t)}
    flat = [size for mask in range(n_t) for size in sizes[mask]]
    outs = call(
        functools.partial(attend_backward_kernel, heads, n_t),
        "attend_backward",
        10,
        smem(3) + vmem(11) + hbm(n_t),
        hbm(2 + len(flat)),
        [sds((3 * cols, rows), bf16), sds((rows, cols), f32)]
        + [sds((size, features), bf16) for size in flat],
        [
            pltpu.VMEM((3 * cols, rows), bf16),
            pltpu.VMEM((rows, cols), f32),
            pltpu.VMEM((rows, cols), bf16),
            pltpu.VMEM((rows, features), bf16),
            pltpu.VMEM((cols, rows), bf16),
            pltpu.VMEM((heads, rows), f32),
            pltpu.VMEM((cols, BLOCK), f32),
            pltpu.VMEM((cols, rows), f32),
            pltpu.VMEM((cols, rows), f32),
            pltpu.SemaphoreType.DMA((len(flat),)),
            pltpu.SemaphoreType.DMA((2 * (rows // BLOCK),)),
        ],
        (place, lo, full, *saved, cosine, sine, start, w, gain, *grads),
    )
    pieces = list(outs[2:])
    return outs[0], outs[1], {m: [pieces.pop(0) for _ in sizes[m]] for m in range(n_t)}


def feed_forward(n_z, n_t, place, xa, xb, ga, gb, wd, gathered):
    tokens, features = xa.shape
    ff = wd.shape[0]
    pieces, masks = [], []
    for mask, parts in gathered.items():
        first = 0
        for part in parts:
            pieces.append(part)
            masks.append((mask, first))
            first += part.shape[0]
    return call(
        functools.partial(feed_forward_kernel, masks),
        "feed_forward",
        0,
        smem(1) + hbm(5 + len(pieces)),
        hbm(4),
        [
            sds((2 * tokens, ff), bf16),
            sds((2 * tokens, 2 * ff), bf16),
            sds((tokens, features), f32),
            sds((tokens, features), bf16),
        ],
        [
            *[pltpu.VMEM((tokens, features), bf16)] * 4,
            pltpu.VMEM((ff, features), bf16),
            pltpu.VMEM((n_z, 2, n_t, features // (2 * n_z * n_t), 2 * ff), bf16),
            pltpu.VMEM((2 * tokens, ff), bf16),
            pltpu.VMEM((2 * tokens, 2 * ff), bf16),
            pltpu.VMEM((tokens, features), f32),
            pltpu.VMEM((tokens, features), bf16),
            pltpu.SemaphoreType.DMA((5 + len(pieces),)),
            pltpu.SemaphoreType.DMA((6 * max(1, tokens // 512),)),
        ],
        (place, xa, xb, ga, gb, wd, *pieces),
    )


def gate_up_grad(n_z, n_t, place, xa, xb, gvu):
    tokens, features = xa.shape
    own = features // (2 * n_z * n_t)
    return call(
        functools.partial(gate_up_grad_kernel, n_t),
        "gate_up_grad",
        0,
        smem(1) + vmem(2) + hbm(1),
        hbm(1),
        [sds((n_t, n_z, 2, own, gvu.shape[1]), bf16)],
        [
            pltpu.VMEM((features, 2 * tokens), bf16),
            pltpu.VMEM((gvu.shape[1] // 256, 2 * tokens, 256), bf16),
            pltpu.VMEM((n_z, 2, n_t, own, gvu.shape[1]), bf16),
            pltpu.SemaphoreType.DMA((gvu.shape[1] // 256,)),
            pltpu.SemaphoreType.DMA((n_t * (gvu.shape[1] // 256),)),
        ],
        (place, xa, xb, gvu),
    )[0]


def output_weight_scratch(near):
    n_z, n_t, height, cols = near.shape
    return [
        pltpu.VMEM((2 * n_z, n_t, height, cols), bf16),
        pltpu.SemaphoreType.DMA((2 * n_z,)),
    ]


def project_out(place, tokens, att, near, far):
    shapes = [sds(tokens.shape, f32), sds(tokens.shape, bf16)]
    return call(
        functools.partial(project_out_kernel, len(att)),
        "project_out",
        20,
        smem(1) + row_blocks([tokens]) + hbm(2) + row_blocks(att),
        row_blocks(shapes),
        shapes,
        output_weight_scratch(near),
        (place, tokens, near, far, *att),
        (tokens.shape[0] // BLOCK,),
    )


def branch_grad(place, hidden, u, u_got, g, near, far):
    _, n_t, _, cols = near.shape
    shapes = [sds(hidden.shape, f32), sds(hidden.shape, bf16)]
    shapes += [sds((hidden.shape[0], cols), bf16)] * n_t
    outs = call(
        branch_grad_kernel,
        "branch_grad",
        0,
        smem(1) + row_blocks([hidden, u, u_got, g]) + hbm(2),
        row_blocks(shapes),
        shapes,
        output_weight_scratch(near),
        (place, hidden, u, u_got, g, near, far),
        (hidden.shape[0] // BLOCK,),
    )
    return outs[0], outs[1], list(outs[2:])


def output_grad(n_z, place, branch, att):
    n_t, cols = len(att), att[0].shape[1]
    shape = (n_z, n_t, branch.shape[1] // (2 * n_z), cols)
    return call(
        output_grad_kernel,
        "output_grad",
        0,
        smem(1) + vmem(1 + n_t),
        vmem(2),
        [sds(shape, bf16)] * 2,
        [pltpu.VMEM(branch.shape[::-1], bf16), pltpu.VMEM((2,) + shape, bf16)],
        (place, branch, *att),
    )


def projection_grad(n_z, place, gt, x):
    height = x.shape[1] // (2 * n_z)
    return call(
        projection_grad_kernel,
        "projection_grad",
        0,
        smem(1) + hbm(2),
        hbm(2),
        [sds((n_z, height, gt.shape[0]), bf16)] * 2,
        [
            pltpu.VMEM(gt.shape, bf16),
            pltpu.VMEM((n_z, x.shape[0], 2 * height), bf16),
            pltpu.VMEM((2, n_z, height, gt.shape[0]), bf16),
            pltpu.SemaphoreType.DMA((1 + n_z,)),
            pltpu.SemaphoreType.DMA((2 * n_z,)),
        ],
        (place, gt, x),
    )


def doc_layout(doc_lengths, total):
    doc_ends = jnp.cumsum(doc_lengths)
    index = jnp.arange(total, dtype=jnp.int32)
    passed = (index[:, None] >= doc_ends[None, :]).astype(jnp.int32)
    return jnp.sum(passed * doc_lengths[None, :], axis=1)


def split_cols(weight, n_z):
    rows = weight.shape[0]
    return weight.reshape(rows, n_z, 2, -1).transpose(2, 0, 1, 3).reshape(2, rows, -1)


def join_cols(parts, n_z):
    rows = parts.shape[1]
    return parts.reshape(2, rows, n_z, -1).transpose(1, 2, 0, 3).reshape(rows, -1)


def body(
    tokens, lengths, first_values, attn_gain, query_weight, key_weight, value_weight,
    output_weight, mlp_gain, gate_weight, up_weight, down_weight, out_cotangent,
):
    n_t = lax.axis_size("tensor")
    n_z = lax.axis_size("z")
    t = lax.axis_index("tensor")
    core = lax.axis_index("core")
    place = jnp.stack([lax.axis_index("z"), core, t]).astype(jnp.int32)
    masks = range(n_t)
    count, features = tokens.shape
    rows = count * n_t
    wrows, cols = query_weight.shape
    heads = cols // HEAD_DIM
    ff_core = gate_weight.shape[1] // 2

    def by_core(near, far, axis):
        return jnp.where(
            core == 0, jnp.stack([near, far], axis=axis), jnp.stack([far, near], axis=axis)
        )

    token_f = tokens.astype(f32)
    inverse_in = lax.rsqrt(jnp.mean(token_f * token_f, axis=-1, keepdims=True) + eps)
    unit_in = (token_f * inverse_in).astype(bf16)
    with jax.named_scope("normed_tokens"):
        x_near = gather_near(unit_in)

    own_joint = jnp.concatenate([query_weight, key_weight, value_weight], axis=1)
    own_gains = attn_gain.shape[0]
    gain_rows = jnp.pad(attn_gain[None], ((0, 7), (0, 3 * cols - own_gains)))
    with jax.named_scope("attention_weights_z"):
        near = spread(jnp.concatenate([own_joint, gain_rows]), "z")

    gain_mid = mlp_gain.astype(f32)[:, None]
    both = jnp.concatenate(
        [split_cols(gate_weight, n_z), split_cols(up_weight, n_z)], axis=2
    ).astype(f32)
    both = (both * gain_mid[None]).astype(bf16)
    mine = lax.dynamic_index_in_dim(both, core, 0, False)
    with jax.named_scope("gate_up_core"):
        theirs = swap_core(lax.dynamic_index_in_dim(both, 1 - core, 0, False))
    with jax.named_scope("core_tokens"):
        grad_far = swap_core(out_cotangent)
    pair = by_core(mine, theirs, 0)

    start = doc_layout(lengths[0], rows)
    position = (jnp.arange(rows, dtype=jnp.int32) - start).astype(f32)
    freqs = rope_base ** (-jnp.arange(HALF, dtype=f32) * 2.0 / HEAD_DIM)
    angles = freqs[:, None] * position[None, :]
    cosine, sine = jnp.cos(angles), jnp.sin(angles)
    block_starts = start.reshape(-1, BLOCK)
    lo = block_starts[:, 0] // BLOCK
    full = jnp.minimum(
        (block_starts[:, -1] + BLOCK - 1) // BLOCK,
        jnp.arange(rows // BLOCK, dtype=jnp.int32),
    )
    start = start[None]

    x_near, near, pair, grad_far, output_weight, down_weight = together(
        x_near, near, pair, grad_far, output_weight, down_weight
    )

    with jax.named_scope("gate_up_z"):
        column = spread(pair, "z")
    with jax.named_scope("normed_tokens"):
        x_far = gather_far(unit_in, x_near)
    with jax.named_scope("attention_weights_core"):
        far = swap_core(near)
    drows = down_weight.shape[0]
    brows = drows + output_weight.size // features
    column_gain = by_core(near[:, wrows, :own_gains], far[:, wrows, :own_gains], 1).reshape(1, -1)
    with jax.named_scope("output_down_tensor"):
        slab = [
            down_weight,
            output_weight.reshape(-1, features),
            jnp.pad(column_gain, ((0, 7), (0, features - column_gain.shape[1]))),
        ]
        slabs = spread_tensor(jnp.concatenate(slab, axis=0))

    x_far, far, slab, column, cosine, sine, start, lo, full = together(
        x_far, far, by_index(slabs), column, cosine, sine, start, lo, full
    )

    with jax.named_scope("down_z"):
        down = lax.all_gather(slab[:, :drows].reshape(-1, features), "z", tiled=True)
    with jax.named_scope("output_weight_z"):
        out_near = send_z(slab[:, drows:brows].reshape(n_t, wrows, cols))
    gain = slab[:, brows, : column_gain.shape[1]].reshape(n_t, 2 * n_z, own_gains)
    gain = gain.transpose(1, 0, 2).astype(f32)
    gain_rows = lax.dynamic_index_in_dim(gain, place[0] * 2 + core, 0, False).reshape(-1, 1)
    gain = gain.reshape(1, features)
    with jax.named_scope("gate_up_tensor"):
        gu_near = gather_near(column)
    x_pieces = []
    for mask, parts in x_far.items():
        offset = 0
        for part in parts:
            x_pieces.append((mask, offset, part))
            offset += part.shape[0]
    qt, kt, kn, vn, ot, lse, x_full, joint_weight, *attended = attend_forward(
        heads, n_t, place, lo, full, x_pieces, near, far, first_values, cosine, sine, start, gain
    )

    attended, gu_near = together(attended, gu_near)

    with jax.named_scope("attended"):
        att = swap_all(attended)
    passed = pass_on(gu_near)
    att, out_near = together(att, out_near)
    with jax.named_scope("output_weight_core"):
        out_far = swap_core(out_near)
    with jax.named_scope("gate_up_tensor"):
        gathered = gather_far(column, gu_near, passed)
    hidden, unit_mid = project_out(place, tokens, att, out_near, out_far)
    unit_mid, gathered = together(unit_mid, gathered)
    with jax.named_scope("core_tokens"):
        unit_far = swap_core(unit_mid)

    inner, gvu, u_own, u_give = feed_forward(
        n_z, n_t, place, unit_mid, unit_far, out_cotangent, grad_far, down, gathered
    )
    with jax.named_scope("u_core"):
        u_got = swap_core(u_give)
    grad_both = jnp.concatenate([out_cotangent, grad_far], axis=0)
    grad_dn = mm(inner, grad_both, TN).astype(bf16).reshape(n_z, -1, features)

    u_got, grad_dn = together(u_got, grad_dn)

    with jax.named_scope("grad_down_z"):
        dn = lax.psum_scatter(grad_dn.reshape(-1, features), "z", scatter_dimension=0, tiled=True)
    grad_hidden, branch, grad_att = branch_grad(
        place, hidden, u_own, u_got, out_cotangent, out_near, out_far
    )
    with jax.named_scope("grad_attended"):
        grad_att = swap_all(grad_att)
    gu_parts = gate_up_grad(n_z, n_t, place, unit_mid, unit_far, gvu)
    keep_ow, give_ow = output_grad(n_z, place, branch, att)
    with jax.named_scope("grad_output_core"):
        got_ow = swap_core(give_ow)

    grad_att, gu_parts, got_ow = together(grad_att, gu_parts, got_ow)

    with jax.named_scope("grad_gate_up_tensor"):
        gu_terms = exchange(gu_parts, "tensor")
    with jax.named_scope("grad_output_z"):
        ow_terms = scatter_z(sums_z([keep_ow, got_ow]))
    gt, grad_first, in_parts = attend_backward(
        heads, n_t, place, lo, full, (qt, kt, kn, vn, ot, lse), grad_att, cosine, sine, start,
        joint_weight, gain,
    )

    in_parts, gt, ow_terms, dn = together(in_parts, gt, ow_terms, dn)

    with jax.named_scope("grad_normed"):
        in_far = scatter_far(in_parts)
    keep_jw, give_jw = projection_grad(n_z, place, gt, x_full)
    with jax.named_scope("grad_projection_core"):
        got_jw = swap_core(give_jw)
    jw_sums, inner = together(sums_z([keep_jw, got_jw]), inner)
    with jax.named_scope("grad_projection_z"):
        jw_terms = scatter_z(jw_sums)
    out_part = mm(inner, down)
    out_give = out_part[count:].astype(bf16)

    jw_own, ow_terms = together(jw_sums[0], ow_terms)
    jw_terms[0] = jw_own
    ow = total(ow_terms).astype(bf16).reshape(n_t, -1, features)
    both = jnp.concatenate([dn.reshape(n_t, -1, features), ow], axis=1)
    both = [lax.dynamic_index_in_dim(both, t ^ m, 0, False) for m in masks]

    in_far, gu_terms, jw_terms, out_give, both = together(
        in_far, gu_terms, jw_terms, out_give, both
    )
    with jax.named_scope("grad_output_down_tensor"):
        both_terms = swap_all(both)

    gu_sum = total(gu_terms).astype(bf16)
    in_joined = scatter_join(in_parts, in_far)
    with jax.named_scope("grad_gate_up_z"):
        gu_terms = exchange(gu_sum, "z")
    in_joined, jw_terms, both_terms = together(in_joined, jw_terms, both_terms)
    with jax.named_scope("grad_normed"):
        in_terms = scatter_near(in_parts, in_joined)
    with jax.named_scope("layer_out"):
        out_got = swap_core(out_give)
    layer_out = (hidden + out_part[:count] + out_got.astype(f32)).astype(bf16)

    grad_jw = total(jw_terms)
    gain_part = jnp.sum(grad_jw * own_joint.astype(f32), axis=1).reshape(n_t, -1)
    with jax.named_scope("grad_gain"):
        gain_terms = swap_all([lax.dynamic_index_in_dim(gain_part, t ^ m, 0) for m in masks])
    grad_jw = grad_jw * gain_rows

    in_terms, gu_terms, both_terms, grad_jw, gain_terms, layer_out = together(
        in_terms, gu_terms, both_terms, grad_jw, gain_terms, layer_out
    )
    grad_attn_gain = total(gain_terms)
    grad_down = total(both_terms)
    grad_output = grad_down[drows:].reshape(wrows, cols)
    grad_down = grad_down[:drows]

    gu = total(gu_terms)
    gu_mine = lax.dynamic_index_in_dim(gu, core, 0, False)
    with jax.named_scope("grad_gate_up_core"):
        gu_other = swap_core(lax.dynamic_index_in_dim(gu, 1 - core, 0, False))

    grad_input = grad_hidden + norm_backward(token_f, total(in_terms), inverse_in)

    gu = by_core(gu_mine, gu_other, 0)
    grad_gate = join_cols(gu[:, :, :ff_core], n_z)
    grad_up = join_cols(gu[:, :, ff_core:], n_z)
    grad_mlp_gain = jnp.sum(
        grad_gate * gate_weight.astype(f32) + grad_up * up_weight.astype(f32), axis=1
    )
    grad_gate = grad_gate * gain_mid
    grad_up = grad_up * gain_mid

    return (
        layer_out,
        grad_input,
        grad_first,
        grad_attn_gain[0],
        grad_jw[:, :cols],
        grad_jw[:, cols : 2 * cols],
        grad_jw[:, 2 * cols :],
        grad_output,
        grad_mlp_gain,
        grad_gate,
        grad_up,
        grad_down,
    )


def solution(mesh):
    n_dp, n_t = mesh.shape["dp"], mesh.shape["tensor"]
    mesh = Mesh(mesh.devices.reshape(n_dp // 2, 2, n_t), ("z", "core", "tensor"))
    dp = ("z", "core")
    both = ("z", "core", "tensor")
    in_specs = (
        P(both, None),
        P(dp, None),
        P(dp, "tensor"),
        P(both),
        P(dp, "tensor"),
        P(dp, "tensor"),
        P(dp, "tensor"),
        P(dp, "tensor"),
        P(both),
        P(both, None),
        P(both, None),
        P(both, None),
        P(both, None),
    )
    out_specs = (
        P(both, None),
        P(both, None),
        P(dp, "tensor"),
        P(both),
        P(dp, "tensor"),
        P(dp, "tensor"),
        P(dp, "tensor"),
        P(dp, "tensor"),
        P(both),
        P(both, None),
        P(both, None),
        P(both, None),
    )
    return jax.shard_map(body, mesh=mesh, in_specs=in_specs, out_specs=out_specs, check_vma=False)
```
